128 devices in a mesh: feed: 4 (over x_hi, core), pts: 32 (over x_lo, z, y).
Axes of the slice: x: 4 (x_hi: 2, x_lo: 2; x = x_hi * 2 + x_lo), y: 4, z: 4, core: 2. Of those that a mesh axis runs over, the one named last changes fastest.
Arguments:
- illumination: bfloat16 [2, 200, 16384], P(None, 'feed', 'pts'), may hold values from -48 to 48
- excitation: bfloat16 [2, 200, 200], P(None, None, 'feed'), may hold values from -1.25 to 1.25
- beam_group: int32 [200], replicated, may hold values from 0 to 7
- positions: float32 [2, 16384], P(None, 'pts'), may hold values from -86 to 86
- params: float32 [2, 16384], P(None, 'pts'), may hold values from 0 to 1
- span_rows: int32 [128], P('pts'), may hold values from 0 to 60
- span_cols: int32 [128], P('pts'), may hold values from 0 to 60
- surface_coef: float32 [4096], replicated, may hold values from -2 to 2
- directions: float32 [2, 8192], replicated, may hold values from -0.05 to 0.05
- cover_blocks: int32 [200, 8], replicated, may hold values from 0 to 63
- cover_count: int32 [200], replicated, may hold values from 1 to 8, 900 in all
Outputs:
- objective: float32 [], replicated
- grad_coef: float32 [4096], replicated
- grad_exc: float32 [2, 200, 200], P(None, None, 'feed')
The draws below stay inside these ranges and needn't reach their ends.
Inputs may be any that keep to these rules, and one draw needn't show every extreme that they name: `cover_blocks`: slots of a beam past its count are padding; a beam may name a block more than once. `cover_count`: some beam has all 8 slots live.
All inputs are finite; a program needn't handle non-finite values.
Results may differ from the reference program's by a relative error of at most 0.012.
The reference program's roundings to bfloat16 on the way count: a program that leaves them out, or rounds other values in their place, can miss the bound.
Values may be sent and summed in bfloat16 or wider, within the bound.
A program may use at most 128 MiB of HBM per device.

```python
import math
import jax
import jax.numpy as jnp
import numpy as np
from jax import lax

FEEDS = 200
BEAMS = 200
GROUPS = 8
GROUP_SIZE = 25
PTS_DEV = 512
PTS = 16384
BLOCK = 128
NBLK = 128
NDB = 64
GRP = 4
DIRS = 8192
CBMAX = 8
NCU = 64
NCV = 64
NC = 4096


def draw_illumination(key, part):
    key = jax.random.fold_in(key, 11)
    base_key, patch_key = jax.random.split(key)
    base = jnp.clip(jax.random.normal(base_key, (2, FEEDS, PTS), jnp.float32), -6.0, 6.0)
    patch = jax.random.randint(patch_key, (GROUPS,), 0, PTS // PTS_DEV)
    group_of = jnp.arange(FEEDS, dtype=jnp.int32) // GROUP_SIZE
    shard_of = jnp.arange(PTS, dtype=jnp.int32) // PTS_DEV
    lit = patch[group_of][:, None] == shard_of[None, :]
    amplitude = jnp.where(lit, 8.0, 1.0).astype(jnp.float32)
    return (base * amplitude[None]).astype(jnp.bfloat16)


def plant(drawn, own_key, smallest, top_value):
    spot = [jax.random.randint(jax.random.fold_in(own_key, axis), (), 0, length) for axis, length in enumerate(drawn.shape)]
    widest = drawn.shape.index(max(drawn.shape))
    beside = spot[:widest] + [(spot[widest] + 1) % drawn.shape[widest]] + spot[widest + 1:]
    return drawn.at[tuple(spot)].set(smallest).at[tuple(beside)].set(top_value)


def block_levels(own_key, extent, cuts, low, high):
    level = 1.0
    for dim, parts in cuts:
        steps = jax.random.uniform(jax.random.fold_in(jax.random.fold_in(own_key, 6), dim), (parts,), jnp.float32, low / len(cuts), high / len(cuts))
        level = level * jnp.repeat(jnp.exp(steps), extent[dim] // parts).reshape((-1,) + (1,) * (len(extent) - 1 - dim))
    return level


def rank_table(number_of, lean):
    loads = [(1 << 20) // math.isqrt(rank ** lean) + 1 for rank in range(1, number_of + 1)]
    deviation = 1 + sum(loads) // (1 << 30)
    return np.cumsum(np.array([max(1, weight // deviation) for weight in loads]))


def skewed_ids(rng, extent, count, skew):
    table = rank_table(count, skew)
    lot = jax.random.randint(jax.random.fold_in(rng, 1), extent, 0, int(table[count - 1]))
    grade = jnp.searchsorted(jnp.asarray(table, jnp.int32), lot, side="right")
    return jax.random.permutation(jax.random.fold_in(rng, 2), count)[grade].astype(jnp.int32)


def split_up(count, total, reach, skew):
    portions = [(1 << 20) // math.isqrt(grade ** skew) + 1 for grade in range(2, count + 1)]
    surplus, holding = total - reach - (count - 1), [1] * (count - 1)
    while surplus > 0:
        free = [i for i in range(count - 1) if holding[i] < reach]
        pool, left = sum([portions[i] for i in free]), surplus
        for i in free:
            addition = min(reach - holding[i], max(1, left * portions[i] // pool), surplus)
            holding[i] = holding[i] + addition
            surplus = surplus - addition
    return np.array([reach] + holding)


def uneven_parts(rng, number_of, total, most, skew):
    if number_of == 2:
        one = jax.random.randint(rng, (), max(1, total - most), min(most, total - 1) + 1)
        return jnp.stack([one, total - one])
    sizes = jnp.asarray(split_up(number_of, total, most, skew), jnp.int32)
    twos = (number_of - 1) // 2
    source_of, receiver = sizes[1:1 + 2 * twos:2], sizes[2:2 + 2 * twos:2]
    margin = jnp.minimum(source_of - 1, most - receiver)
    moved = jax.random.randint(jax.random.fold_in(rng, 1), (twos,), 0, 1 << 20) % (margin + 1)
    sizes = sizes.at[1:1 + 2 * twos:2].set(source_of - moved).at[2:2 + 2 * twos:2].set(receiver + moved)
    return sizes[jax.random.permutation(jax.random.fold_in(rng, 2), number_of)]


def noise(rng, dims, scale, reach, pieces=(), held_as=jnp.bfloat16):
    array = jax.random.normal(rng, dims, jnp.float32) * scale
    if len(pieces) > 0:
        array = block_levels(rng, dims, pieces, -0.22, 0.18) * array
    return jnp.clip(array, min=-reach, max=reach).astype(held_as)


def setup_inputs(seed: int = 0) -> dict:
    keys = jax.random.split(jax.random.key(seed), 12)
    return {
        "illumination": draw_illumination(jax.random.fold_in(keys[11], 71), 0),
        "excitation": noise(keys[1], (2, BEAMS, FEEDS), GROUP_SIZE ** -0.5, 1.25, ((2, 4),)),
        "beam_group": plant(skewed_ids(keys[2], (BEAMS,), GROUPS, 2), jax.random.fold_in(keys[2], 3), 0, GROUPS - 1).astype(jnp.int32),
        "positions": jnp.clip(jax.random.uniform(keys[3], (2, PTS), jnp.float32, -86.0, 86.0) * block_levels(keys[3], (2, PTS), ((1, 32),), -0.4, 0.0), -86.0, 86.0),
        "params": jnp.clip(1.0 * jax.random.uniform(keys[4], (2, PTS), jnp.float32) ** block_levels(keys[4], (2, PTS), ((1, 32),), -0.2, 0.2), 0.0, 1.0),
        "span_rows": plant(jax.random.randint(keys[5], (NBLK,), 0, NCU - 3), jax.random.fold_in(keys[5], 1), 0, (NCU - 3) - 1).astype(jnp.int32),
        "span_cols": plant(jax.random.randint(keys[6], (NBLK,), 0, NCV - 3), jax.random.fold_in(keys[6], 1), 0, (NCV - 3) - 1).astype(jnp.int32),
        "surface_coef": noise(keys[7], (NC,), 0.3, 2.0, (), jnp.float32),
        "directions": jnp.clip(jax.random.uniform(keys[8], (2, DIRS), jnp.float32, -0.05, 0.05), -0.05, 0.05),
        "cover_blocks": plant(jax.random.randint(keys[9], (BEAMS, CBMAX), 0, NDB), jax.random.fold_in(keys[9], 1), 0, NDB - 1).astype(jnp.int32),
        "cover_count": uneven_parts(keys[10], BEAMS, BEAMS * (CBMAX + 1) // 2, CBMAX, 0).astype(jnp.int32),
    }


SHARPNESS = 2.0
TWO_PI = 2.0 * math.pi

def spline_basis(coord):
    one_minus = 1.0 - coord
    t_sq = coord * coord
    t_cube = t_sq * coord
    return jnp.stack([one_minus * one_minus * one_minus / 6.0, (3.0 * t_cube - 6.0 * t_sq + 4.0) / 6.0, (-3.0 * t_cube + 3.0 * t_sq + 3.0 * coord + 1.0) / 6.0, t_cube / 6.0])

def spline_weights(params):
    return (spline_basis(params[0])[:, None, :] * spline_basis(params[1])[None, :, :]).reshape(16, params.shape[1])

def spline_index(span_rows, span_cols):
    offsets = (jnp.arange(4, dtype=jnp.int32)[:, None] * NCV + jnp.arange(4, dtype=jnp.int32)[None, :]).reshape(16)
    span_base = span_rows * NCV + span_cols
    return jnp.repeat(span_base[None, :] + offsets[:, None], BLOCK, axis=1)

def currents(illumination, excitation, member):
    masked = excitation * member[None].astype(excitation.dtype)
    stacked_left = jnp.concatenate([jnp.concatenate([masked[0], -masked[1]], 1), jnp.concatenate([masked[1], masked[0]], 1)], 0)
    stacked_right = jnp.concatenate([illumination[0], illumination[1]], 0)
    return jnp.dot(stacked_left, stacked_right, preferred_element_type=jnp.float32).astype(jnp.bfloat16)

def kernel(positions, height, dir_block):
    dir_x = dir_block[0]
    dir_y = dir_block[1]
    dir_z = jnp.sqrt(1.0 - dir_x * dir_x - dir_y * dir_y)
    phase_arg = TWO_PI * (positions[0][:, None] * dir_x[None, :] + positions[1][:, None] * dir_y[None, :] + height[:, None] * (1.0 + dir_z)[None, :])
    return (jnp.cos(phase_arg).astype(jnp.bfloat16), jnp.sin(phase_arg).astype(jnp.bfloat16), TWO_PI * (1.0 + dir_z))

def forward_fields(current, positions, height, dir_groups, field_scale):
    beam_count = current.shape[0] // 2

    def group_step(acc_pair, dir_block):
        kern_re, kern_im, phase_rate = kernel(positions, height, dir_block)
        prod_cos = jnp.dot(current, kern_re, preferred_element_type=jnp.float32)
        prod_sin = jnp.dot(current, kern_im, preferred_element_type=jnp.float32)
        fld_re = field_scale * (prod_cos[:beam_count] - prod_sin[beam_count:])
        fld_im = field_scale * (prod_sin[:beam_count] + prod_cos[beam_count:])
        return (acc_pair, (fld_re, fld_im))
    ignored, fields = lax.scan(group_step, jnp.zeros((), jnp.float32), dir_groups)
    return fields

def to_grid(sens, group_idx, beam_idx, sub_idx, beam_count):
    sens_grid = jnp.zeros((NDB // GRP, beam_count, GRP, BLOCK), jnp.float32)
    sens_grid = sens_grid.at[group_idx, beam_idx, sub_idx].add(sens.astype(jnp.float32))
    return sens_grid.astype(jnp.bfloat16).reshape(NDB // GRP, beam_count, GRP * BLOCK)

def backward_terms(positions, height, dir_groups, grid_re, grid_im):
    contract = (((1,), (1,)), ((), ()))
    width_rows = 4 * grid_re.shape[1]
    start = (jnp.zeros((width_rows, positions.shape[1]), jnp.float32), jnp.zeros((width_rows, positions.shape[1]), jnp.float32))

    def group_step(acc_pair, inputs):
        dir_block, sens_re, sens_im = inputs
        kern_re, kern_im, phase_rate = kernel(positions, height, dir_block)
        rated_re = (phase_rate[None, :] * sens_re.astype(jnp.float32)).astype(jnp.bfloat16)
        rated_im = (phase_rate[None, :] * sens_im.astype(jnp.float32)).astype(jnp.bfloat16)
        stacked_left = jnp.concatenate([sens_re, sens_im, rated_re, rated_im], 0)
        back_cos = lax.dot_general(stacked_left, kern_re, contract, preferred_element_type=jnp.float32)
        back_sin = lax.dot_general(stacked_left, kern_im, contract, preferred_element_type=jnp.float32)
        return ((acc_pair[0] + back_cos, acc_pair[1] + back_sin), jnp.zeros((), jnp.float32))
    acc_pair, ignored = lax.scan(group_step, start, (dir_groups, grid_re, grid_im))
    return acc_pair

def excitation_grad(grad_re, grad_im, illumination, member):
    g_re = grad_re.astype(jnp.bfloat16)
    g_im = grad_im.astype(jnp.bfloat16)
    stacked_right = jnp.concatenate([illumination[0], illumination[1]], 1)
    contract = (((1,), (1,)), ((), ()))
    grad_real = lax.dot_general(jnp.concatenate([g_re, g_im], 1), stacked_right, contract, preferred_element_type=jnp.float32)
    grad_imag = lax.dot_general(jnp.concatenate([g_im, -g_re], 1), stacked_right, contract, preferred_element_type=jnp.float32)
    keep_mask = member.astype(jnp.float32)
    return jnp.stack([grad_real * keep_mask, grad_imag * keep_mask])

def reference(illumination, excitation, beam_group, positions, params, span_rows, span_cols, surface_coef, directions, cover_blocks, cover_count):
    beam_count = excitation.shape[1]
    member = jnp.arange(FEEDS, dtype=jnp.int32)[None, :] // GROUP_SIZE == beam_group[:, None]
    weights = spline_weights(params)
    coef_index = spline_index(span_rows, span_cols)
    height = lax.optimization_barrier(jnp.sum(weights * surface_coef[coef_index], axis=0))
    current = currents(illumination, excitation, member)
    field_scale = 1.0 / math.sqrt(PTS)
    dir_groups = directions.reshape(2, NDB // GRP, GRP * BLOCK).transpose(1, 0, 2)
    fld_re, fld_im = forward_fields(current, positions, height, dir_groups, field_scale)
    group_idx = cover_blocks // GRP
    sub_idx = cover_blocks % GRP
    beam_idx = jnp.arange(beam_count, dtype=jnp.int32)[:, None]
    cov_re = fld_re.reshape(NDB // GRP, beam_count, GRP, BLOCK)[group_idx, beam_idx, sub_idx]
    cov_im = fld_im.reshape(NDB // GRP, beam_count, GRP, BLOCK)[group_idx, beam_idx, sub_idx]
    is_live = (jnp.arange(CBMAX, dtype=jnp.int32)[None, :] < cover_count[:, None])[:, :, None]
    neg_gain = -SHARPNESS * (cov_re * cov_re + cov_im * cov_im)
    masked = jnp.where(is_live, neg_gain, -1e+30)
    peak_score = jnp.max(masked)
    expo_terms = jnp.exp(masked - peak_score)
    denom_sum = jnp.sum(expo_terms)
    objective = -(peak_score + jnp.log(denom_sum)) / SHARPNESS
    sens_re = (2.0 * (expo_terms / denom_sum) * cov_re).astype(jnp.bfloat16)
    sens_im = (2.0 * (expo_terms / denom_sum) * cov_im).astype(jnp.bfloat16)
    grid_re = to_grid(sens_re, group_idx, beam_idx, sub_idx, beam_count)
    grid_im = to_grid(sens_im, group_idx, beam_idx, sub_idx, beam_count)
    back_cos, back_sin = backward_terms(positions, height, dir_groups, grid_re, grid_im)
    nb = beam_count
    grad_cur_re = field_scale * (back_cos[:nb] + back_sin[nb:2 * nb])
    grad_cur_im = field_scale * (back_cos[nb:2 * nb] - back_sin[:nb])
    turn_re = back_cos[3 * nb:] - back_sin[2 * nb:3 * nb]
    turn_im = -back_cos[2 * nb:3 * nb] - back_sin[3 * nb:]
    cur_f32 = current.astype(jnp.float32)
    slope = field_scale * lax.optimization_barrier(jnp.sum(cur_f32[:nb] * turn_re + cur_f32[nb:] * turn_im, axis=0))
    grad_coef = jax.ops.segment_sum((weights * slope[None, :]).reshape(-1), coef_index.reshape(-1), num_segments=NC)
    grad_exc = excitation_grad(grad_cur_re, grad_cur_im, illumination, member)
    return (objective, grad_coef, grad_exc)
```

```python
import functools
import math

import jax
import jax.numpy as jnp
from jax import lax
from jax.experimental import pallas as pl
from jax.experimental.pallas import tpu as pltpu
from jax.sharding import PartitionSpec as P

MESH = pl.DeviceIdType.MESH
F32 = jnp.float32
BF16 = jnp.bfloat16

GROUP_SIZE = 25
BEAMS = 200
NDB = 64
BLOCK = 128
CBMAX = 8
NCV = 64
NC = 4096
SHARPNESS = 2.0
TWO_PI = 2.0 * math.pi

FEED = 4
PTSD = 32
PLOC = 512
BP = 256
EB = 208
SLOTS = NDB // FEED
CAP = 384
CH = 24
NEG = -1e30

COS_C = (0.99999921, -19.73898036, 64.92865742, -85.27162153, 58.79049212, -21.07110563)
SIN_C = (6.28318492, -41.34158923, 81.59994333, -76.61447253, 41.34288235, -12.47124354)


def horner(coefs, z):
    acc = jnp.full(z.shape, coefs[-1], F32)
    for c in coefs[-2::-1]:
        acc = acc * z + c
    return acc


def iota(shape, dim):
    return lax.broadcasted_iota(jnp.int32, shape, dim)


def columns(row, n):
    return jnp.transpose(jnp.broadcast_to(row, (n, row.shape[1])))


def dot(a, b):
    return jnp.dot(a, b, preferred_element_type=F32)


def body(
    il_ref, ex_ref, bg_ref, pos_ref, par_ref, row_ref, col_ref, coef_ref, dir_ref, cb_ref, cnt_ref,
    obj_ref, gcoef_ref, gexc_ref,
    il_all, e_all, dirx, diry, xb, yb, hb, w16, kall, rates, pad_a, pad_b,
    rt_s, mt_s, rank_s, rs_s, ms_s, off_s, end_s, ohm, oh, multb, jre, jim, jtre, jtim, jsel,
    fbuf, frecv, agbuf, covre, covim, st, rhs, accs, stats, gbuf, grecv, fb, gag,
    il_ss, il_rs, e_ss, e_rs, rs_ss, rs_rs, ag_ss, ag_rs, st_ss, st_rs, g_ss, g_rs, b_ss, b_rs, c_ss, c_rs,
):
    f = lax.axis_index("feed")
    p = lax.axis_index("pts")
    sib = f + 1 - 2 * (f % 2)
    par = (f + 2) % FEED
    par_sib = (sib + 2) % FEED

    barrier = pltpu.get_barrier_semaphore()

    def greet(d, carry):
        pl.semaphore_signal(barrier, inc=1, device_id={"pts": (p + d) % PTSD}, device_id_type=MESH)
        return carry

    lax.fori_loop(1, PTSD, greet, 0)
    for d in range(1, FEED):
        pl.semaphore_signal(barrier, inc=1, device_id={"feed": (f + d) % FEED}, device_id_type=MESH)

    r64 = iota((64, 50), 0)
    place = jnp.where(
        (iota((64, 50), 1) == GROUP_SIZE * (r64 // 32) + r64 % 32) & (r64 % 32 < GROUP_SIZE), 1.0, 0.0
    ).astype(BF16)
    il_all[f, 0:64, :] = dot(place, il_ref[0]).astype(BF16)
    il_all[f, 64:128, :] = dot(place, il_ref[1]).astype(BF16)

    pad_a[...] = jnp.full((8, BP), -1.0, F32)
    pad_a[0:1, 0:BEAMS] = bg_ref[...].astype(F32)
    grp_row = pad_a[0:1, :]
    l128 = iota((50, 128), 1)
    r50 = iota((50, 128), 0)
    lane_feed = GROUP_SIZE * ((l128 % 64) // 32) + l128 % 32
    fits = (r50 == lane_feed) & (l128 % 32 < GROUP_SIZE)
    q_re = jnp.where(fits & (l128 < 64), 1.0, 0.0).astype(BF16)
    q_im = jnp.where(fits & (l128 >= 64), 1.0, 0.0).astype(BF16)
    ex = dot(ex_ref[0], q_re) + dot(ex_ref[1], q_im)
    grp_cols = columns(grp_row, 128)[0:BEAMS, :]
    lane_grp = ((iota((BEAMS, 128), 1) % 64) // 32 + 2 * f).astype(F32)
    e_all[f, 0:BEAMS, :] = jnp.where(grp_cols == lane_grp, ex, 0.0).astype(BF16)
    e_all[f, BEAMS:EB, :] = jnp.zeros((EB - BEAMS, 128), BF16)

    pl.semaphore_wait(barrier, PTSD - 1 + FEED - 1)

    def feed_copy(buf, slot, target, ss, rs, k):
        return pltpu.make_async_remote_copy(
            src_ref=buf.at[slot], dst_ref=buf.at[slot], send_sem=ss.at[k], recv_sem=rs.at[k],
            device_id={"feed": target}, device_id_type=MESH,
        )

    il_copies = [feed_copy(il_all, f, par, il_ss, il_rs, 0), feed_copy(il_all, f, sib, il_ss, il_rs, 1)]
    e_copies = [feed_copy(e_all, f, par, e_ss, e_rs, 0), feed_copy(e_all, f, sib, e_ss, e_rs, 1)]
    e_copies[0].start()
    il_copies[0].start()
    e_copies[1].start()
    il_copies[1].start()

    pad_b[...] = jnp.full((BP, 128), -1.0, F32)
    pad_b[0:BEAMS, 0:CBMAX] = cb_ref[...].astype(F32)
    pad_a[...] = jnp.zeros((8, BP), F32)
    pad_a[0:1, 0:BEAMS] = cnt_ref[...].astype(F32)
    cover = jnp.transpose(pad_b[...])
    count = pad_a[0:1, :]
    k_io = iota((NDB, BP), 0).astype(F32)
    mult = jnp.zeros((NDB, BP), F32)
    for c in range(CBMAX):
        mult = mult + jnp.where((cover[c : c + 1, :] == k_io) & (count > c), 1.0, 0.0)
    ind = jnp.where(mult > 0.0, 1.0, 0.0)
    n_col = jnp.sum(ind, axis=1, keepdims=True)
    n_b = jnp.broadcast_to(n_col, (NDB, 128))
    n_row = jnp.transpose(jnp.concatenate([n_b, jnp.full((NDB, 128), -1.0, F32)], 0))[0:1, :]
    lane = iota((NDB, 128), 1)
    sub = iota((NDB, 128), 0)
    ahead = (n_row > n_b) | ((n_row == n_b) & (lane < sub))
    rank = jnp.sum(jnp.where(ahead, 1.0, 0.0), axis=1, keepdims=True)
    rank_b = jnp.broadcast_to(rank, (NDB, 128))

    def deal(r):
        level = jnp.floor(r * 0.25)
        odd = level - 2.0 * jnp.floor(level * 0.5)
        place_in = r - 4.0 * level
        return level, jnp.where(odd > 0.5, 3.0 - place_in, place_in)

    fq = f.astype(F32)
    lev_b, bin_b = deal(rank_b)
    rank_row = jnp.transpose(jnp.concatenate([rank_b, jnp.full((NDB, 128), 400.0, F32)], 0))[0:1, :]
    lev_row, bin_row = deal(rank_row)
    before = (bin_row == fq) & (lev_row < lev_b) & (lane < NDB)
    off_col = jnp.sum(jnp.where(before, n_row, 0.0), axis=1, keepdims=True)
    upper = jnp.where(iota((BP, BP), 0) < iota((BP, BP), 1), 1.0, 0.0).astype(BF16)
    prefix = dot(ind.astype(BF16), upper)
    mine = (ind > 0.0) & (bin_b[:, 0:1] == fq)
    rt_s[...] = jnp.where(mine, prefix + off_col, -1.0)
    mt_s[...] = mult
    rank_s[...] = rank_b
    off_b = jnp.broadcast_to(off_col, (NDB, 128))

    def target(s):
        return 4 * s + f + (s % 2) * (3 - 2 * f)

    for s in range(SLOTS):
        is_s = rank_b == target(s).astype(F32)
        off = jnp.sum(jnp.where(is_s, off_b, 0.0), axis=0, keepdims=True)
        off_s[s : s + 1, :] = off
        end_s[s : s + 1, :] = off + jnp.sum(jnp.where(is_s, n_b, 0.0), axis=0, keepdims=True)
        is_w = is_s[:, 0:1]
        rs_s[s : s + 1, :] = jnp.sum(jnp.where(is_w, rt_s[...], 0.0), axis=0, keepdims=True)
        ms_s[s : s + 1, :] = jnp.sum(jnp.where(is_w, mt_s[...], 0.0), axis=0, keepdims=True)

    def one_hot(rc, carry):
        base = pl.multiple_of(rc * 128, 128)
        rows = (iota((128, BP), 0) + base).astype(F32)
        acc = jnp.zeros((128, BP), F32)
        for s in range(SLOTS):
            acc = jnp.where(rs_s[s : s + 1, :] == rows, ms_s[s : s + 1, :], acc)
        ohm[pl.ds(base, 128), :] = acc.astype(BF16)
        oh[pl.ds(base, 128), :] = jnp.where(acc > 0.0, 1.0, 0.0).astype(BF16)
        multb[pl.ds(base, 128), :] = jnp.broadcast_to(jnp.sum(acc, axis=1, keepdims=True), (128, 128))
        return carry

    lax.fori_loop(0, CAP // 128, one_hot, 0)

    def basis(t):
        m = 1.0 - t
        t2 = t * t
        t3 = t2 * t
        return [
            m * m * m / 6.0,
            (3.0 * t3 - 6.0 * t2 + 4.0) / 6.0,
            (-3.0 * t3 + 3.0 * t2 + 3.0 * t + 1.0) / 6.0,
            t3 / 6.0,
        ]

    bu = basis(par_ref[0:1, :])
    bv = basis(par_ref[1:2, :])
    for i in range(4):
        for j in range(4):
            w16[4 * i + j : 4 * i + j + 1, :] = bu[i] * bv[j]
    heights = []
    for blk in range(PLOC // BLOCK):
        base = row_ref[blk] * NCV + col_ref[blk]
        h = jnp.zeros((1, BLOCK), F32)
        for i in range(4):
            for j in range(4):
                k = 4 * i + j
                h = h + w16[k : k + 1, blk * BLOCK : (blk + 1) * BLOCK] * coef_ref[base + i * NCV + j]
        heights.append(h)
    hb[...] = columns(jnp.concatenate(heights, axis=1), 128)
    xb[...] = columns(pos_ref[0:1, :], 128)
    yb[...] = columns(pos_ref[1:2, :], 128)

    for k in range(NDB):
        dirx[k : k + 1, :] = dir_ref[0:1, k * BLOCK : (k + 1) * BLOCK]
        diry[k : k + 1, :] = dir_ref[1:2, k * BLOCK : (k + 1) * BLOCK]

    def phases(s, carry):
        is_s = rank_s[...] == target(s).astype(F32)
        ux = jnp.sum(jnp.where(is_s, dirx[...], 0.0), axis=0, keepdims=True)
        uy = jnp.sum(jnp.where(is_s, diry[...], 0.0), axis=0, keepdims=True)
        uz1 = 1.0 + jnp.sqrt(1.0 - ux * ux - uy * uy)
        rates[s] = columns(TWO_PI * uz1, 128)
        base = pl.multiple_of(s * 256, 256)
        for c in range(PLOC // 64):
            rows = pl.ds(64 * c, 64)
            t = xb[rows, :] * ux + yb[rows, :] * uy + hb[rows, :] * uz1
            r = t - jnp.round(t)
            z = r * r
            kall[rows, pl.ds(base, 128)] = horner(COS_C, z).astype(BF16)
            kall[rows, pl.ds(base + 128, 128)] = (r * horner(SIN_C, z)).astype(BF16)
        return carry

    lax.fori_loop(0, SLOTS, phases, 0)

    e_copies[0].wait_recv()
    e_copies.append(feed_copy(e_all, par, sib, e_ss, e_rs, 2))
    e_copies[2].start()
    il_copies[0].wait_recv()
    il_copies.append(feed_copy(il_all, par, sib, il_ss, il_rs, 2))
    il_copies[2].start()
    for k in (1, 2):
        e_copies[k].wait_recv()
        il_copies[k].wait_recv()

    exc = jnp.concatenate([e_all[k] for k in range(FEED)], axis=1)
    left = [il_all[k] for k in range(FEED)]
    mix_re = jnp.concatenate([x for b in left for x in (b[0:64, :], -b[64:128, :])], axis=0)
    mix_im = jnp.concatenate([x for b in left for x in (b[64:128, :], b[0:64, :])], axis=0)
    jre[EB:BP, :] = jnp.zeros((BP - EB, PLOC), BF16)
    jim[EB:BP, :] = jnp.zeros((BP - EB, PLOC), BF16)
    jre[0:EB, :] = dot(exc, mix_re).astype(BF16)
    jim[0:EB, :] = dot(exc, mix_im).astype(BF16)
    jsel[0:CAP, :] = dot(oh[...], jre[...]).astype(BF16)
    jsel[CAP : 2 * CAP, :] = dot(oh[...], jim[...]).astype(BF16)

    covre[...] = jnp.zeros((CAP, BLOCK), F32)
    covim[...] = jnp.zeros((CAP, BLOCK), F32)
    scale = 1.0 / math.sqrt(PLOC * PTSD)

    def forward(s, carry):
        base = pl.multiple_of(s * 256, 256)
        prod = dot(jsel[...], kall[:, pl.ds(base, 256)])
        row = iota((CAP, BLOCK), 0).astype(F32)
        own = (row >= off_s[pl.ds(s, 1), :]) & (row < end_s[pl.ds(s, 1), :])
        re = prod[0:CAP, 0:128] - prod[CAP:, 128:]
        im = prod[0:CAP, 128:] + prod[CAP:, 0:128]
        covre[...] = jnp.where(own, re, covre[...])
        covim[...] = jnp.where(own, im, covim[...])
        return carry

    lax.fori_loop(0, SLOTS, forward, 0)

    low = iota((8, BLOCK), 0) < 4
    for c in range(PTSD):
        fbuf[c, 0:8, :] = scale * covre[8 * c : 8 * c + 8, :]
        fbuf[c, 8:16, :] = scale * covim[8 * c : 8 * c + 8, :]
    for t in range(PTSD // 2):
        re = scale * covre[256 + 8 * t : 264 + 8 * t, :]
        im = scale * covim[256 + 8 * t : 264 + 8 * t, :]
        fbuf[2 * t, 16:24, :] = jnp.where(low, re, pltpu.roll(im, 4, 0))
        fbuf[2 * t + 1, 16:24, :] = jnp.where(low, pltpu.roll(re, 4, 0), im)

    def scatter_copy(d, src, dst, ss, rs):
        to = (p + d) % PTSD
        return pltpu.make_async_remote_copy(
            src_ref=src.at[to], dst_ref=dst.at[d - 1], send_sem=ss, recv_sem=rs,
            device_id={"pts": to}, device_id_type=MESH,
        )

    def gather_copy(d, buf, ss, rs):
        return pltpu.make_async_remote_copy(
            src_ref=buf.at[p], dst_ref=buf.at[p], send_sem=ss, recv_sem=rs,
            device_id={"pts": (p + d) % PTSD}, device_id_type=MESH,
        )

    def start_scatter(src, dst, ss, rs):
        def step(d, carry):
            scatter_copy(d, src, dst, ss, rs).start()
            return carry

        lax.fori_loop(1, PTSD, step, 0)

    def start_gather(buf, ss, rs):
        def step(d, carry):
            gather_copy(d, buf, ss, rs).start()
            return carry

        lax.fori_loop(1, PTSD, step, 0)

    def wait_all(buf, sem):
        pltpu.make_async_copy(buf.at[pl.ds(0, PTSD - 1)], buf.at[pl.ds(0, PTSD - 1)], sem).wait()

    start_scatter(fbuf, frecv, rs_ss, rs_rs)
    for n in range(PLOC // 128):
        rows = pl.ds(n * 128, 128)
        jtre[rows, :] = jnp.transpose(jre[:, n * 128 : (n + 1) * 128].astype(F32))
        jtim[rows, :] = jnp.transpose(jim[:, n * 128 : (n + 1) * 128].astype(F32))
    wait_all(frecv, rs_rs)
    whole = fbuf[p]
    for d in range(PTSD - 1):
        whole = whole + frecv[d]
    agbuf[p] = whole
    start_gather(agbuf, ag_ss, ag_rs)
    wait_all(fbuf, rs_ss)
    wait_all(agbuf, ag_rs)

    for c in range(PTSD):
        covre[8 * c : 8 * c + 8, :] = agbuf[c, 0:8, :]
        covim[8 * c : 8 * c + 8, :] = agbuf[c, 8:16, :]
    for t in range(PTSD // 2):
        even = agbuf[2 * t, 16:24, :]
        odd = agbuf[2 * t + 1, 16:24, :]
        covre[256 + 8 * t : 264 + 8 * t, :] = jnp.where(low, even, pltpu.roll(odd, 4, 0))
        covim[256 + 8 * t : 264 + 8 * t, :] = jnp.where(low, pltpu.roll(even, 4, 0), odd)
    cre = covre[...]
    cim = covim[...]
    mrow = multb[...]
    neg = jnp.where(mrow > 0.0, -SHARPNESS * (cre * cre + cim * cim), NEG)
    peak = jnp.max(jnp.max(neg, axis=0, keepdims=True), axis=1, keepdims=True)
    expo = jnp.where(mrow > 0.0, jnp.exp(neg - peak), 0.0)
    part = jnp.sum(jnp.sum(mrow * expo, axis=0, keepdims=True), axis=1, keepdims=True)
    first = iota((8, BLOCK), 0) < 1
    stats[f] = jnp.where(first, jnp.broadcast_to(peak, (8, BLOCK)), jnp.broadcast_to(part, (8, BLOCK)))

    def feed_copies(buf, ss, rs):
        return [
            pltpu.make_async_remote_copy(
                src_ref=buf.at[f], dst_ref=buf.at[f], send_sem=ss.at[d - 1], recv_sem=rs.at[d - 1],
                device_id={"feed": (f + d) % FEED}, device_id_type=MESH,
            )
            for d in range(1, FEED)
        ]

    st_copies = feed_copies(stats, st_ss, st_rs)
    for c in st_copies:
        c.start()
    twice = 2.0 * expo
    st[0:128, :] = jnp.transpose(twice * cre)
    st[128:256, :] = jnp.transpose(twice * cim)

    def spread(s, carry):
        lanes = iota((1, CAP), 1).astype(F32)
        own = (lanes >= off_s[pl.ds(s, 1), 0:1]) & (lanes < end_s[pl.ds(s, 1), 0:1])
        part_s = jnp.where(own, st[...], 0.0).astype(BF16)
        grid = dot(part_s, ohm[...]).astype(BF16)
        gridf = grid.astype(F32)
        rate = jnp.concatenate([rates[s], rates[s]], axis=1)
        rr = (rate * gridf[0:128, :]).astype(BF16)
        ri = (rate * gridf[128:256, :]).astype(BF16)
        sr = grid[0:128, :]
        si = grid[128:256, :]
        top = pl.ds(pl.multiple_of(s * 256, 256), 128)
        bot = pl.ds(pl.multiple_of(s * 256 + 128, 128), 128)
        rhs[0, top, :] = sr
        rhs[1, top, :] = si
        rhs[2, top, :] = ri
        rhs[3, top, :] = -rr
        rhs[0, bot, :] = si
        rhs[1, bot, :] = -sr
        rhs[2, bot, :] = -rr
        rhs[3, bot, :] = -ri
        return carry

    lax.fori_loop(0, SLOTS, spread, 0)

    def backward(n, carry):
        accs[n] = dot(kall[...], rhs[n])
        return carry

    lax.fori_loop(0, 4, backward, 0)

    for c in st_copies:
        c.wait_recv()
    peaks = [stats[k, 0:1, 0:1] for k in range(FEED)]
    parts = [stats[k, 1:2, 0:1] for k in range(FEED)]
    top_peak = jnp.maximum(jnp.maximum(peaks[0], peaks[1]), jnp.maximum(peaks[2], peaks[3]))
    denom = sum(parts[k] * jnp.exp(peaks[k] - top_peak) for k in range(FEED))
    obj_ref[...] = -(top_peak + jnp.log(denom)) / SHARPNESS
    factor = scale * jnp.exp(peak - top_peak) / denom

    slope = factor * jnp.sum(jtre[...] * accs[2] + jtim[...] * accs[3], axis=1, keepdims=True)
    slope_row = jnp.transpose(jnp.broadcast_to(slope, (PLOC, 128)))[0:1, :]
    weighted = w16[...] * slope_row
    m = iota((32, 128), 0) * 128 + iota((32, 128), 1)
    grid_coef = jnp.zeros((32, 128), F32)
    for blk in range(PLOC // BLOCK):
        sums = jnp.sum(weighted[:, blk * BLOCK : (blk + 1) * BLOCK], axis=1, keepdims=True)
        i = m // NCV - row_ref[blk]
        j = m % NCV - col_ref[blk]
        key = jnp.where((i >= 0) & (i < 4) & (j >= 0) & (j < 4), 4 * i + j, -1)
        for k in range(16):
            grid_coef = grid_coef + jnp.where(key == k, sums[k : k + 1, :], 0.0)

    grad = jnp.concatenate([(factor * accs[0]).astype(BF16), (factor * accs[1]).astype(BF16)], axis=1)
    light = jnp.concatenate([il_all[k] for k in range(FEED)], axis=0)
    prod = dot(light, grad)
    pad_a[...] = jnp.full((8, BP), -1.0, F32)
    pad_a[0:1, 0:BEAMS] = bg_ref[...].astype(F32)
    grp = pad_a[0:1, :]
    ge_re = jnp.zeros((32, BP), F32)
    ge_im = jnp.zeros((32, BP), F32)
    for k in range(FEED):
        up = prod[128 * k : 128 * k + 64, :]
        dn = prod[128 * k + 64 : 128 * k + 128, :]
        re = up[:, 0:BP] + dn[:, BP:]
        im = up[:, BP:] - dn[:, 0:BP]
        for h in range(2):
            own = grp == float(2 * k + h)
            ge_re = ge_re + jnp.where(own, re[32 * h : 32 * h + 32, :], 0.0)
            ge_im = ge_im + jnp.where(own, im[32 * h : 32 * h + 32, :], 0.0)
    gbuf[...] = jnp.zeros((PTSD, 8, 128), F32)
    pieces = (ge_re[:, 0:128], ge_re[:, 128:], ge_im[:, 0:128], ge_im[:, 128:], grid_coef)
    for k, piece in enumerate(pieces):
        for c in range(PTSD):
            gbuf[c, k : k + 1, :] = piece[c : c + 1, :]

    start_scatter(gbuf, grecv, g_ss, g_rs)
    wait_all(grecv, g_rs)
    tile = gbuf[p]
    for d in range(PTSD - 1):
        tile = tile + grecv[d]
    fb[f] = tile
    fb_copies = feed_copies(fb, b_ss, b_rs)
    for c in fb_copies:
        c.start()
    for c in fb_copies:
        c.wait_recv()
    gag[p] = (fb[0] + fb[1]) + (fb[2] + fb[3])
    start_gather(gag, c_ss, c_rs)
    wait_all(gag, c_rs)

    for c in range(PTSD):
        gcoef_ref[c : c + 1, :] = gag[c, 4:5, :]
    half = [jnp.concatenate([gag[c, k : k + 1, :] for c in range(PTSD)], axis=0) for k in range(4)]
    for k in range(2):
        rows = jnp.concatenate([half[2 * k], half[2 * k + 1]], axis=1)
        pad_b[0:64, 0:128] = jnp.zeros((64, 128), F32)
        for b in range(2):
            lanes = slice(128 * b, 128 * b + 128)
            keep0 = grp[:, lanes] == (2 * f).astype(F32)
            keep1 = grp[:, lanes] == (2 * f + 1).astype(F32)
            pad_b[128 * b : 128 * b + 128, :] = jnp.zeros((128, 128), F32)
            pad_b[128 * b : 128 * b + GROUP_SIZE, :] = jnp.where(keep0, rows[0:GROUP_SIZE, lanes], 0.0)
            pad_b[128 * b + GROUP_SIZE : 128 * b + 2 * GROUP_SIZE, :] = jnp.where(
                keep1, rows[0:GROUP_SIZE, lanes], 0.0
            )
            out = jnp.transpose(pad_b[128 * b : 128 * b + 128, :])
            n = min(128, BEAMS - 128 * b)
            gexc_ref[k, 128 * b : 128 * b + n, :] = out[0:n, 0 : 2 * GROUP_SIZE]

    for c in il_copies + e_copies + st_copies + fb_copies:
        c.wait_send()
    wait_all(agbuf, ag_ss)
    wait_all(gbuf, g_ss)
    wait_all(gag, c_ss)


def local(
    illumination,
    excitation,
    beam_group,
    positions,
    params,
    span_rows,
    span_cols,
    surface_coef,
    directions,
    cover_blocks,
    cover_count,
):
    vmem = pl.BlockSpec(memory_space=pltpu.VMEM)
    smem = pl.BlockSpec(memory_space=pltpu.SMEM)
    dma = pltpu.SemaphoreType.DMA
    scratch = [
        pltpu.VMEM((FEED, 128, PLOC), BF16),
        pltpu.VMEM((FEED, EB, 128), BF16),
        pltpu.VMEM((NDB, BLOCK), F32),
        pltpu.VMEM((NDB, BLOCK), F32),
        pltpu.VMEM((PLOC, 128), F32),
        pltpu.VMEM((PLOC, 128), F32),
        pltpu.VMEM((PLOC, 128), F32),
        pltpu.VMEM((16, PLOC), F32),
        pltpu.VMEM((PLOC, SLOTS * 256), BF16),
        pltpu.VMEM((SLOTS, 128, 128), F32),
        pltpu.VMEM((8, BP), F32),
        pltpu.VMEM((BP, 128), F32),
        pltpu.VMEM((NDB, BP), F32),
        pltpu.VMEM((NDB, BP), F32),
        pltpu.VMEM((NDB, 128), F32),
        pltpu.VMEM((SLOTS, BP), F32),
        pltpu.VMEM((SLOTS, BP), F32),
        pltpu.VMEM((SLOTS, 128), F32),
        pltpu.VMEM((SLOTS, 128), F32),
        pltpu.VMEM((CAP, BP), BF16),
        pltpu.VMEM((CAP, BP), BF16),
        pltpu.VMEM((CAP, 128), F32),
        pltpu.VMEM((BP, PLOC), BF16),
        pltpu.VMEM((BP, PLOC), BF16),
        pltpu.VMEM((PLOC, BP), F32),
        pltpu.VMEM((PLOC, BP), F32),
        pltpu.VMEM((2 * CAP, PLOC), BF16),
        pltpu.VMEM((PTSD, CH, 128), F32),
        pltpu.VMEM((PTSD - 1, CH, 128), F32),
        pltpu.VMEM((PTSD, CH, 128), F32),
        pltpu.VMEM((CAP, 128), F32),
        pltpu.VMEM((CAP, 128), F32),
        pltpu.VMEM((256, CAP), F32),
        pltpu.VMEM((4, SLOTS * 256, BP), BF16),
        pltpu.VMEM((4, PLOC, BP), F32),
        pltpu.VMEM((FEED, 8, 128), F32),
        pltpu.VMEM((PTSD, 8, 128), F32),
        pltpu.VMEM((PTSD - 1, 8, 128), F32),
        pltpu.VMEM((FEED, 8, 128), F32),
        pltpu.VMEM((PTSD, 8, 128), F32),
        dma((3,)), dma((3,)), dma((3,)), dma((3,)),
        dma, dma, dma, dma,
        dma((3,)), dma((3,)),
        dma, dma,
        dma((3,)), dma((3,)),
        dma, dma,
    ]
    objective, grad_coef, grad_exc = pl.pallas_call(
        body,
        out_shape=(
            jax.ShapeDtypeStruct((1, 1), F32),
            jax.ShapeDtypeStruct((32, 128), F32),
            jax.ShapeDtypeStruct((2, BEAMS, 2 * GROUP_SIZE), F32),
        ),
        in_specs=[vmem, vmem, vmem, vmem, vmem, smem, smem, smem, vmem, vmem, vmem],
        out_specs=(vmem, vmem, vmem),
        scratch_shapes=scratch,
        compiler_params=pltpu.CompilerParams(
            collective_id=0, has_side_effects=True, vmem_limit_bytes=48 * 1024 * 1024
        ),
        name="coverage",
    )(
        illumination,
        excitation,
        beam_group.reshape(1, BEAMS),
        positions,
        params,
        span_rows,
        span_cols,
        surface_coef,
        directions,
        cover_blocks,
        cover_count.reshape(1, BEAMS),
    )
    return objective.reshape(()), grad_coef.reshape(NC), grad_exc


def solution(mesh):
    return jax.shard_map(
        local,
        mesh=mesh,
        in_specs=(
            P(None, "feed", "pts"),
            P(None, None, "feed"),
            P(),
            P(None, "pts"),
            P(None, "pts"),
            P("pts"),
            P("pts"),
            P(),
            P(),
            P(),
            P(),
        ),
        out_specs=(P(), P(), P(None, None, "feed")),
        check_vma=False,
    )
```

```python
import functools
import math

import jax
import jax.numpy as jnp
from jax import lax
from jax.experimental import pallas as pl
from jax.experimental.pallas import tpu as pltpu
from jax.sharding import PartitionSpec as P

MESH = pl.DeviceIdType.MESH
F32 = jnp.float32
BF16 = jnp.bfloat16

GROUP_SIZE = 25
BEAMS = 200
NDB = 64
BLOCK = 128
CBMAX = 8
NCV = 64
NC = 4096
SHARPNESS = 2.0
TWO_PI = 2.0 * math.pi

FEED = 4
PTSD = 32
PLOC = 512
BP = 256
EB = 208
SLOTS = NDB // FEED
CAP = 384
CH = 24
NEG = -1e30
PAIRS = 900
WIDTH = tuple(-(-min(BEAMS, PAIRS // (FEED * s + 1)) // 16) * 16 for s in range(SLOTS))
BASE = tuple(sum(WIDTH[:s]) for s in range(SLOTS))
ROWS = -(-sum(WIDTH) // 128) * 128
PLANE = 16
RING = 8

COS_C = (0.99999921, -19.73898036, 64.92865742, -85.27162153, 58.79049212, -21.07110563)
SIN_C = (6.28318492, -41.34158923, 81.59994333, -76.61447253, 41.34288235, -12.47124354)


def horner(coefs, z):
    acc = jnp.full(z.shape, coefs[-1], F32)
    for c in coefs[-2::-1]:
        acc = acc * z + c
    return acc


def iota(shape, dim):
    return lax.broadcasted_iota(jnp.int32, shape, dim)


def columns(row, n):
    return jnp.transpose(jnp.broadcast_to(row, (n, row.shape[1])))


def dot(a, b):
    return jnp.dot(a, b, preferred_element_type=F32)


def body(
    il_ref, ex_ref, bg_ref, pos_ref, par_ref, row_ref, col_ref, coef_ref, dir_ref, cb_ref, cnt_ref,
    obj_ref, gcoef_ref, gexc_ref,
    il_all, e_all, dirx, diry, xb, yb, hb, w16, kall, rates, pad_a, pad_b,
    rt_s, mt_s, rank_s, ohb, ohbt, ohc, ohct, multq, multb, jre, jim, jlre, jlim, fs,
    fbuf, frecv, agbuf, covre, covim, sens, grid, yg, stats, gbuf, grecv, fb, gag, ring_sem, plane_sem,
    il_ss, il_rs, e_ss, e_rs, rs_ss, rs_rs, ag_ss, ag_rs, st_ss, st_rs, g_ss, g_rs, b_ss, b_rs, c_ss, c_rs,
):
    f = lax.axis_index("feed")
    p = lax.axis_index("pts")
    sib = f + 1 - 2 * (f % 2)
    par = (f + 2) % FEED
    par_sib = (sib + 2) % FEED

    barrier = pltpu.get_barrier_semaphore()
    far = p // PLANE
    flat = p % PLANE
    y = p % 4
    z = flat // 4
    y_ring = [{"pts": p - y + (y + d) % 4} for d in range(1, 4)]
    z_ring = [{"pts": p - 4 * z + 4 * ((z + d) % 4)} for d in range(1, 4)]
    across = {"pts": (p + PLANE) % PTSD}
    x_ring = [
        {"feed": (f + d // 2) % FEED, "pts": (p + PLANE * (d % 2)) % PTSD} for d in range(1, RING)
    ]
    greeted = y_ring + z_ring + x_ring
    for to in greeted:
        pl.semaphore_signal(barrier, inc=1, device_id=to, device_id_type=MESH)

    r64 = iota((64, 50), 0)
    place = jnp.where(
        (iota((64, 50), 1) == GROUP_SIZE * (r64 // 32) + r64 % 32) & (r64 % 32 < GROUP_SIZE), 1.0, 0.0
    ).astype(BF16)
    il_all[f, 0:64, :] = dot(place, il_ref[0]).astype(BF16)
    il_all[f, 64:128, :] = dot(place, il_ref[1]).astype(BF16)

    pad_a[...] = jnp.full((8, BP), -1.0, F32)
    pad_a[0:1, 0:BEAMS] = bg_ref[...].astype(F32)
    grp_row = pad_a[0:1, :]
    l128 = iota((50, 128), 1)
    r50 = iota((50, 128), 0)
    lane_feed = GROUP_SIZE * ((l128 % 64) // 32) + l128 % 32
    fits = (r50 == lane_feed) & (l128 % 32 < GROUP_SIZE)
    q_re = jnp.where(fits & (l128 < 64), 1.0, 0.0).astype(BF16)
    q_im = jnp.where(fits & (l128 >= 64), 1.0, 0.0).astype(BF16)
    ex = dot(ex_ref[0], q_re) + dot(ex_ref[1], q_im)
    grp_cols = columns(grp_row, 128)[0:BEAMS, :]
    lane_grp = ((iota((BEAMS, 128), 1) % 64) // 32 + 2 * f).astype(F32)
    e_all[f, 0:BEAMS, :] = jnp.where(grp_cols == lane_grp, ex, 0.0).astype(BF16)
    e_all[f, BEAMS:EB, :] = jnp.zeros((EB - BEAMS, 128), BF16)

    pl.semaphore_wait(barrier, len(greeted))
    for to in y_ring:
        pl.semaphore_signal(ring_sem, inc=1, device_id=to, device_id_type=MESH)

    def feed_copy(buf, slot, target, ss, rs, k):
        return pltpu.make_async_remote_copy(
            src_ref=buf.at[slot], dst_ref=buf.at[slot], send_sem=ss.at[k], recv_sem=rs.at[k],
            device_id={"feed": target}, device_id_type=MESH,
        )

    il_copies = [feed_copy(il_all, f, par, il_ss, il_rs, 0), feed_copy(il_all, f, sib, il_ss, il_rs, 1)]
    e_copies = [feed_copy(e_all, f, par, e_ss, e_rs, 0), feed_copy(e_all, f, sib, e_ss, e_rs, 1)]
    e_copies[0].start()
    il_copies[0].start()
    e_copies[1].start()
    il_copies[1].start()

    pad_b[...] = jnp.full((BP, 128), -1.0, F32)
    pad_b[0:BEAMS, 0:CBMAX] = cb_ref[...].astype(F32)
    pad_a[...] = jnp.zeros((8, BP), F32)
    pad_a[0:1, 0:BEAMS] = cnt_ref[...].astype(F32)
    cover = jnp.transpose(pad_b[...])
    count = pad_a[0:1, :]
    k_io = iota((NDB, BP), 0).astype(F32)
    mult = jnp.zeros((NDB, BP), F32)
    for c in range(CBMAX):
        mult = mult + jnp.where((cover[c : c + 1, :] == k_io) & (count > c), 1.0, 0.0)
    ind = jnp.where(mult > 0.0, 1.0, 0.0)
    n_col = jnp.sum(ind, axis=1, keepdims=True)
    n_b = jnp.broadcast_to(n_col, (NDB, 128))
    n_row = jnp.transpose(jnp.concatenate([n_b, jnp.full((NDB, 128), -1.0, F32)], 0))[0:1, :]
    lane = iota((NDB, 128), 1)
    sub = iota((NDB, 128), 0)
    ahead = (n_row > n_b) | ((n_row == n_b) & (lane < sub))
    rank = jnp.sum(jnp.where(ahead, 1.0, 0.0), axis=1, keepdims=True)
    rank_b = jnp.broadcast_to(rank, (NDB, 128))

    def deal(r):
        level = jnp.floor(r * 0.25)
        odd = level - 2.0 * jnp.floor(level * 0.5)
        place_in = r - 4.0 * level
        return level, jnp.where(odd > 0.5, 3.0 - place_in, place_in)

    fq = f.astype(F32)
    lev_b, bin_b = deal(rank_b)
    rank_row = jnp.transpose(jnp.concatenate([rank_b, jnp.full((NDB, 128), 400.0, F32)], 0))[0:1, :]
    lev_row, bin_row = deal(rank_row)
    before = (bin_row == fq) & (lev_row < lev_b) & (lane < NDB)
    off_col = jnp.sum(jnp.where(before, n_row, 0.0), axis=1, keepdims=True)
    upper = jnp.where(iota((BP, BP), 0) < iota((BP, BP), 1), 1.0, 0.0).astype(BF16)
    rt_s[...] = jnp.where(ind > 0.0, dot(ind.astype(BF16), upper), -1.0)
    mt_s[...] = mult
    rank_s[...] = rank_b
    off_b = jnp.broadcast_to(off_col, (NDB, 128))

    def target(s):
        return 4 * s + f + (s % 2) * (3 - 2 * f)

    used = BASE[-1] + WIDTH[-1]
    ohb[used:ROWS, :] = jnp.zeros((ROWS - used, BP), BF16)
    ohct[used:ROWS, :] = jnp.zeros((ROWS - used, CAP), BF16)
    multq[used:ROWS, :] = jnp.zeros((ROWS - used, 128), F32)
    for s in range(SLOTS):
        rows = slice(BASE[s], BASE[s] + WIDTH[s])
        is_s = rank_b == target(s).astype(F32)
        off = jnp.sum(jnp.where(is_s, off_b, 0.0), axis=0, keepdims=True)[:, 0:1]
        load = jnp.sum(jnp.where(is_s, n_b, 0.0), axis=0, keepdims=True)[:, 0:1]
        is_w = is_s[:, 0:1]
        order = jnp.sum(jnp.where(is_w, rt_s[...], 0.0), axis=0, keepdims=True)
        times = jnp.sum(jnp.where(is_w, mt_s[...], 0.0), axis=0, keepdims=True)
        hit = order == iota((WIDTH[s], BP), 0).astype(F32)
        ohb[rows, :] = jnp.where(hit, 1.0, 0.0).astype(BF16)
        multq[rows, :] = jnp.broadcast_to(
            jnp.sum(jnp.where(hit, times, 0.0), axis=1, keepdims=True), (WIDTH[s], 128)
        )
        w = iota((WIDTH[s], CAP), 0).astype(F32)
        r = iota((WIDTH[s], CAP), 1).astype(F32)
        ohct[rows, :] = jnp.where((r - w == off) & (w < load), 1.0, 0.0).astype(BF16)
    for n in range(ROWS // 128):
        cols = slice(128 * n, 128 * n + 128)
        ohc[:, cols] = jnp.transpose(ohct[cols, :].astype(F32)).astype(BF16)

    def basis(t):
        m = 1.0 - t
        t2 = t * t
        t3 = t2 * t
        return [
            m * m * m / 6.0,
            (3.0 * t3 - 6.0 * t2 + 4.0) / 6.0,
            (-3.0 * t3 + 3.0 * t2 + 3.0 * t + 1.0) / 6.0,
            t3 / 6.0,
        ]

    bu = basis(par_ref[0:1, :])
    bv = basis(par_ref[1:2, :])
    for i in range(4):
        for j in range(4):
            w16[4 * i + j : 4 * i + j + 1, :] = bu[i] * bv[j]
    heights = []
    for blk in range(PLOC // BLOCK):
        base = row_ref[blk] * NCV + col_ref[blk]
        h = jnp.zeros((1, BLOCK), F32)
        for i in range(4):
            for j in range(4):
                k = 4 * i + j
                h = h + w16[k : k + 1, blk * BLOCK : (blk + 1) * BLOCK] * coef_ref[base + i * NCV + j]
        heights.append(h)
    hb[...] = columns(jnp.concatenate(heights, axis=1), 128)
    xb[...] = columns(pos_ref[0:1, :], 128)
    yb[...] = columns(pos_ref[1:2, :], 128)

    for k in range(NDB):
        dirx[k : k + 1, :] = dir_ref[0:1, k * BLOCK : (k + 1) * BLOCK]
        diry[k : k + 1, :] = dir_ref[1:2, k * BLOCK : (k + 1) * BLOCK]

    def phases(s, carry):
        is_s = rank_s[...] == target(s).astype(F32)
        ux = jnp.sum(jnp.where(is_s, dirx[...], 0.0), axis=0, keepdims=True)
        uy = jnp.sum(jnp.where(is_s, diry[...], 0.0), axis=0, keepdims=True)
        uz1 = 1.0 + jnp.sqrt(1.0 - ux * ux - uy * uy)
        rates[pl.ds(s, 1), :] = TWO_PI * uz1
        base = pl.multiple_of(s * 256, 256)
        for c in range(PLOC // 64):
            rows = pl.ds(64 * c, 64)
            t = xb[rows, :] * ux + yb[rows, :] * uy + hb[rows, :] * uz1
            r = t - jnp.round(t)
            z = r * r
            kall[rows, pl.ds(base, 128)] = horner(COS_C, z).astype(BF16)
            kall[rows, pl.ds(base + 128, 128)] = (r * horner(SIN_C, z)).astype(BF16)
        return carry

    lax.fori_loop(0, SLOTS, phases, 0)

    pl.semaphore_wait(ring_sem, len(y_ring))
    pl.semaphore_signal(plane_sem, inc=1, device_id=across, device_id_type=MESH)

    e_copies[0].wait_recv()
    e_copies.append(feed_copy(e_all, par, sib, e_ss, e_rs, 2))
    e_copies[2].start()
    il_copies[0].wait_recv()
    il_copies.append(feed_copy(il_all, par, sib, il_ss, il_rs, 2))
    il_copies[2].start()
    for k in (1, 2):
        e_copies[k].wait_recv()
        il_copies[k].wait_recv()

    exc = jnp.concatenate([e_all[k] for k in range(FEED)], axis=1)
    left = [il_all[k] for k in range(FEED)]
    mix_re = jnp.concatenate([x for b in left for x in (b[0:64, :], -b[64:128, :])], axis=0)
    mix_im = jnp.concatenate([x for b in left for x in (b[64:128, :], b[0:64, :])], axis=0)
    jre[EB:BP, :] = jnp.zeros((BP - EB, PLOC), BF16)
    jim[EB:BP, :] = jnp.zeros((BP - EB, PLOC), BF16)
    jre[0:EB, :] = dot(exc, mix_re).astype(BF16)
    jim[0:EB, :] = dot(exc, mix_im).astype(BF16)
    jlre[...] = dot(ohb[...], jre[...]).astype(BF16)
    jlim[...] = dot(ohb[...], jim[...]).astype(BF16)
    scale = 1.0 / math.sqrt(PLOC * PTSD)

    fs[used:ROWS, :] = jnp.zeros((ROWS - used, 512), BF16)
    for s in range(SLOTS):
        w = WIDTH[s]
        rows = slice(BASE[s], BASE[s] + w)
        prod = dot(jnp.concatenate([jlre[rows, :], jlim[rows, :]], axis=0), kall[:, 256 * s : 256 * s + 256])
        re = prod[0:w, 0:128] - prod[w:, 128:]
        im = prod[0:w, 128:] + prod[w:, 0:128]
        for k, val in enumerate((re, im)):
            high = val.astype(BF16)
            fs[rows, 128 * k : 128 * k + 128] = high
            fs[rows, 256 + 128 * k : 384 + 128 * k] = (val - high.astype(F32)).astype(BF16)
    placed = dot(ohc[...], fs[...])
    covre[...] = placed[:, 0:128] + placed[:, 256:384]
    covim[...] = placed[:, 128:256] + placed[:, 384:512]

    low = iota((8, BLOCK), 0) < 4
    for c in range(PTSD):
        fbuf[c, 0:8, :] = scale * covre[8 * c : 8 * c + 8, :]
        fbuf[c, 8:16, :] = scale * covim[8 * c : 8 * c + 8, :]
    for t in range(PTSD // 2):
        re = scale * covre[256 + 8 * t : 264 + 8 * t, :]
        im = scale * covim[256 + 8 * t : 264 + 8 * t, :]
        fbuf[2 * t, 16:24, :] = jnp.where(low, re, pltpu.roll(im, 4, 0))
        fbuf[2 * t + 1, 16:24, :] = jnp.where(low, pltpu.roll(re, 4, 0), im)

    def scatter_copy(d, src, dst, ss, rs):
        to = (p + d) % PTSD
        return pltpu.make_async_remote_copy(
            src_ref=src.at[to], dst_ref=dst.at[d - 1], send_sem=ss, recv_sem=rs,
            device_id={"pts": to}, device_id_type=MESH,
        )

    def gather_copy(d, buf, ss, rs):
        return pltpu.make_async_remote_copy(
            src_ref=buf.at[p], dst_ref=buf.at[p], send_sem=ss, recv_sem=rs,
            device_id={"pts": (p + d) % PTSD}, device_id_type=MESH,
        )

    def start_scatter(src, dst, ss, rs):
        def step(d, carry):
            scatter_copy(d, src, dst, ss, rs).start()
            return carry

        lax.fori_loop(1, PTSD, step, 0)

    def start_gather(buf, ss, rs):
        def step(d, carry):
            gather_copy(d, buf, ss, rs).start()
            return carry

        lax.fori_loop(1, PTSD, step, 0)

    def wait_all(buf, sem):
        pltpu.make_async_copy(buf.at[pl.ds(0, PTSD - 1)], buf.at[pl.ds(0, PTSD - 1)], sem).wait()

    pl.semaphore_wait(plane_sem, 1)
    start_scatter(fbuf, frecv, rs_ss, rs_rs)
    for n in range(ROWS // 128):
        cols = slice(128 * n, 128 * n + 128)
        ohbt[:, cols] = jnp.transpose(ohb[cols, :].astype(F32)).astype(BF16)
    multb[...] = dot(ohc[...], multq[...].astype(BF16))
    wait_all(frecv, rs_rs)
    whole = fbuf[p]
    for d in range(PTSD - 1):
        whole = whole + frecv[d]
    agbuf[p] = whole
    start_gather(agbuf, ag_ss, ag_rs)
    wait_all(fbuf, rs_ss)
    wait_all(agbuf, ag_rs)

    for c in range(PTSD):
        covre[8 * c : 8 * c + 8, :] = agbuf[c, 0:8, :]
        covim[8 * c : 8 * c + 8, :] = agbuf[c, 8:16, :]
    for t in range(PTSD // 2):
        even = agbuf[2 * t, 16:24, :]
        odd = agbuf[2 * t + 1, 16:24, :]
        covre[256 + 8 * t : 264 + 8 * t, :] = jnp.where(low, even, pltpu.roll(odd, 4, 0))
        covim[256 + 8 * t : 264 + 8 * t, :] = jnp.where(low, pltpu.roll(even, 4, 0), odd)
    cre = covre[...]
    cim = covim[...]
    mrow = multb[...]
    neg = jnp.where(mrow > 0.0, -SHARPNESS * (cre * cre + cim * cim), NEG)
    peak = jnp.max(jnp.max(neg, axis=0, keepdims=True), axis=1, keepdims=True)
    expo = jnp.where(mrow > 0.0, jnp.exp(neg - peak), 0.0)
    part = jnp.sum(jnp.sum(mrow * expo, axis=0, keepdims=True), axis=1, keepdims=True)
    first = iota((8, BLOCK), 0) < 1
    stats[f] = jnp.where(first, jnp.broadcast_to(peak, (8, BLOCK)), jnp.broadcast_to(part, (8, BLOCK)))

    def feed_copies(buf, ss, rs):
        return [
            pltpu.make_async_remote_copy(
                src_ref=buf.at[f], dst_ref=buf.at[f], send_sem=ss.at[d - 1], recv_sem=rs.at[d - 1],
                device_id={"feed": (f + d) % FEED}, device_id_type=MESH,
            )
            for d in range(1, FEED)
        ]

    st_copies = feed_copies(stats, st_ss, st_rs)
    for c in st_copies:
        c.start()
    twice = 2.0 * expo
    sens[:, 0:128] = (twice * cre).astype(BF16)
    sens[:, 128:256] = (twice * cim).astype(BF16)
    times = jnp.concatenate([multq[...], multq[...]], axis=1)
    grid[...] = (times * dot(ohct[...], sens[...])).astype(BF16)

    yg[used:ROWS, :] = jnp.zeros((ROWS - used, 2 * PLOC), BF16)
    slope8 = jnp.zeros((8, PLOC), F32)
    for s in range(SLOTS):
        w = WIDTH[s]
        rows = slice(BASE[s], BASE[s] + w)
        sr = grid[rows, 0:128]
        si = grid[rows, 128:256]
        rate = rates[s : s + 1, :]
        rr = (rate * sr.astype(F32)).astype(BF16)
        ri = (rate * si.astype(F32)).astype(BF16)
        left_s = jnp.concatenate(
            [
                jnp.concatenate([sr, si], axis=1),
                jnp.concatenate([si, -sr], axis=1),
                jnp.concatenate([ri, -rr], axis=1),
                jnp.concatenate([-rr, -ri], axis=1),
            ],
            axis=0,
        )
        back = lax.dot_general(
            left_s, kall[:, 256 * s : 256 * s + 256], (((1,), (1,)), ((), ())), preferred_element_type=F32
        )
        yg[rows, 0:PLOC] = back[0:w, :].astype(BF16)
        yg[rows, PLOC:] = back[w : 2 * w, :].astype(BF16)
        turn = jlre[rows, :].astype(F32) * back[2 * w : 3 * w, :] + jlim[rows, :].astype(F32) * back[3 * w :, :]
        slope8 = slope8 + jnp.sum(turn.reshape(w // 8, 8, PLOC), axis=0)
    slope_row = jnp.sum(slope8, axis=0, keepdims=True)

    for c in st_copies:
        c.wait_recv()
    peaks = [stats[k, 0:1, 0:1] for k in range(FEED)]
    parts = [stats[k, 1:2, 0:1] for k in range(FEED)]
    top_peak = jnp.maximum(jnp.maximum(peaks[0], peaks[1]), jnp.maximum(peaks[2], peaks[3]))
    denom = sum(parts[k] * jnp.exp(peaks[k] - top_peak) for k in range(FEED))
    obj_ref[...] = -(top_peak + jnp.log(denom)) / SHARPNESS
    factor = scale * jnp.exp(peak - top_peak) / denom

    weighted = w16[...] * slope_row
    m = iota((32, 128), 0) * 128 + iota((32, 128), 1)
    grid_coef = jnp.zeros((32, 128), F32)
    for blk in range(PLOC // BLOCK):
        sums = jnp.sum(weighted[:, blk * BLOCK : (blk + 1) * BLOCK], axis=1, keepdims=True)
        i = m // NCV - row_ref[blk]
        j = m % NCV - col_ref[blk]
        key = jnp.where((i >= 0) & (i < 4) & (j >= 0) & (j < 4), 4 * i + j, -1)
        for k in range(16):
            grid_coef = grid_coef + jnp.where(key == k, sums[k : k + 1, :], 0.0)

    by_beam = dot(ohbt[...], yg[...]).astype(BF16)
    grad = jnp.concatenate([by_beam[:, 0:PLOC], by_beam[:, PLOC:]], axis=0)
    light = jnp.concatenate([il_all[k] for k in range(FEED)], axis=0)
    prod = lax.dot_general(light, grad, (((1,), (1,)), ((), ())), preferred_element_type=F32)
    pad_a[...] = jnp.full((8, BP), -1.0, F32)
    pad_a[0:1, 0:BEAMS] = bg_ref[...].astype(F32)
    grp = pad_a[0:1, :]
    ge_re = jnp.zeros((32, BP), F32)
    ge_im = jnp.zeros((32, BP), F32)
    for k in range(FEED):
        up = prod[128 * k : 128 * k + 64, :]
        dn = prod[128 * k + 64 : 128 * k + 128, :]
        re = up[:, 0:BP] + dn[:, BP:]
        im = up[:, BP:] - dn[:, 0:BP]
        for h in range(2):
            own = grp == float(2 * k + h)
            ge_re = ge_re + jnp.where(own, re[32 * h : 32 * h + 32, :], 0.0)
            ge_im = ge_im + jnp.where(own, im[32 * h : 32 * h + 32, :], 0.0)
    gbuf[...] = jnp.zeros((PTSD, 8, 128), F32)
    pieces = (ge_re[:, 0:128], ge_re[:, 128:], ge_im[:, 0:128], ge_im[:, 128:], grid_coef)
    for k, piece in enumerate(pieces):
        for c in range(PTSD):
            gbuf[c, k : k + 1, :] = factor * piece[c : c + 1, :]

    def plane_scatter(d):
        to = (flat + d) % PLANE
        return pltpu.make_async_remote_copy(
            src_ref=gbuf.at[pl.ds(2 * to, 2)], dst_ref=grecv.at[d - 1], send_sem=g_ss, recv_sem=g_rs,
            device_id={"pts": p - flat + to}, device_id_type=MESH,
        )

    def plane_gather(d):
        mine2 = gag.at[pl.ds(2 * flat, 2)]
        return pltpu.make_async_remote_copy(
            src_ref=mine2, dst_ref=mine2, send_sem=c_ss, recv_sem=c_rs,
            device_id={"pts": p - flat + (flat + d) % PLANE}, device_id_type=MESH,
        )

    def wait_plane(sem):
        pltpu.make_async_copy(grecv, grecv, sem).wait()

    for d in range(1, PLANE):
        plane_scatter(d).start()
    wait_plane(g_rs)
    tile = gbuf[pl.ds(2 * flat, 2)]
    for d in range(PLANE - 1):
        tile = tile + grecv[d]
    spot = 2 * f + far
    fb[spot] = tile
    fb_copies = [
        pltpu.make_async_remote_copy(
            src_ref=fb.at[spot], dst_ref=fb.at[spot], send_sem=b_ss.at[k], recv_sem=b_rs.at[k],
            device_id=to, device_id_type=MESH,
        )
        for k, to in enumerate(x_ring)
    ]
    for c in fb_copies:
        c.start()
    for c in fb_copies:
        c.wait_recv()
    total = fb[0]
    for k in range(1, RING):
        total = total + fb[k]
    gag[pl.ds(2 * flat, 2)] = total
    for d in range(1, PLANE):
        plane_gather(d).start()
    wait_plane(c_rs)

    for c in range(PTSD):
        gcoef_ref[c : c + 1, :] = gag[c, 4:5, :]
    half = [jnp.concatenate([gag[c, k : k + 1, :] for c in range(PTSD)], axis=0) for k in range(4)]
    for k in range(2):
        rows = jnp.concatenate([half[2 * k], half[2 * k + 1]], axis=1)
        pad_b[0:64, 0:128] = jnp.zeros((64, 128), F32)
        for b in range(2):
            lanes = slice(128 * b, 128 * b + 128)
            keep0 = grp[:, lanes] == (2 * f).astype(F32)
            keep1 = grp[:, lanes] == (2 * f + 1).astype(F32)
            pad_b[128 * b : 128 * b + 128, :] = jnp.zeros((128, 128), F32)
            pad_b[128 * b : 128 * b + GROUP_SIZE, :] = jnp.where(keep0, rows[0:GROUP_SIZE, lanes], 0.0)
            pad_b[128 * b + GROUP_SIZE : 128 * b + 2 * GROUP_SIZE, :] = jnp.where(
                keep1, rows[0:GROUP_SIZE, lanes], 0.0
            )
            out = jnp.transpose(pad_b[128 * b : 128 * b + 128, :])
            n = min(128, BEAMS - 128 * b)
            gexc_ref[k, 128 * b : 128 * b + n, :] = out[0:n, 0 : 2 * GROUP_SIZE]

    for c in il_copies + e_copies + st_copies + fb_copies:
        c.wait_send()
    wait_all(agbuf, ag_ss)
    wait_plane(g_ss)
    wait_plane(c_ss)


def local(
    illumination,
    excitation,
    beam_group,
    positions,
    params,
    span_rows,
    span_cols,
    surface_coef,
    directions,
    cover_blocks,
    cover_count,
):
    vmem = pl.BlockSpec(memory_space=pltpu.VMEM)
    smem = pl.BlockSpec(memory_space=pltpu.SMEM)
    dma = pltpu.SemaphoreType.DMA
    scratch = [
        pltpu.VMEM((FEED, 128, PLOC), BF16),
        pltpu.VMEM((FEED, EB, 128), BF16),
        pltpu.VMEM((NDB, BLOCK), F32),
        pltpu.VMEM((NDB, BLOCK), F32),
        pltpu.VMEM((PLOC, 128), F32),
        pltpu.VMEM((PLOC, 128), F32),
        pltpu.VMEM((PLOC, 128), F32),
        pltpu.VMEM((16, PLOC), F32),
        pltpu.VMEM((PLOC, SLOTS * 256), BF16),
        pltpu.VMEM((SLOTS, 128), F32),
        pltpu.VMEM((8, BP), F32),
        pltpu.VMEM((BP, 128), F32),
        pltpu.VMEM((NDB, BP), F32),
        pltpu.VMEM((NDB, BP), F32),
        pltpu.VMEM((NDB, 128), F32),
        pltpu.VMEM((ROWS, BP), BF16),
        pltpu.VMEM((BP, ROWS), BF16),
        pltpu.VMEM((CAP, ROWS), BF16),
        pltpu.VMEM((ROWS, CAP), BF16),
        pltpu.VMEM((ROWS, 128), F32),
        pltpu.VMEM((CAP, 128), F32),
        pltpu.VMEM((BP, PLOC), BF16),
        pltpu.VMEM((BP, PLOC), BF16),
        pltpu.VMEM((ROWS, PLOC), BF16),
        pltpu.VMEM((ROWS, PLOC), BF16),
        pltpu.VMEM((ROWS, 512), BF16),
        pltpu.VMEM((PTSD, CH, 128), F32),
        pltpu.VMEM((PTSD - 1, CH, 128), F32),
        pltpu.VMEM((PTSD, CH, 128), F32),
        pltpu.VMEM((CAP, 128), F32),
        pltpu.VMEM((CAP, 128), F32),
        pltpu.VMEM((CAP, 256), BF16),
        pltpu.VMEM((ROWS, 256), BF16),
        pltpu.VMEM((ROWS, 2 * PLOC), BF16),
        pltpu.VMEM((FEED, 8, 128), F32),
        pltpu.VMEM((PTSD, 8, 128), F32),
        pltpu.VMEM((PLANE - 1, 2, 8, 128), F32),
        pltpu.VMEM((RING, 2, 8, 128), F32),
        pltpu.VMEM((PTSD, 8, 128), F32),
        pltpu.SemaphoreType.REGULAR,
        pltpu.SemaphoreType.REGULAR,
        dma((3,)), dma((3,)), dma((3,)), dma((3,)),
        dma, dma, dma, dma,
        dma((3,)), dma((3,)),
        dma, dma,
        dma((RING - 1,)), dma((RING - 1,)),
        dma, dma,
    ]
    objective, grad_coef, grad_exc = pl.pallas_call(
        body,
        out_shape=(
            jax.ShapeDtypeStruct((1, 1), F32),
            jax.ShapeDtypeStruct((32, 128), F32),
            jax.ShapeDtypeStruct((2, BEAMS, 2 * GROUP_SIZE), F32),
        ),
        in_specs=[vmem, vmem, vmem, vmem, vmem, smem, smem, smem, vmem, vmem, vmem],
        out_specs=(vmem, vmem, vmem),
        scratch_shapes=scratch,
        compiler_params=pltpu.CompilerParams(
            collective_id=0, has_side_effects=True, vmem_limit_bytes=48 * 1024 * 1024
        ),
        name="coverage",
    )(
        illumination,
        excitation,
        beam_group.reshape(1, BEAMS),
        positions,
        params,
        span_rows,
        span_cols,
        surface_coef,
        directions,
        cover_blocks,
        cover_count.reshape(1, BEAMS),
    )
    return objective.reshape(()), grad_coef.reshape(NC), grad_exc


def solution(mesh):
    return jax.shard_map(
        local,
        mesh=mesh,
        in_specs=(
            P(None, "feed", "pts"),
            P(None, None, "feed"),
            P(),
            P(None, "pts"),
            P(None, "pts"),
            P("pts"),
            P("pts"),
            P(),
            P(),
            P(),
            P(),
        ),
        out_specs=(P(), P(), P(None, None, "feed")),
        check_vma=False,
    )
```

```python
import functools
import math

import jax
import jax.numpy as jnp
from jax import lax
from jax.experimental import pallas as pl
from jax.experimental.pallas import tpu as pltpu
from jax.sharding import PartitionSpec as P

MESH = pl.DeviceIdType.MESH
F32 = jnp.float32
BF16 = jnp.bfloat16

GROUP_SIZE = 25
BEAMS = 200
NDB = 64
BLOCK = 128
CBMAX = 8
NCV = 64
NC = 4096
SHARPNESS = 2.0
TWO_PI = 2.0 * math.pi

FEED = 4
PTSD = 32
PLOC = 512
BP = 256
EB = 208
SLOTS = NDB // FEED
CAP = 384
CH = 24
NEG = -1e30
PAIRS = 900
WIDTH = tuple(-(-min(BEAMS, PAIRS // (FEED * s + 1)) // 16) * 16 for s in range(SLOTS))
BASE = tuple(sum(WIDTH[:s]) for s in range(SLOTS))
ROWS = -(-sum(WIDTH) // 128) * 128
PLANE = 16
RING = 8

COS_C = (0.99999921, -19.73898036, 64.92865742, -85.27162153, 58.79049212, -21.07110563)
SIN_C = (6.28318492, -41.34158923, 81.59994333, -76.61447253, 41.34288235, -12.47124354)


def horner(coefs, z):
    acc = jnp.full(z.shape, coefs[-1], F32)
    for c in coefs[-2::-1]:
        acc = acc * z + c
    return acc


def iota(shape, dim):
    return lax.broadcasted_iota(jnp.int32, shape, dim)


def columns(row, n):
    return jnp.transpose(jnp.broadcast_to(row, (n, row.shape[1])))


def dot(a, b):
    return jnp.dot(a, b, preferred_element_type=F32)


def body(
    il_ref, ex_ref, bg_ref, pos_ref, par_ref, row_ref, col_ref, coef_ref, dir_ref, cb_ref, cnt_ref,
    obj_ref, gcoef_ref, gexc_ref,
    il_all, e_all, dirx, diry, xb, yb, hb, w16, kall, rates, pad_a,
    rt_s, mt_s, rank_s, ohb, ohbt, ohc, ohct, multq, multb, jre, jim, jlre, jlim, fs,
    fbuf, frecv, agbuf, covre, covim, sens, grid, yg, stats, gbuf, grecv, fb, gag, next_sem, row_sem, plane_sem,
    il_ss, il_rs, rs_ss, rs_rs, ag_ss, ag_rs, st_ss, st_rs, g_ss, g_rs, b_ss, b_rs, c_ss, c_rs,
):
    f = lax.axis_index("feed")
    p = lax.axis_index("pts")
    sib = f + 1 - 2 * (f % 2)
    par = (f + 2) % FEED
    par_sib = (sib + 2) % FEED

    barrier = pltpu.get_barrier_semaphore()
    far = p // PLANE
    flat = p % PLANE
    y = p % 4
    z = flat // 4
    y_ring = [{"pts": p - y + (y + d) % 4} for d in range(1, 4)]
    z_next = [{"pts": p - 4 * z + 4 * ((z + d) % 4)} for d in (1, 3)]
    across = {"pts": (p + PLANE) % PTSD}
    x_ring = [
        {"feed": (f + d // 2) % FEED, "pts": (p + PLANE * (d % 2)) % PTSD} for d in range(1, RING)
    ]
    greeted = [{"feed": par}, {"feed": sib}, *y_ring, *z_next, across]
    for to in greeted:
        pl.semaphore_signal(barrier, inc=1, device_id=to, device_id_type=MESH)

    r64 = iota((64, 50), 0)
    place = jnp.where(
        (iota((64, 50), 1) == GROUP_SIZE * (r64 // 32) + r64 % 32) & (r64 % 32 < GROUP_SIZE), 1.0, 0.0
    ).astype(BF16)
    il_all[f, 0:64, :] = dot(place, il_ref[:, 0, :]).astype(BF16)
    il_all[f, 64:128, :] = dot(place, il_ref[:, 1, :]).astype(BF16)

    pad_a[...] = jnp.full((8, BP), -1.0, F32)
    pad_a[0:1, 0:BEAMS] = bg_ref[...].astype(F32)
    grp_row = pad_a[0:1, :]
    l128 = iota((50, 128), 1)
    r50 = iota((50, 128), 0)
    lane_feed = GROUP_SIZE * ((l128 % 64) // 32) + l128 % 32
    fits = (r50 == lane_feed) & (l128 % 32 < GROUP_SIZE)
    q_re = jnp.where(fits & (l128 < 64), 1.0, 0.0).astype(BF16)
    q_im = jnp.where(fits & (l128 >= 64), 1.0, 0.0).astype(BF16)
    first_dims = (((0,), (0,)), ((), ()))
    ex = lax.dot_general(ex_ref[:, 0, :], q_re, first_dims, preferred_element_type=F32)
    ex = ex + lax.dot_general(ex_ref[:, 1, :], q_im, first_dims, preferred_element_type=F32)
    grp_cols = columns(grp_row, 128)[0:BEAMS, :]
    lane_grp = ((iota((BEAMS, 128), 1) % 64) // 32 + 2 * f).astype(F32)
    e_all[f, 0:BEAMS, :] = jnp.where(grp_cols == lane_grp, ex, 0.0).astype(BF16)
    e_all[f, BEAMS:EB, :] = jnp.zeros((EB - BEAMS, 128), BF16)

    pad_a[...] = jnp.full((8, BP), -1.0, F32)
    pad_a[:, 0:BEAMS] = cb_ref[...].astype(F32)
    cover = pad_a[...]
    pad_a[...] = jnp.zeros((8, BP), F32)
    pad_a[0:1, 0:BEAMS] = cnt_ref[...].astype(F32)
    count = pad_a[0:1, :]
    k_io = iota((NDB, BP), 0).astype(F32)
    mult = jnp.zeros((NDB, BP), F32)
    for c in range(CBMAX):
        mult = mult + jnp.where((cover[c : c + 1, :] == k_io) & (count > c), 1.0, 0.0)
    ind = jnp.where(mult > 0.0, 1.0, 0.0)
    n_col = jnp.sum(ind, axis=1, keepdims=True)
    n_b = jnp.broadcast_to(n_col, (NDB, 128))
    n_row = jnp.transpose(jnp.concatenate([n_b, jnp.full((NDB, 128), -1.0, F32)], 0))[0:1, :]
    lane = iota((NDB, 128), 1)
    sub = iota((NDB, 128), 0)
    ahead = (n_row > n_b) | ((n_row == n_b) & (lane < sub))
    rank = jnp.sum(jnp.where(ahead, 1.0, 0.0), axis=1, keepdims=True)
    rank_b = jnp.broadcast_to(rank, (NDB, 128))

    def deal(r):
        level = jnp.floor(r * 0.25)
        odd = level - 2.0 * jnp.floor(level * 0.5)
        place_in = r - 4.0 * level
        return level, jnp.where(odd > 0.5, 3.0 - place_in, place_in)

    fq = f.astype(F32)
    lev_b, bin_b = deal(rank_b)
    rank_row = jnp.transpose(jnp.concatenate([rank_b, jnp.full((NDB, 128), 400.0, F32)], 0))[0:1, :]
    lev_row, bin_row = deal(rank_row)
    before = (bin_row == fq) & (lev_row < lev_b) & (lane < NDB)
    off_col = jnp.sum(jnp.where(before, n_row, 0.0), axis=1, keepdims=True)
    upper = jnp.where(iota((BP, BP), 0) < iota((BP, BP), 1), 1.0, 0.0).astype(BF16)
    rt_s[...] = jnp.where(ind > 0.0, dot(ind.astype(BF16), upper), -1.0)
    mt_s[...] = mult
    rank_s[...] = rank_b
    off_b = jnp.broadcast_to(off_col, (NDB, 128))

    def target(s):
        return 4 * s + f + (s % 2) * (3 - 2 * f)

    def basis(t):
        m = 1.0 - t
        t2 = t * t
        t3 = t2 * t
        return [
            m * m * m / 6.0,
            (3.0 * t3 - 6.0 * t2 + 4.0) / 6.0,
            (-3.0 * t3 + 3.0 * t2 + 3.0 * t + 1.0) / 6.0,
            t3 / 6.0,
        ]

    bu = basis(par_ref[0:1, :])
    bv = basis(par_ref[1:2, :])
    for i in range(4):
        for j in range(4):
            w16[4 * i + j : 4 * i + j + 1, :] = bu[i] * bv[j]
    heights = []
    for blk in range(PLOC // BLOCK):
        base = row_ref[blk] * NCV + col_ref[blk]
        h = jnp.zeros((1, BLOCK), F32)
        for i in range(4):
            for j in range(4):
                k = 4 * i + j
                h = h + w16[k : k + 1, blk * BLOCK : (blk + 1) * BLOCK] * coef_ref[base + i * NCV + j]
        heights.append(h)
    hb[...] = columns(jnp.concatenate(heights, axis=1), 128)
    xb[...] = columns(pos_ref[0:1, :], 128)
    yb[...] = columns(pos_ref[1:2, :], 128)

    for k in range(NDB):
        dirx[k : k + 1, :] = dir_ref[0:1, k * BLOCK : (k + 1) * BLOCK]
        diry[k : k + 1, :] = dir_ref[1:2, k * BLOCK : (k + 1) * BLOCK]

    def phases(s, carry):
        is_s = rank_s[...] == target(s).astype(F32)
        ux = jnp.sum(jnp.where(is_s, dirx[...], 0.0), axis=0, keepdims=True)
        uy = jnp.sum(jnp.where(is_s, diry[...], 0.0), axis=0, keepdims=True)
        uz1 = 1.0 + jnp.sqrt(1.0 - ux * ux - uy * uy)
        rates[pl.ds(s, 1), :] = TWO_PI * uz1
        base = pl.multiple_of(s * 256, 256)
        for c in range(PLOC // 64):
            rows = pl.ds(64 * c, 64)
            t = xb[rows, :] * ux + yb[rows, :] * uy + hb[rows, :] * uz1
            r = t - jnp.round(t)
            z = r * r
            kall[rows, pl.ds(base, 128)] = horner(COS_C, z).astype(BF16)
            kall[rows, pl.ds(base + 128, 128)] = (r * horner(SIN_C, z)).astype(BF16)
        return carry

    early = 3 * SLOTS // 4
    lax.fori_loop(0, early, phases, 0)

    pl.semaphore_wait(barrier, len(greeted))
    for to in z_next:
        pl.semaphore_signal(next_sem, inc=1, device_id=to, device_id_type=MESH)

    def feed_copy(k, slot, to):
        part = e_all.at[slot] if k % 3 == 0 else il_all.at[slot, pl.ds(64 * (k % 3 - 1), 64)]
        return pltpu.make_async_remote_copy(
            src_ref=part, dst_ref=part, send_sem=il_ss.at[k], recv_sem=il_rs.at[k],
            device_id={"feed": to}, device_id_type=MESH,
        )

    to_par = [feed_copy(k, f, par) for k in range(3)]
    to_sib = [feed_copy(k + 3, f, sib) for k in range(3)]
    passed = [feed_copy(k + 6, par, sib) for k in range(3)]
    for c in to_par + to_sib:
        c.start()

    lax.fori_loop(early, SLOTS, phases, 0)

    used = BASE[-1] + WIDTH[-1]
    ohb[used:ROWS, :] = jnp.zeros((ROWS - used, BP), BF16)
    ohct[used:ROWS, :] = jnp.zeros((ROWS - used, CAP), BF16)
    multq[used:ROWS, :] = jnp.zeros((ROWS - used, 128), F32)
    for s in range(SLOTS):
        rows = slice(BASE[s], BASE[s] + WIDTH[s])
        is_s = rank_b == target(s).astype(F32)
        off = jnp.sum(jnp.where(is_s, off_b, 0.0), axis=0, keepdims=True)[:, 0:1]
        load = jnp.sum(jnp.where(is_s, n_b, 0.0), axis=0, keepdims=True)[:, 0:1]
        is_w = is_s[:, 0:1]
        order = jnp.sum(jnp.where(is_w, rt_s[...], 0.0), axis=0, keepdims=True)
        times = jnp.sum(jnp.where(is_w, mt_s[...], 0.0), axis=0, keepdims=True)
        hit = order == iota((WIDTH[s], BP), 0).astype(F32)
        ohb[rows, :] = jnp.where(hit, 1.0, 0.0).astype(BF16)
        multq[rows, :] = jnp.broadcast_to(
            jnp.sum(jnp.where(hit, times, 0.0), axis=1, keepdims=True), (WIDTH[s], 128)
        )
        w = iota((WIDTH[s], CAP), 0).astype(F32)
        r = iota((WIDTH[s], CAP), 1).astype(F32)
        ohct[rows, :] = jnp.where((r - w == off) & (w < load), 1.0, 0.0).astype(BF16)
    for n in range(ROWS // 128):
        cols = slice(128 * n, 128 * n + 128)
        ohc[:, cols] = jnp.transpose(ohct[cols, :].astype(F32)).astype(BF16)

    pl.semaphore_wait(next_sem, len(z_next))
    for to in z_next:
        pl.semaphore_signal(row_sem, inc=1, device_id=to, device_id_type=MESH)
    for c, onward in zip(to_par, passed):
        c.wait_recv()
        onward.start()
    pl.semaphore_wait(row_sem, len(z_next))
    pl.semaphore_signal(plane_sem, inc=1, device_id=across, device_id_type=MESH)
    for c in to_sib + passed:
        c.wait_recv()

    exc = jnp.concatenate([e_all[k] for k in range(FEED)], axis=1)
    left = [il_all[k] for k in range(FEED)]
    mix_re = jnp.concatenate([x for b in left for x in (b[0:64, :], -b[64:128, :])], axis=0)
    mix_im = jnp.concatenate([x for b in left for x in (b[64:128, :], b[0:64, :])], axis=0)
    jre[EB:BP, :] = jnp.zeros((BP - EB, PLOC), BF16)
    jim[EB:BP, :] = jnp.zeros((BP - EB, PLOC), BF16)
    jre[0:EB, :] = dot(exc, mix_re).astype(BF16)
    jim[0:EB, :] = dot(exc, mix_im).astype(BF16)
    jlre[...] = dot(ohb[...], jre[...]).astype(BF16)
    jlim[...] = dot(ohb[...], jim[...]).astype(BF16)
    scale = 1.0 / math.sqrt(PLOC * PTSD)

    fs[used:ROWS, :] = jnp.zeros((ROWS - used, 512), BF16)
    for s in range(SLOTS):
        w = WIDTH[s]
        rows = slice(BASE[s], BASE[s] + w)
        prod = dot(jnp.concatenate([jlre[rows, :], jlim[rows, :]], axis=0), kall[:, 256 * s : 256 * s + 256])
        re = prod[0:w, 0:128] - prod[w:, 128:]
        im = prod[0:w, 128:] + prod[w:, 0:128]
        for k, val in enumerate((re, im)):
            high = val.astype(BF16)
            fs[rows, 128 * k : 128 * k + 128] = high
            fs[rows, 256 + 128 * k : 384 + 128 * k] = (val - high.astype(F32)).astype(BF16)
    placed = dot(ohc[...], fs[...])
    covre[...] = placed[:, 0:128] + placed[:, 256:384]
    covim[...] = placed[:, 128:256] + placed[:, 384:512]

    low = iota((8, BLOCK), 0) < 4
    for c in range(PTSD):
        fbuf[c, 0:8, :] = scale * covre[8 * c : 8 * c + 8, :]
        fbuf[c, 8:16, :] = scale * covim[8 * c : 8 * c + 8, :]
    for t in range(PTSD // 2):
        re = scale * covre[256 + 8 * t : 264 + 8 * t, :]
        im = scale * covim[256 + 8 * t : 264 + 8 * t, :]
        fbuf[2 * t, 16:24, :] = jnp.where(low, re, pltpu.roll(im, 4, 0))
        fbuf[2 * t + 1, 16:24, :] = jnp.where(low, pltpu.roll(re, 4, 0), im)

    def scatter_copy(d, src, dst, ss, rs):
        to = (p + d) % PTSD
        return pltpu.make_async_remote_copy(
            src_ref=src.at[to], dst_ref=dst.at[d - 1], send_sem=ss, recv_sem=rs,
            device_id={"pts": to}, device_id_type=MESH,
        )

    def gather_copy(d, buf, ss, rs):
        return pltpu.make_async_remote_copy(
            src_ref=buf.at[p], dst_ref=buf.at[p], send_sem=ss, recv_sem=rs,
            device_id={"pts": (p + d) % PTSD}, device_id_type=MESH,
        )

    def start_scatter(src, dst, ss, rs):
        def step(d, carry):
            scatter_copy(d, src, dst, ss, rs).start()
            return carry

        lax.fori_loop(1, PTSD, step, 0)

    def start_gather(buf, ss, rs):
        def step(d, carry):
            gather_copy(d, buf, ss, rs).start()
            return carry

        lax.fori_loop(1, PTSD, step, 0)

    def wait_all(buf, sem):
        pltpu.make_async_copy(buf.at[pl.ds(0, PTSD - 1)], buf.at[pl.ds(0, PTSD - 1)], sem).wait()

    pl.semaphore_wait(plane_sem, 1)
    start_scatter(fbuf, frecv, rs_ss, rs_rs)
    for n in range(ROWS // 128):
        cols = slice(128 * n, 128 * n + 128)
        ohbt[:, cols] = jnp.transpose(ohb[cols, :].astype(F32)).astype(BF16)
    multb[...] = dot(ohc[...], multq[...].astype(BF16))
    wait_all(frecv, rs_rs)
    whole = fbuf[p]
    for d in range(PTSD - 1):
        whole = whole + frecv[d]
    agbuf[p] = whole
    start_gather(agbuf, ag_ss, ag_rs)
    wait_all(fbuf, rs_ss)
    wait_all(agbuf, ag_rs)

    for c in range(PTSD):
        covre[8 * c : 8 * c + 8, :] = agbuf[c, 0:8, :]
        covim[8 * c : 8 * c + 8, :] = agbuf[c, 8:16, :]
    for t in range(PTSD // 2):
        even = agbuf[2 * t, 16:24, :]
        odd = agbuf[2 * t + 1, 16:24, :]
        covre[256 + 8 * t : 264 + 8 * t, :] = jnp.where(low, even, pltpu.roll(odd, 4, 0))
        covim[256 + 8 * t : 264 + 8 * t, :] = jnp.where(low, pltpu.roll(even, 4, 0), odd)
    cre = covre[...]
    cim = covim[...]
    mrow = multb[...]
    neg = jnp.where(mrow > 0.0, -SHARPNESS * (cre * cre + cim * cim), NEG)
    peak = jnp.max(jnp.max(neg, axis=0, keepdims=True), axis=1, keepdims=True)
    expo = jnp.where(mrow > 0.0, jnp.exp(neg - peak), 0.0)
    part = jnp.sum(jnp.sum(mrow * expo, axis=0, keepdims=True), axis=1, keepdims=True)
    first = iota((8, BLOCK), 0) < 1
    stats[f] = jnp.where(first, jnp.broadcast_to(peak, (8, BLOCK)), jnp.broadcast_to(part, (8, BLOCK)))

    def feed_copies(buf, ss, rs):
        return [
            pltpu.make_async_remote_copy(
                src_ref=buf.at[f], dst_ref=buf.at[f], send_sem=ss.at[d - 1], recv_sem=rs.at[d - 1],
                device_id={"feed": (f + d) % FEED}, device_id_type=MESH,
            )
            for d in range(1, FEED)
        ]

    st_copies = feed_copies(stats, st_ss, st_rs)
    for c in st_copies:
        c.start()
    twice = 2.0 * expo
    sens[:, 0:128] = (twice * cre).astype(BF16)
    sens[:, 128:256] = (twice * cim).astype(BF16)
    times = jnp.concatenate([multq[...], multq[...]], axis=1)
    grid[...] = (times * dot(ohct[...], sens[...])).astype(BF16)

    yg[used:ROWS, :] = jnp.zeros((ROWS - used, 2 * PLOC), BF16)
    slope8 = jnp.zeros((8, PLOC), F32)
    for s in range(SLOTS):
        w = WIDTH[s]
        rows = slice(BASE[s], BASE[s] + w)
        sr = grid[rows, 0:128]
        si = grid[rows, 128:256]
        rate = rates[s : s + 1, :]
        rr = (rate * sr.astype(F32)).astype(BF16)
        ri = (rate * si.astype(F32)).astype(BF16)
        left_s = jnp.concatenate(
            [
                jnp.concatenate([sr, si], axis=1),
                jnp.concatenate([si, -sr], axis=1),
                jnp.concatenate([ri, -rr], axis=1),
                jnp.concatenate([-rr, -ri], axis=1),
            ],
            axis=0,
        )
        back = lax.dot_general(
            left_s, kall[:, 256 * s : 256 * s + 256], (((1,), (1,)), ((), ())), preferred_element_type=F32
        )
        yg[rows, 0:PLOC] = back[0:w, :].astype(BF16)
        yg[rows, PLOC:] = back[w : 2 * w, :].astype(BF16)
        turn = jlre[rows, :].astype(F32) * back[2 * w : 3 * w, :] + jlim[rows, :].astype(F32) * back[3 * w :, :]
        slope8 = slope8 + jnp.sum(turn.reshape(w // 8, 8, PLOC), axis=0)
    slope_row = jnp.sum(slope8, axis=0, keepdims=True)

    for c in st_copies:
        c.wait_recv()
    peaks = [stats[k, 0:1, 0:1] for k in range(FEED)]
    parts = [stats[k, 1:2, 0:1] for k in range(FEED)]
    top_peak = jnp.maximum(jnp.maximum(peaks[0], peaks[1]), jnp.maximum(peaks[2], peaks[3]))
    denom = sum(parts[k] * jnp.exp(peaks[k] - top_peak) for k in range(FEED))
    obj_ref[...] = -(top_peak + jnp.log(denom)) / SHARPNESS
    factor = scale * jnp.exp(peak - top_peak) / denom

    weighted = w16[...] * slope_row
    m = iota((32, 128), 0) * 128 + iota((32, 128), 1)
    grid_coef = jnp.zeros((32, 128), F32)
    for blk in range(PLOC // BLOCK):
        sums = jnp.sum(weighted[:, blk * BLOCK : (blk + 1) * BLOCK], axis=1, keepdims=True)
        i = m // NCV - row_ref[blk]
        j = m % NCV - col_ref[blk]
        key = jnp.where((i >= 0) & (i < 4) & (j >= 0) & (j < 4), 4 * i + j, -1)
        for k in range(16):
            grid_coef = grid_coef + jnp.where(key == k, sums[k : k + 1, :], 0.0)

    by_beam = dot(ohbt[...], yg[...]).astype(BF16)
    grad = jnp.concatenate([by_beam[:, 0:PLOC], by_beam[:, PLOC:]], axis=0)
    light = jnp.concatenate([il_all[k] for k in range(FEED)], axis=0)
    prod = lax.dot_general(light, grad, (((1,), (1,)), ((), ())), preferred_element_type=F32)
    pad_a[...] = jnp.full((8, BP), -1.0, F32)
    pad_a[0:1, 0:BEAMS] = bg_ref[...].astype(F32)
    grp = pad_a[0:1, :]
    ge_re = jnp.zeros((32, BP), F32)
    ge_im = jnp.zeros((32, BP), F32)
    for k in range(FEED):
        up = prod[128 * k : 128 * k + 64, :]
        dn = prod[128 * k + 64 : 128 * k + 128, :]
        re = up[:, 0:BP] + dn[:, BP:]
        im = up[:, BP:] - dn[:, 0:BP]
        for h in range(2):
            own = grp == float(2 * k + h)
            ge_re = ge_re + jnp.where(own, re[32 * h : 32 * h + 32, :], 0.0)
            ge_im = ge_im + jnp.where(own, im[32 * h : 32 * h + 32, :], 0.0)
    gbuf[...] = jnp.zeros((PTSD, 8, 128), F32)
    pieces = (ge_re[:, 0:128], ge_re[:, 128:], ge_im[:, 0:128], ge_im[:, 128:], grid_coef)
    for k, piece in enumerate(pieces):
        for c in range(PTSD):
            gbuf[c, k : k + 1, :] = factor * piece[c : c + 1, :]

    def plane_scatter(d):
        to = (flat + d) % PLANE
        return pltpu.make_async_remote_copy(
            src_ref=gbuf.at[pl.ds(2 * to, 2)], dst_ref=grecv.at[d - 1], send_sem=g_ss, recv_sem=g_rs,
            device_id={"pts": p - flat + to}, device_id_type=MESH,
        )

    def plane_gather(d):
        mine2 = gag.at[pl.ds(2 * flat, 2)]
        return pltpu.make_async_remote_copy(
            src_ref=mine2, dst_ref=mine2, send_sem=c_ss, recv_sem=c_rs,
            device_id={"pts": p - flat + (flat + d) % PLANE}, device_id_type=MESH,
        )

    def wait_plane(sem):
        pltpu.make_async_copy(grecv, grecv, sem).wait()

    for d in range(1, PLANE):
        plane_scatter(d).start()
    wait_plane(g_rs)
    tile = gbuf[pl.ds(2 * flat, 2)]
    for d in range(PLANE - 1):
        tile = tile + grecv[d]
    spot = 2 * f + far
    fb[spot] = tile
    fb_copies = [
        pltpu.make_async_remote_copy(
            src_ref=fb.at[spot], dst_ref=fb.at[spot], send_sem=b_ss.at[k], recv_sem=b_rs.at[k],
            device_id=to, device_id_type=MESH,
        )
        for k, to in enumerate(x_ring)
    ]
    for c in fb_copies:
        c.start()
    for c in fb_copies:
        c.wait_recv()
    total = fb[0]
    for k in range(1, RING):
        total = total + fb[k]
    gag[pl.ds(2 * flat, 2)] = total
    for d in range(1, PLANE):
        plane_gather(d).start()
    wait_plane(c_rs)

    for c in range(PTSD):
        gcoef_ref[c : c + 1, :] = gag[c, 4:5, :]
    half = [jnp.concatenate([gag[c, k : k + 1, :] for c in range(PTSD)], axis=0) for k in range(4)]
    for h in range(2):
        keep = grp == (2 * f + h).astype(F32)
        for k in range(2):
            rows = jnp.concatenate([half[2 * k], half[2 * k + 1]], axis=1)
            out = jnp.where(keep, rows, 0.0)
            gexc_ref[GROUP_SIZE * h : GROUP_SIZE * (h + 1), k, :] = out[0:GROUP_SIZE, 0:BEAMS]

    for c in to_par + to_sib + passed + st_copies + fb_copies:
        c.wait_send()
    wait_all(agbuf, ag_ss)
    wait_plane(g_ss)
    wait_plane(c_ss)


def local(
    illumination,
    excitation,
    beam_group,
    positions,
    params,
    span_rows,
    span_cols,
    surface_coef,
    directions,
    cover_blocks,
    cover_count,
):
    vmem = pl.BlockSpec(memory_space=pltpu.VMEM)
    smem = pl.BlockSpec(memory_space=pltpu.SMEM)
    dma = pltpu.SemaphoreType.DMA
    scratch = [
        pltpu.VMEM((FEED, 128, PLOC), BF16),
        pltpu.VMEM((FEED, EB, 128), BF16),
        pltpu.VMEM((NDB, BLOCK), F32),
        pltpu.VMEM((NDB, BLOCK), F32),
        pltpu.VMEM((PLOC, 128), F32),
        pltpu.VMEM((PLOC, 128), F32),
        pltpu.VMEM((PLOC, 128), F32),
        pltpu.VMEM((16, PLOC), F32),
        pltpu.VMEM((PLOC, SLOTS * 256), BF16),
        pltpu.VMEM((SLOTS, 128), F32),
        pltpu.VMEM((8, BP), F32),
        pltpu.VMEM((NDB, BP), F32),
        pltpu.VMEM((NDB, BP), F32),
        pltpu.VMEM((NDB, 128), F32),
        pltpu.VMEM((ROWS, BP), BF16),
        pltpu.VMEM((BP, ROWS), BF16),
        pltpu.VMEM((CAP, ROWS), BF16),
        pltpu.VMEM((ROWS, CAP), BF16),
        pltpu.VMEM((ROWS, 128), F32),
        pltpu.VMEM((CAP, 128), F32),
        pltpu.VMEM((BP, PLOC), BF16),
        pltpu.VMEM((BP, PLOC), BF16),
        pltpu.VMEM((ROWS, PLOC), BF16),
        pltpu.VMEM((ROWS, PLOC), BF16),
        pltpu.VMEM((ROWS, 512), BF16),
        pltpu.VMEM((PTSD, CH, 128), F32),
        pltpu.VMEM((PTSD - 1, CH, 128), F32),
        pltpu.VMEM((PTSD, CH, 128), F32),
        pltpu.VMEM((CAP, 128), F32),
        pltpu.VMEM((CAP, 128), F32),
        pltpu.VMEM((CAP, 256), BF16),
        pltpu.VMEM((ROWS, 256), BF16),
        pltpu.VMEM((ROWS, 2 * PLOC), BF16),
        pltpu.VMEM((FEED, 8, 128), F32),
        pltpu.VMEM((PTSD, 8, 128), F32),
        pltpu.VMEM((PLANE - 1, 2, 8, 128), F32),
        pltpu.VMEM((RING, 2, 8, 128), F32),
        pltpu.VMEM((PTSD, 8, 128), F32),
        pltpu.SemaphoreType.REGULAR,
        pltpu.SemaphoreType.REGULAR,
        pltpu.SemaphoreType.REGULAR,
        dma((9,)), dma((9,)),
        dma, dma, dma, dma,
        dma((3,)), dma((3,)),
        dma, dma,
        dma((RING - 1,)), dma((RING - 1,)),
        dma, dma,
    ]
    objective, grad_coef, grad_exc = pl.pallas_call(
        body,
        out_shape=(
            jax.ShapeDtypeStruct((1, 1), F32),
            jax.ShapeDtypeStruct((32, 128), F32),
            jax.ShapeDtypeStruct((2 * GROUP_SIZE, 2, BEAMS), F32),
        ),
        in_specs=[vmem, vmem, vmem, vmem, vmem, smem, smem, smem, vmem, vmem, vmem],
        out_specs=(vmem, vmem, vmem),
        scratch_shapes=scratch,
        compiler_params=pltpu.CompilerParams(
            collective_id=0, has_side_effects=True, vmem_limit_bytes=48 * 1024 * 1024
        ),
        name="coverage",
    )(
        jnp.transpose(illumination, (1, 0, 2)),
        jnp.transpose(excitation, (2, 0, 1)),
        beam_group.reshape(1, BEAMS),
        positions,
        params,
        span_rows,
        span_cols,
        surface_coef,
        directions,
        cover_blocks.T,
        cover_count.reshape(1, BEAMS),
    )
    return objective.reshape(()), grad_coef.reshape(NC), jnp.transpose(grad_exc, (1, 2, 0))


def solution(mesh):
    return jax.shard_map(
        local,
        mesh=mesh,
        in_specs=(
            P(None, "feed", "pts"),
            P(None, None, "feed"),
            P(),
            P(None, "pts"),
            P(None, "pts"),
            P("pts"),
            P("pts"),
            P(),
            P(),
            P(),
            P(),
        ),
        out_specs=(P(), P(), P(None, None, "feed")),
        check_vma=False,
    )
```

```python
import functools
import math

import jax
import jax.numpy as jnp
from jax import lax
from jax.experimental import pallas as pl
from jax.experimental.pallas import tpu as pltpu
from jax.sharding import PartitionSpec as P

MESH = pl.DeviceIdType.MESH
F32 = jnp.float32
BF16 = jnp.bfloat16

GROUP_SIZE = 25
BEAMS = 200
NDB = 64
BLOCK = 128
CBMAX = 8
NCV = 64
NC = 4096
SHARPNESS = 2.0
TWO_PI = 2.0 * math.pi

FEED = 4
PTSD = 32
PLOC = 512
BP = 256
EB = 208
SLOTS = NDB // FEED
CAP = 384
CH = 24
NEG = -1e30
PAIRS = 900
WIDTH = tuple(-(-min(BEAMS, PAIRS // (FEED * s + 1)) // 16) * 16 for s in range(SLOTS))
BASE = tuple(sum(WIDTH[:s]) for s in range(SLOTS))
ROWS = -(-sum(WIDTH) // 128) * 128
PLANE = 16
RING = 8

COS_C = (0.99999921, -19.73898036, 64.92865742, -85.27162153, 58.79049212, -21.07110563)
SIN_C = (6.28318492, -41.34158923, 81.59994333, -76.61447253, 41.34288235, -12.47124354)


def horner(coefs, z):
    acc = jnp.full(z.shape, coefs[-1], F32)
    for c in coefs[-2::-1]:
        acc = acc * z + c
    return acc


def iota(shape, dim):
    return lax.broadcasted_iota(jnp.int32, shape, dim)


def columns(row, n):
    return jnp.transpose(jnp.broadcast_to(row, (n, row.shape[1])))


def dot(a, b):
    return jnp.dot(a, b, preferred_element_type=F32)


def body(
    il_in, ex_in, bg_in, pos_in, par_in, row_in, col_in, coef_in, dir_in, cb_in, cnt_in,
    obj_ref, gcoef_ref, gexc_ref,
    il_ref, ex_ref, bg_ref, pos_ref, par_ref, row_ref, col_ref, coef_ref, dir_ref, cb_ref, cnt_ref, in_sem,
    il_all, e_all, dirx, diry, xb, yb, hb, w16, kall, rates, pad_a,
    rt_s, mt_s, rank_s, ohb, ohbt, ohc, ohct, multq, multb, jre, jim, jlre, jlim, fs,
    fbuf, frecv, agbuf, covre, covim, sens, grid, yg, stats, gbuf, grecv, fb, gag, next_sem, row_sem, plane_sem,
    il_ss, il_rs, rs_ss, rs_rs, ag_ss, ag_rs, st_ss, st_rs, g_ss, g_rs, b_ss, b_rs, c_ss, c_rs,
):
    f = lax.axis_index("feed")
    p = lax.axis_index("pts")
    sib = f + 1 - 2 * (f % 2)
    par = (f + 2) % FEED
    par_sib = (sib + 2) % FEED

    barrier = pltpu.get_barrier_semaphore()
    far = p // PLANE
    flat = p % PLANE
    y = p % 4
    z = flat // 4
    y_ring = [{"pts": p - y + (y + d) % 4} for d in range(1, 4)]
    z_next = [{"pts": p - 4 * z + 4 * ((z + d) % 4)} for d in (1, 3)]
    across = {"pts": (p + PLANE) % PTSD}
    x_ring = [
        {"feed": (f + d // 2) % FEED, "pts": (p + PLANE * (d % 2)) % PTSD} for d in range(1, RING)
    ]
    greeted = [{"feed": par}, {"feed": sib}, *y_ring, *z_next, across]
    for to in greeted:
        pl.semaphore_signal(barrier, inc=1, device_id=to, device_id_type=MESH)

    held = (il_ref, ex_ref, bg_ref, cb_ref, cnt_ref, dir_ref, pos_ref, par_ref, coef_ref, row_ref, col_ref)
    given = (il_in, ex_in, bg_in, cb_in, cnt_in, dir_in, pos_in, par_in, coef_in, row_in, col_in)
    loads = [pltpu.make_async_copy(a, b, in_sem.at[k]) for k, (a, b) in enumerate(zip(given, held))]
    for c in loads:
        c.start()
    for c in loads[:3]:
        c.wait()

    r64 = iota((64, 50), 0)
    place = jnp.where(
        (iota((64, 50), 1) == GROUP_SIZE * (r64 // 32) + r64 % 32) & (r64 % 32 < GROUP_SIZE), 1.0, 0.0
    ).astype(BF16)
    il_all[f, 0:64, :] = dot(place, il_ref[:, 0, :]).astype(BF16)
    il_all[f, 64:128, :] = dot(place, il_ref[:, 1, :]).astype(BF16)

    pad_a[...] = jnp.full((8, BP), -1.0, F32)
    pad_a[0:1, 0:BEAMS] = bg_ref[...].astype(F32)
    grp_row = pad_a[0:1, :]
    l128 = iota((50, 128), 1)
    r50 = iota((50, 128), 0)
    lane_feed = GROUP_SIZE * ((l128 % 64) // 32) + l128 % 32
    fits = (r50 == lane_feed) & (l128 % 32 < GROUP_SIZE)
    q_re = jnp.where(fits & (l128 < 64), 1.0, 0.0).astype(BF16)
    q_im = jnp.where(fits & (l128 >= 64), 1.0, 0.0).astype(BF16)
    first_dims = (((0,), (0,)), ((), ()))
    ex = lax.dot_general(ex_ref[:, 0, :], q_re, first_dims, preferred_element_type=F32)
    ex = ex + lax.dot_general(ex_ref[:, 1, :], q_im, first_dims, preferred_element_type=F32)
    grp_cols = columns(grp_row, 128)[0:BEAMS, :]
    lane_grp = ((iota((BEAMS, 128), 1) % 64) // 32 + 2 * f).astype(F32)
    e_all[f, 0:BEAMS, :] = jnp.where(grp_cols == lane_grp, ex, 0.0).astype(BF16)
    e_all[f, BEAMS:EB, :] = jnp.zeros((EB - BEAMS, 128), BF16)

    pl.semaphore_wait(barrier, len(greeted))
    for to in z_next:
        pl.semaphore_signal(next_sem, inc=1, device_id=to, device_id_type=MESH)

    def feed_copy(k, slot, to):
        part = e_all.at[slot] if k % 3 == 0 else il_all.at[slot, pl.ds(64 * (k % 3 - 1), 64)]
        return pltpu.make_async_remote_copy(
            src_ref=part, dst_ref=part, send_sem=il_ss.at[k], recv_sem=il_rs.at[k],
            device_id={"feed": to}, device_id_type=MESH,
        )

    to_par = [feed_copy(k, f, par) for k in range(3)]
    to_sib = [feed_copy(k + 3, f, sib) for k in range(3)]
    passed = [feed_copy(k + 6, par, sib) for k in range(3)]
    for c in to_par + to_sib:
        c.start()

    for c in loads[3:]:
        c.wait()

    pad_a[...] = jnp.full((8, BP), -1.0, F32)
    pad_a[:, 0:BEAMS] = cb_ref[...].astype(F32)
    cover = pad_a[...]
    pad_a[...] = jnp.zeros((8, BP), F32)
    pad_a[0:1, 0:BEAMS] = cnt_ref[...].astype(F32)
    count = pad_a[0:1, :]
    k_io = iota((NDB, BP), 0).astype(F32)
    mult = jnp.zeros((NDB, BP), F32)
    for c in range(CBMAX):
        mult = mult + jnp.where((cover[c : c + 1, :] == k_io) & (count > c), 1.0, 0.0)
    ind = jnp.where(mult > 0.0, 1.0, 0.0)
    n_col = jnp.sum(ind, axis=1, keepdims=True)
    n_b = jnp.broadcast_to(n_col, (NDB, 128))
    n_row = jnp.transpose(jnp.concatenate([n_b, jnp.full((NDB, 128), -1.0, F32)], 0))[0:1, :]
    lane = iota((NDB, 128), 1)
    sub = iota((NDB, 128), 0)
    ahead = (n_row > n_b) | ((n_row == n_b) & (lane < sub))
    rank = jnp.sum(jnp.where(ahead, 1.0, 0.0), axis=1, keepdims=True)
    rank_b = jnp.broadcast_to(rank, (NDB, 128))

    def deal(r):
        level = jnp.floor(r * 0.25)
        odd = level - 2.0 * jnp.floor(level * 0.5)
        place_in = r - 4.0 * level
        return level, jnp.where(odd > 0.5, 3.0 - place_in, place_in)

    fq = f.astype(F32)
    lev_b, bin_b = deal(rank_b)
    rank_row = jnp.transpose(jnp.concatenate([rank_b, jnp.full((NDB, 128), 400.0, F32)], 0))[0:1, :]
    lev_row, bin_row = deal(rank_row)
    before = (bin_row == fq) & (lev_row < lev_b) & (lane < NDB)
    off_col = jnp.sum(jnp.where(before, n_row, 0.0), axis=1, keepdims=True)
    upper = jnp.where(iota((BP, BP), 0) < iota((BP, BP), 1), 1.0, 0.0).astype(BF16)
    rt_s[...] = jnp.where(ind > 0.0, dot(ind.astype(BF16), upper), -1.0)
    mt_s[...] = mult
    rank_s[...] = rank_b
    off_b = jnp.broadcast_to(off_col, (NDB, 128))

    def target(s):
        return 4 * s + f + (s % 2) * (3 - 2 * f)

    def basis(t):
        m = 1.0 - t
        t2 = t * t
        t3 = t2 * t
        return [
            m * m * m / 6.0,
            (3.0 * t3 - 6.0 * t2 + 4.0) / 6.0,
            (-3.0 * t3 + 3.0 * t2 + 3.0 * t + 1.0) / 6.0,
            t3 / 6.0,
        ]

    bu = basis(par_ref[0:1, :])
    bv = basis(par_ref[1:2, :])
    for i in range(4):
        for j in range(4):
            w16[4 * i + j : 4 * i + j + 1, :] = bu[i] * bv[j]
    heights = []
    for blk in range(PLOC // BLOCK):
        base = row_ref[blk] * NCV + col_ref[blk]
        h = jnp.zeros((1, BLOCK), F32)
        for i in range(4):
            for j in range(4):
                k = 4 * i + j
                h = h + w16[k : k + 1, blk * BLOCK : (blk + 1) * BLOCK] * coef_ref[base + i * NCV + j]
        heights.append(h)
    hb[...] = columns(jnp.concatenate(heights, axis=1), 128)
    xb[...] = columns(pos_ref[0:1, :], 128)
    yb[...] = columns(pos_ref[1:2, :], 128)

    for k in range(NDB):
        dirx[k : k + 1, :] = dir_ref[0:1, k * BLOCK : (k + 1) * BLOCK]
        diry[k : k + 1, :] = dir_ref[1:2, k * BLOCK : (k + 1) * BLOCK]

    def phases(s, carry):
        is_s = rank_s[...] == target(s).astype(F32)
        ux = jnp.sum(jnp.where(is_s, dirx[...], 0.0), axis=0, keepdims=True)
        uy = jnp.sum(jnp.where(is_s, diry[...], 0.0), axis=0, keepdims=True)
        uz1 = 1.0 + jnp.sqrt(1.0 - ux * ux - uy * uy)
        rates[pl.ds(s, 1), :] = TWO_PI * uz1
        base = pl.multiple_of(s * 256, 256)
        for c in range(PLOC // 64):
            rows = pl.ds(64 * c, 64)
            t = xb[rows, :] * ux + yb[rows, :] * uy + hb[rows, :] * uz1
            r = t - jnp.round(t)
            z = r * r
            kall[rows, pl.ds(base, 128)] = horner(COS_C, z).astype(BF16)
            kall[rows, pl.ds(base + 128, 128)] = (r * horner(SIN_C, z)).astype(BF16)
        return carry

    lax.fori_loop(0, SLOTS, phases, 0)

    used = BASE[-1] + WIDTH[-1]
    ohb[used:ROWS, :] = jnp.zeros((ROWS - used, BP), BF16)
    ohct[used:ROWS, :] = jnp.zeros((ROWS - used, CAP), BF16)
    multq[used:ROWS, :] = jnp.zeros((ROWS - used, 128), F32)
    for s in range(SLOTS):
        rows = slice(BASE[s], BASE[s] + WIDTH[s])
        is_s = rank_b == target(s).astype(F32)
        off = jnp.sum(jnp.where(is_s, off_b, 0.0), axis=0, keepdims=True)[:, 0:1]
        load = jnp.sum(jnp.where(is_s, n_b, 0.0), axis=0, keepdims=True)[:, 0:1]
        is_w = is_s[:, 0:1]
        order = jnp.sum(jnp.where(is_w, rt_s[...], 0.0), axis=0, keepdims=True)
        times = jnp.sum(jnp.where(is_w, mt_s[...], 0.0), axis=0, keepdims=True)
        hit = order == iota((WIDTH[s], BP), 0).astype(F32)
        ohb[rows, :] = jnp.where(hit, 1.0, 0.0).astype(BF16)
        multq[rows, :] = jnp.broadcast_to(
            jnp.sum(jnp.where(hit, times, 0.0), axis=1, keepdims=True), (WIDTH[s], 128)
        )
        w = iota((WIDTH[s], CAP), 0).astype(F32)
        r = iota((WIDTH[s], CAP), 1).astype(F32)
        ohct[rows, :] = jnp.where((r - w == off) & (w < load), 1.0, 0.0).astype(BF16)
    for n in range(ROWS // 128):
        cols = slice(128 * n, 128 * n + 128)
        ohc[:, cols] = jnp.transpose(ohct[cols, :].astype(F32)).astype(BF16)

    pl.semaphore_wait(next_sem, len(z_next))
    for to in z_next:
        pl.semaphore_signal(row_sem, inc=1, device_id=to, device_id_type=MESH)
    for c, onward in zip(to_par, passed):
        c.wait_recv()
        onward.start()
    pl.semaphore_wait(row_sem, len(z_next))
    pl.semaphore_signal(plane_sem, inc=1, device_id=across, device_id_type=MESH)
    for c in to_sib + passed:
        c.wait_recv()

    exc = jnp.concatenate([e_all[k] for k in range(FEED)], axis=1)
    left = [il_all[k] for k in range(FEED)]
    mix_re = jnp.concatenate([x for b in left for x in (b[0:64, :], -b[64:128, :])], axis=0)
    mix_im = jnp.concatenate([x for b in left for x in (b[64:128, :], b[0:64, :])], axis=0)
    jre[EB:BP, :] = jnp.zeros((BP - EB, PLOC), BF16)
    jim[EB:BP, :] = jnp.zeros((BP - EB, PLOC), BF16)
    jre[0:EB, :] = dot(exc, mix_re).astype(BF16)
    jim[0:EB, :] = dot(exc, mix_im).astype(BF16)
    jlre[...] = dot(ohb[...], jre[...]).astype(BF16)
    jlim[...] = dot(ohb[...], jim[...]).astype(BF16)
    scale = 1.0 / math.sqrt(PLOC * PTSD)

    fs[used:ROWS, :] = jnp.zeros((ROWS - used, 512), BF16)
    for s in range(SLOTS):
        w = WIDTH[s]
        rows = slice(BASE[s], BASE[s] + w)
        prod = dot(jnp.concatenate([jlre[rows, :], jlim[rows, :]], axis=0), kall[:, 256 * s : 256 * s + 256])
        re = prod[0:w, 0:128] - prod[w:, 128:]
        im = prod[0:w, 128:] + prod[w:, 0:128]
        for k, val in enumerate((re, im)):
            high = val.astype(BF16)
            fs[rows, 128 * k : 128 * k + 128] = high
            fs[rows, 256 + 128 * k : 384 + 128 * k] = (val - high.astype(F32)).astype(BF16)
    placed = dot(ohc[...], fs[...])
    covre[...] = placed[:, 0:128] + placed[:, 256:384]
    covim[...] = placed[:, 128:256] + placed[:, 384:512]

    low = iota((8, BLOCK), 0) < 4
    for c in range(PTSD):
        fbuf[c, 0:8, :] = scale * covre[8 * c : 8 * c + 8, :]
        fbuf[c, 8:16, :] = scale * covim[8 * c : 8 * c + 8, :]
    for t in range(PTSD // 2):
        re = scale * covre[256 + 8 * t : 264 + 8 * t, :]
        im = scale * covim[256 + 8 * t : 264 + 8 * t, :]
        fbuf[2 * t, 16:24, :] = jnp.where(low, re, pltpu.roll(im, 4, 0))
        fbuf[2 * t + 1, 16:24, :] = jnp.where(low, pltpu.roll(re, 4, 0), im)

    def scatter_copy(d, src, dst, ss, rs):
        to = (p + d) % PTSD
        return pltpu.make_async_remote_copy(
            src_ref=src.at[to], dst_ref=dst.at[d - 1], send_sem=ss, recv_sem=rs,
            device_id={"pts": to}, device_id_type=MESH,
        )

    def gather_copy(d, buf, ss, rs):
        return pltpu.make_async_remote_copy(
            src_ref=buf.at[p], dst_ref=buf.at[p], send_sem=ss, recv_sem=rs,
            device_id={"pts": (p + d) % PTSD}, device_id_type=MESH,
        )

    def start_scatter(src, dst, ss, rs):
        def step(d, carry):
            scatter_copy(d, src, dst, ss, rs).start()
            return carry

        lax.fori_loop(1, PTSD, step, 0)

    def start_gather(buf, ss, rs):
        def step(d, carry):
            gather_copy(d, buf, ss, rs).start()
            return carry

        lax.fori_loop(1, PTSD, step, 0)

    def wait_all(buf, sem):
        pltpu.make_async_copy(buf.at[pl.ds(0, PTSD - 1)], buf.at[pl.ds(0, PTSD - 1)], sem).wait()

    pl.semaphore_wait(plane_sem, 1)
    start_scatter(fbuf, frecv, rs_ss, rs_rs)
    for n in range(ROWS // 128):
        cols = slice(128 * n, 128 * n + 128)
        ohbt[:, cols] = jnp.transpose(ohb[cols, :].astype(F32)).astype(BF16)
    multb[...] = dot(ohc[...], multq[...].astype(BF16))
    wait_all(frecv, rs_rs)
    whole = fbuf[p]
    for d in range(PTSD - 1):
        whole = whole + frecv[d]
    agbuf[p] = whole
    start_gather(agbuf, ag_ss, ag_rs)
    wait_all(fbuf, rs_ss)
    wait_all(agbuf, ag_rs)

    for c in range(PTSD):
        covre[8 * c : 8 * c + 8, :] = agbuf[c, 0:8, :]
        covim[8 * c : 8 * c + 8, :] = agbuf[c, 8:16, :]
    for t in range(PTSD // 2):
        even = agbuf[2 * t, 16:24, :]
        odd = agbuf[2 * t + 1, 16:24, :]
        covre[256 + 8 * t : 264 + 8 * t, :] = jnp.where(low, even, pltpu.roll(odd, 4, 0))
        covim[256 + 8 * t : 264 + 8 * t, :] = jnp.where(low, pltpu.roll(even, 4, 0), odd)
    cre = covre[...]
    cim = covim[...]
    mrow = multb[...]
    neg = jnp.where(mrow > 0.0, -SHARPNESS * (cre * cre + cim * cim), NEG)
    peak = jnp.max(jnp.max(neg, axis=0, keepdims=True), axis=1, keepdims=True)
    expo = jnp.where(mrow > 0.0, jnp.exp(neg - peak), 0.0)
    part = jnp.sum(jnp.sum(mrow * expo, axis=0, keepdims=True), axis=1, keepdims=True)
    first = iota((8, BLOCK), 0) < 1
    stats[f] = jnp.where(first, jnp.broadcast_to(peak, (8, BLOCK)), jnp.broadcast_to(part, (8, BLOCK)))

    def feed_copies(buf, ss, rs):
        return [
            pltpu.make_async_remote_copy(
                src_ref=buf.at[f], dst_ref=buf.at[f], send_sem=ss.at[d - 1], recv_sem=rs.at[d - 1],
                device_id={"feed": (f + d) % FEED}, device_id_type=MESH,
            )
            for d in range(1, FEED)
        ]

    st_copies = feed_copies(stats, st_ss, st_rs)
    for c in st_copies:
        c.start()
    twice = 2.0 * expo
    sens[:, 0:128] = (twice * cre).astype(BF16)
    sens[:, 128:256] = (twice * cim).astype(BF16)
    times = jnp.concatenate([multq[...], multq[...]], axis=1)
    grid[...] = (times * dot(ohct[...], sens[...])).astype(BF16)

    yg[used:ROWS, :] = jnp.zeros((ROWS - used, 2 * PLOC), BF16)
    slope8 = jnp.zeros((8, PLOC), F32)
    for s in range(SLOTS):
        w = WIDTH[s]
        rows = slice(BASE[s], BASE[s] + w)
        sr = grid[rows, 0:128]
        si = grid[rows, 128:256]
        rate = rates[s : s + 1, :]
        rr = (rate * sr.astype(F32)).astype(BF16)
        ri = (rate * si.astype(F32)).astype(BF16)
        left_s = jnp.concatenate(
            [
                jnp.concatenate([sr, si], axis=1),
                jnp.concatenate([si, -sr], axis=1),
                jnp.concatenate([ri, -rr], axis=1),
                jnp.concatenate([-rr, -ri], axis=1),
            ],
            axis=0,
        )
        back = lax.dot_general(
            left_s, kall[:, 256 * s : 256 * s + 256], (((1,), (1,)), ((), ())), preferred_element_type=F32
        )
        yg[rows, 0:PLOC] = back[0:w, :].astype(BF16)
        yg[rows, PLOC:] = back[w : 2 * w, :].astype(BF16)
        turn = jlre[rows, :].astype(F32) * back[2 * w : 3 * w, :] + jlim[rows, :].astype(F32) * back[3 * w :, :]
        slope8 = slope8 + jnp.sum(turn.reshape(w // 8, 8, PLOC), axis=0)
    slope_row = jnp.sum(slope8, axis=0, keepdims=True)

    for c in st_copies:
        c.wait_recv()
    peaks = [stats[k, 0:1, 0:1] for k in range(FEED)]
    parts = [stats[k, 1:2, 0:1] for k in range(FEED)]
    top_peak = jnp.maximum(jnp.maximum(peaks[0], peaks[1]), jnp.maximum(peaks[2], peaks[3]))
    denom = sum(parts[k] * jnp.exp(peaks[k] - top_peak) for k in range(FEED))
    obj_ref[...] = jnp.broadcast_to(-(top_peak + jnp.log(denom)) / SHARPNESS, (1, 128))
    factor = scale * jnp.exp(peak - top_peak) / denom

    weighted = w16[...] * slope_row
    m = iota((32, 128), 0) * 128 + iota((32, 128), 1)
    grid_coef = jnp.zeros((32, 128), F32)
    for blk in range(PLOC // BLOCK):
        sums = jnp.sum(weighted[:, blk * BLOCK : (blk + 1) * BLOCK], axis=1, keepdims=True)
        i = m // NCV - row_ref[blk]
        j = m % NCV - col_ref[blk]
        key = jnp.where((i >= 0) & (i < 4) & (j >= 0) & (j < 4), 4 * i + j, -1)
        for k in range(16):
            grid_coef = grid_coef + jnp.where(key == k, sums[k : k + 1, :], 0.0)

    by_beam = dot(ohbt[...], yg[...]).astype(BF16)
    grad = jnp.concatenate([by_beam[:, 0:PLOC], by_beam[:, PLOC:]], axis=0)
    light = jnp.concatenate([il_all[k] for k in range(FEED)], axis=0)
    prod = lax.dot_general(light, grad, (((1,), (1,)), ((), ())), preferred_element_type=F32)
    pad_a[...] = jnp.full((8, BP), -1.0, F32)
    pad_a[0:1, 0:BEAMS] = bg_ref[...].astype(F32)
    grp = pad_a[0:1, :]
    ge_re = jnp.zeros((32, BP), F32)
    ge_im = jnp.zeros((32, BP), F32)
    for k in range(FEED):
        up = prod[128 * k : 128 * k + 64, :]
        dn = prod[128 * k + 64 : 128 * k + 128, :]
        re = up[:, 0:BP] + dn[:, BP:]
        im = up[:, BP:] - dn[:, 0:BP]
        for h in range(2):
            own = grp == float(2 * k + h)
            ge_re = ge_re + jnp.where(own, re[32 * h : 32 * h + 32, :], 0.0)
            ge_im = ge_im + jnp.where(own, im[32 * h : 32 * h + 32, :], 0.0)
    gbuf[...] = jnp.zeros((PTSD, 8, 128), F32)
    pieces = (ge_re[:, 0:128], ge_re[:, 128:], ge_im[:, 0:128], ge_im[:, 128:], grid_coef)
    for k, piece in enumerate(pieces):
        for c in range(PTSD):
            gbuf[c, k : k + 1, :] = factor * piece[c : c + 1, :]

    def plane_scatter(d):
        to = (flat + d) % PLANE
        return pltpu.make_async_remote_copy(
            src_ref=gbuf.at[pl.ds(2 * to, 2)], dst_ref=grecv.at[d - 1], send_sem=g_ss, recv_sem=g_rs,
            device_id={"pts": p - flat + to}, device_id_type=MESH,
        )

    def plane_gather(d):
        mine2 = gag.at[pl.ds(2 * flat, 2)]
        return pltpu.make_async_remote_copy(
            src_ref=mine2, dst_ref=mine2, send_sem=c_ss, recv_sem=c_rs,
            device_id={"pts": p - flat + (flat + d) % PLANE}, device_id_type=MESH,
        )

    def wait_plane(sem):
        pltpu.make_async_copy(grecv, grecv, sem).wait()

    for d in range(1, PLANE):
        plane_scatter(d).start()
    wait_plane(g_rs)
    tile = gbuf[pl.ds(2 * flat, 2)]
    for d in range(PLANE - 1):
        tile = tile + grecv[d]
    spot = 2 * f + far
    fb[spot] = tile
    fb_copies = [
        pltpu.make_async_remote_copy(
            src_ref=fb.at[spot], dst_ref=fb.at[spot], send_sem=b_ss.at[k], recv_sem=b_rs.at[k],
            device_id=to, device_id_type=MESH,
        )
        for k, to in enumerate(x_ring)
    ]
    for c in fb_copies:
        c.start()
    for c in fb_copies:
        c.wait_recv()
    total = fb[0]
    for k in range(1, RING):
        total = total + fb[k]
    gag[pl.ds(2 * flat, 2)] = total
    for d in range(1, PLANE):
        plane_gather(d).start()
    wait_plane(c_rs)

    for c in range(PTSD):
        gcoef_ref[c : c + 1, :] = gag[c, 4:5, :]
    half = [jnp.concatenate([gag[c, k : k + 1, :] for c in range(PTSD)], axis=0) for k in range(4)]
    for h in range(2):
        keep = grp == (2 * f + h).astype(F32)
        for k in range(2):
            rows = jnp.concatenate([half[2 * k], half[2 * k + 1]], axis=1)
            out = jnp.where(keep, rows, 0.0)
            gexc_ref[GROUP_SIZE * h : GROUP_SIZE * (h + 1), k, :] = out[0:GROUP_SIZE, 0:BEAMS]

    for c in to_par + to_sib + passed + st_copies + fb_copies:
        c.wait_send()
    wait_all(agbuf, ag_ss)
    wait_plane(g_ss)
    wait_plane(c_ss)


def store(obj_ref, gcoef_ref, gexc_ref, obj_out, gcoef_out, gexc_out, sem):
    copies = [
        pltpu.make_async_copy(a, b, sem.at[k])
        for k, (a, b) in enumerate(((gexc_ref, gexc_out), (gcoef_ref, gcoef_out), (obj_ref, obj_out)))
    ]
    for c in copies:
        c.start()
    for c in copies:
        c.wait()


def local(
    illumination,
    excitation,
    beam_group,
    positions,
    params,
    span_rows,
    span_cols,
    surface_coef,
    directions,
    cover_blocks,
    cover_count,
):
    vmem = pl.BlockSpec(memory_space=pltpu.VMEM)
    hbm = pl.BlockSpec(memory_space=pltpu.HBM)
    dma = pltpu.SemaphoreType.DMA
    values = (
        jnp.transpose(illumination, (1, 0, 2)),
        jnp.transpose(excitation, (2, 0, 1)),
        beam_group.reshape(1, BEAMS),
        positions,
        params,
        span_rows,
        span_cols,
        surface_coef,
        directions,
        cover_blocks.T,
        cover_count.reshape(1, BEAMS),
    )
    scalar = (5, 6, 7)
    scratch = [
        *[(pltpu.SMEM if k in scalar else pltpu.VMEM)(v.shape, v.dtype) for k, v in enumerate(values)],
        dma((len(values),)),
        pltpu.VMEM((FEED, 128, PLOC), BF16),
        pltpu.VMEM((FEED, EB, 128), BF16),
        pltpu.VMEM((NDB, BLOCK), F32),
        pltpu.VMEM((NDB, BLOCK), F32),
        pltpu.VMEM((PLOC, 128), F32),
        pltpu.VMEM((PLOC, 128), F32),
        pltpu.VMEM((PLOC, 128), F32),
        pltpu.VMEM((16, PLOC), F32),
        pltpu.VMEM((PLOC, SLOTS * 256), BF16),
        pltpu.VMEM((SLOTS, 128), F32),
        pltpu.VMEM((8, BP), F32),
        pltpu.VMEM((NDB, BP), F32),
        pltpu.VMEM((NDB, BP), F32),
        pltpu.VMEM((NDB, 128), F32),
        pltpu.VMEM((ROWS, BP), BF16),
        pltpu.VMEM((BP, ROWS), BF16),
        pltpu.VMEM((CAP, ROWS), BF16),
        pltpu.VMEM((ROWS, CAP), BF16),
        pltpu.VMEM((ROWS, 128), F32),
        pltpu.VMEM((CAP, 128), F32),
        pltpu.VMEM((BP, PLOC), BF16),
        pltpu.VMEM((BP, PLOC), BF16),
        pltpu.VMEM((ROWS, PLOC), BF16),
        pltpu.VMEM((ROWS, PLOC), BF16),
        pltpu.VMEM((ROWS, 512), BF16),
        pltpu.VMEM((PTSD, CH, 128), F32),
        pltpu.VMEM((PTSD - 1, CH, 128), F32),
        pltpu.VMEM((PTSD, CH, 128), F32),
        pltpu.VMEM((CAP, 128), F32),
        pltpu.VMEM((CAP, 128), F32),
        pltpu.VMEM((CAP, 256), BF16),
        pltpu.VMEM((ROWS, 256), BF16),
        pltpu.VMEM((ROWS, 2 * PLOC), BF16),
        pltpu.VMEM((FEED, 8, 128), F32),
        pltpu.VMEM((PTSD, 8, 128), F32),
        pltpu.VMEM((PLANE - 1, 2, 8, 128), F32),
        pltpu.VMEM((RING, 2, 8, 128), F32),
        pltpu.VMEM((PTSD, 8, 128), F32),
        pltpu.SemaphoreType.REGULAR,
        pltpu.SemaphoreType.REGULAR,
        pltpu.SemaphoreType.REGULAR,
        dma((9,)), dma((9,)),
        dma, dma, dma, dma,
        dma((3,)), dma((3,)),
        dma, dma,
        dma((RING - 1,)), dma((RING - 1,)),
        dma, dma,
    ]
    shapes = (
        jax.ShapeDtypeStruct((1, 128), F32),
        jax.ShapeDtypeStruct((32, 128), F32),
        jax.ShapeDtypeStruct((2 * GROUP_SIZE, 2, BEAMS), F32),
    )
    results = pl.pallas_call(
        body,
        out_shape=shapes,
        in_specs=[hbm] * len(values),
        out_specs=(vmem, vmem, vmem),
        scratch_shapes=scratch,
        compiler_params=pltpu.CompilerParams(
            collective_id=0, has_side_effects=True, vmem_limit_bytes=60 * 1024 * 1024
        ),
        name="coverage",
    )(*values)
    objective, grad_coef, grad_exc = pl.pallas_call(
        store,
        out_shape=shapes,
        in_specs=[vmem] * 3,
        out_specs=(hbm, hbm, hbm),
        scratch_shapes=[dma((3,))],
        name="store",
    )(*results)
    return objective[0, 0], grad_coef.reshape(NC), jnp.transpose(grad_exc, (1, 2, 0))


def solution(mesh):
    return jax.shard_map(
        local,
        mesh=mesh,
        in_specs=(
            P(None, "feed", "pts"),
            P(None, None, "feed"),
            P(),
            P(None, "pts"),
            P(None, "pts"),
            P("pts"),
            P("pts"),
            P(),
            P(),
            P(),
            P(),
        ),
        out_specs=(P(), P(), P(None, None, "feed")),
        check_vma=False,
    )
```

```python
import functools
import math

import jax
import jax.numpy as jnp
from jax import lax
from jax.experimental import pallas as pl
from jax.experimental.pallas import tpu as pltpu
from jax.sharding import PartitionSpec as P

MESH = pl.DeviceIdType.MESH
F32 = jnp.float32
BF16 = jnp.bfloat16

GROUP_SIZE = 25
BEAMS = 200
NDB = 64
BLOCK = 128
CBMAX = 8
NCV = 64
NC = 4096
SHARPNESS = 2.0
TWO_PI = 2.0 * math.pi

FEED = 4
PTSD = 32
PLOC = 512
BP = 256
EB = 208
SLOTS = NDB // FEED
CAP = 384
CH = 24
NEG = -1e30
PAIRS = 900
WIDTH = tuple(-(-min(BEAMS, PAIRS // (FEED * s + 1)) // 16) * 16 for s in range(SLOTS))
BASE = tuple(sum(WIDTH[:s]) for s in range(SLOTS))
ROWS = -(-sum(WIDTH) // 128) * 128
PLANE = 16
RING = 8

COS_C = (0.99999921, -19.73898036, 64.92865742, -85.27162153, 58.79049212, -21.07110563)
SIN_C = (6.28318492, -41.34158923, 81.59994333, -76.61447253, 41.34288235, -12.47124354)


def horner(coefs, z):
    acc = jnp.full(z.shape, coefs[-1], F32)
    for c in coefs[-2::-1]:
        acc = acc * z + c
    return acc


def iota(shape, dim):
    return lax.broadcasted_iota(jnp.int32, shape, dim)


def columns(row, n):
    return jnp.transpose(jnp.broadcast_to(row, (n, row.shape[1])))


def dot(a, b):
    return jnp.dot(a, b, preferred_element_type=F32)


def body(
    il_in, ex_in, bg_in, pos_in, par_in, row_in, col_in, coef_in, dir_in, cb_in, cnt_in,
    obj_ref, gcoef_ref, gexc_ref,
    il_ref, ex_ref, bg_ref, pos_ref, par_ref, row_ref, col_ref, coef_ref, dir_ref, cb_ref, cnt_ref, in_sem,
    il_all, e_all, dirx, diry, xb, yb, hb, w16, kall, rates, pad_a,
    rt_s, mt_s, rank_s, ohb, ohbt, ohc, ohct, multq, multb, jre, jim, jlre, jlim, fs,
    fbuf, frecv, agbuf, covre, covim, sens, peak_s, part_s, grid, yg, stats, gbuf, grecv, fb, gag, next_sem, row_sem, plane_sem,
    il_ss, il_rs, rs_ss, rs_rs, ag_ss, ag_rs, st_ss, st_rs, g_ss, g_rs, b_ss, b_rs, c_ss, c_rs,
):
    f = lax.axis_index("feed")
    p = lax.axis_index("pts")
    sib = f + 1 - 2 * (f % 2)
    par = (f + 2) % FEED
    par_sib = (sib + 2) % FEED

    barrier = pltpu.get_barrier_semaphore()
    far = p // PLANE
    flat = p % PLANE
    y = p % 4
    z = flat // 4
    y_ring = [{"pts": p - y + (y + d) % 4} for d in range(1, 4)]
    z_next = [{"pts": p - 4 * z + 4 * ((z + d) % 4)} for d in (1, 3)]
    across = {"pts": (p + PLANE) % PTSD}
    x_ring = [
        {"feed": (f + d // 2) % FEED, "pts": (p + PLANE * (d % 2)) % PTSD} for d in range(1, RING)
    ]
    greeted = [{"feed": par}, {"feed": sib}, *y_ring, *z_next, across]
    for to in greeted:
        pl.semaphore_signal(barrier, inc=1, device_id=to, device_id_type=MESH)

    held = (il_ref, ex_ref, bg_ref, cb_ref, cnt_ref, dir_ref, pos_ref, par_ref, coef_ref, row_ref, col_ref)
    given = (il_in, ex_in, bg_in, cb_in, cnt_in, dir_in, pos_in, par_in, coef_in, row_in, col_in)
    loads = [pltpu.make_async_copy(a, b, in_sem.at[k]) for k, (a, b) in enumerate(zip(given, held))]
    for c in loads:
        c.start()
    for c in loads[:3]:
        c.wait()

    r64 = iota((64, 50), 0)
    place = jnp.where(
        (iota((64, 50), 1) == GROUP_SIZE * (r64 // 32) + r64 % 32) & (r64 % 32 < GROUP_SIZE), 1.0, 0.0
    ).astype(BF16)
    il_all[f, 0:64, :] = dot(place, il_ref[:, 0, :]).astype(BF16)
    il_all[f, 64:128, :] = dot(place, il_ref[:, 1, :]).astype(BF16)

    pad_a[...] = jnp.full((8, BP), -1.0, F32)
    pad_a[0:1, 0:BEAMS] = bg_ref[...].astype(F32)
    grp_row = pad_a[0:1, :]
    l128 = iota((50, 128), 1)
    r50 = iota((50, 128), 0)
    lane_feed = GROUP_SIZE * ((l128 % 64) // 32) + l128 % 32
    fits = (r50 == lane_feed) & (l128 % 32 < GROUP_SIZE)
    q_re = jnp.where(fits & (l128 < 64), 1.0, 0.0).astype(BF16)
    q_im = jnp.where(fits & (l128 >= 64), 1.0, 0.0).astype(BF16)
    first_dims = (((0,), (0,)), ((), ()))
    ex = lax.dot_general(ex_ref[:, 0, :], q_re, first_dims, preferred_element_type=F32)
    ex = ex + lax.dot_general(ex_ref[:, 1, :], q_im, first_dims, preferred_element_type=F32)
    grp_cols = columns(grp_row, 128)[0:BEAMS, :]
    lane_grp = ((iota((BEAMS, 128), 1) % 64) // 32 + 2 * f).astype(F32)
    e_all[f, 0:BEAMS, :] = jnp.where(grp_cols == lane_grp, ex, 0.0).astype(BF16)
    e_all[f, BEAMS:EB, :] = jnp.zeros((EB - BEAMS, 128), BF16)

    pl.semaphore_wait(barrier, len(greeted))
    for to in z_next:
        pl.semaphore_signal(next_sem, inc=1, device_id=to, device_id_type=MESH)

    def feed_copy(k, slot, to):
        part = e_all.at[slot] if k % 3 == 0 else il_all.at[slot, pl.ds(64 * (k % 3 - 1), 64)]
        return pltpu.make_async_remote_copy(
            src_ref=part, dst_ref=part, send_sem=il_ss.at[k], recv_sem=il_rs.at[k],
            device_id={"feed": to}, device_id_type=MESH,
        )

    to_par = [feed_copy(k, f, par) for k in range(3)]
    to_sib = [feed_copy(k + 3, f, sib) for k in range(3)]
    passed = [feed_copy(k + 6, par, sib) for k in range(3)]
    for c in to_par + to_sib:
        c.start()

    for c in loads[3:]:
        c.wait()

    pad_a[...] = jnp.full((8, BP), -1.0, F32)
    pad_a[:, 0:BEAMS] = cb_ref[...].astype(F32)
    cover = pad_a[...]
    pad_a[...] = jnp.zeros((8, BP), F32)
    pad_a[0:1, 0:BEAMS] = cnt_ref[...].astype(F32)
    count = pad_a[0:1, :]
    k_io = iota((NDB, BP), 0).astype(F32)
    mult = jnp.zeros((NDB, BP), F32)
    for c in range(CBMAX):
        mult = mult + jnp.where((cover[c : c + 1, :] == k_io) & (count > c), 1.0, 0.0)
    ind = jnp.where(mult > 0.0, 1.0, 0.0)
    n_col = jnp.sum(ind, axis=1, keepdims=True)
    n_b = jnp.broadcast_to(n_col, (NDB, 128))
    n_row = jnp.transpose(jnp.concatenate([n_b, jnp.full((NDB, 128), -1.0, F32)], 0))[0:1, :]
    lane = iota((NDB, 128), 1)
    sub = iota((NDB, 128), 0)
    ahead = (n_row > n_b) | ((n_row == n_b) & (lane < sub))
    rank = jnp.sum(jnp.where(ahead, 1.0, 0.0), axis=1, keepdims=True)
    rank_b = jnp.broadcast_to(rank, (NDB, 128))

    def deal(r):
        level = jnp.floor(r * 0.25)
        odd = level - 2.0 * jnp.floor(level * 0.5)
        place_in = r - 4.0 * level
        return level, jnp.where(odd > 0.5, 3.0 - place_in, place_in)

    fq = f.astype(F32)
    lev_b, bin_b = deal(rank_b)
    rank_row = jnp.transpose(jnp.concatenate([rank_b, jnp.full((NDB, 128), 400.0, F32)], 0))[0:1, :]
    lev_row, bin_row = deal(rank_row)
    before = (bin_row == fq) & (lev_row < lev_b) & (lane < NDB)
    off_col = jnp.sum(jnp.where(before, n_row, 0.0), axis=1, keepdims=True)
    upper = jnp.where(iota((BP, BP), 0) < iota((BP, BP), 1), 1.0, 0.0).astype(BF16)
    rt_s[...] = jnp.where(ind > 0.0, dot(ind.astype(BF16), upper), -1.0)
    mt_s[...] = mult
    rank_s[...] = rank_b
    off_b = jnp.broadcast_to(off_col, (NDB, 128))

    def target(s):
        return 4 * s + f + (s % 2) * (3 - 2 * f)

    def basis(t):
        m = 1.0 - t
        t2 = t * t
        t3 = t2 * t
        return [
            m * m * m / 6.0,
            (3.0 * t3 - 6.0 * t2 + 4.0) / 6.0,
            (-3.0 * t3 + 3.0 * t2 + 3.0 * t + 1.0) / 6.0,
            t3 / 6.0,
        ]

    bu = basis(par_ref[0:1, :])
    bv = basis(par_ref[1:2, :])
    for i in range(4):
        for j in range(4):
            w16[4 * i + j : 4 * i + j + 1, :] = bu[i] * bv[j]
    heights = []
    for blk in range(PLOC // BLOCK):
        base = row_ref[blk] * NCV + col_ref[blk]
        h = jnp.zeros((1, BLOCK), F32)
        for i in range(4):
            for j in range(4):
                k = 4 * i + j
                h = h + w16[k : k + 1, blk * BLOCK : (blk + 1) * BLOCK] * coef_ref[base + i * NCV + j]
        heights.append(h)
    hb[...] = columns(jnp.concatenate(heights, axis=1), 128)
    xb[...] = columns(pos_ref[0:1, :], 128)
    yb[...] = columns(pos_ref[1:2, :], 128)

    for k in range(NDB):
        dirx[k : k + 1, :] = dir_ref[0:1, k * BLOCK : (k + 1) * BLOCK]
        diry[k : k + 1, :] = dir_ref[1:2, k * BLOCK : (k + 1) * BLOCK]

    def phases(s, carry):
        is_s = rank_s[...] == target(s).astype(F32)
        ux = jnp.sum(jnp.where(is_s, dirx[...], 0.0), axis=0, keepdims=True)
        uy = jnp.sum(jnp.where(is_s, diry[...], 0.0), axis=0, keepdims=True)
        uz1 = 1.0 + jnp.sqrt(1.0 - ux * ux - uy * uy)
        rates[pl.ds(s, 1), :] = TWO_PI * uz1
        base = pl.multiple_of(s * 256, 256)
        for c in range(PLOC // 64):
            rows = pl.ds(64 * c, 64)
            t = xb[rows, :] * ux + yb[rows, :] * uy + hb[rows, :] * uz1
            r = t - jnp.round(t)
            z = r * r
            kall[rows, pl.ds(base, 128)] = horner(COS_C, z).astype(BF16)
            kall[rows, pl.ds(base + 128, 128)] = (r * horner(SIN_C, z)).astype(BF16)
        return carry

    lax.fori_loop(0, SLOTS, phases, 0)

    used = BASE[-1] + WIDTH[-1]
    ohb[used:ROWS, :] = jnp.zeros((ROWS - used, BP), BF16)
    ohct[used:ROWS, :] = jnp.zeros((ROWS - used, CAP), BF16)
    multq[used:ROWS, :] = jnp.zeros((ROWS - used, 128), F32)
    for s in range(SLOTS):
        rows = slice(BASE[s], BASE[s] + WIDTH[s])
        is_s = rank_b == target(s).astype(F32)
        off = jnp.sum(jnp.where(is_s, off_b, 0.0), axis=0, keepdims=True)[:, 0:1]
        load = jnp.sum(jnp.where(is_s, n_b, 0.0), axis=0, keepdims=True)[:, 0:1]
        is_w = is_s[:, 0:1]
        order = jnp.sum(jnp.where(is_w, rt_s[...], 0.0), axis=0, keepdims=True)
        times = jnp.sum(jnp.where(is_w, mt_s[...], 0.0), axis=0, keepdims=True)
        hit = order == iota((WIDTH[s], BP), 0).astype(F32)
        ohb[rows, :] = jnp.where(hit, 1.0, 0.0).astype(BF16)
        multq[rows, :] = jnp.broadcast_to(
            jnp.sum(jnp.where(hit, times, 0.0), axis=1, keepdims=True), (WIDTH[s], 128)
        )
        w = iota((WIDTH[s], CAP), 0).astype(F32)
        r = iota((WIDTH[s], CAP), 1).astype(F32)
        ohct[rows, :] = jnp.where((r - w == off) & (w < load), 1.0, 0.0).astype(BF16)
    for n in range(ROWS // 128):
        cols = slice(128 * n, 128 * n + 128)
        ohc[:, cols] = jnp.transpose(ohct[cols, :].astype(F32)).astype(BF16)

    pl.semaphore_wait(next_sem, len(z_next))
    for to in z_next:
        pl.semaphore_signal(row_sem, inc=1, device_id=to, device_id_type=MESH)
    for c, onward in zip(to_par, passed):
        c.wait_recv()
        onward.start()
    pl.semaphore_wait(row_sem, len(z_next))
    pl.semaphore_signal(plane_sem, inc=1, device_id=across, device_id_type=MESH)
    for c in to_sib + passed:
        c.wait_recv()

    exc = jnp.concatenate([e_all[k] for k in range(FEED)], axis=1)
    left = [il_all[k] for k in range(FEED)]
    mix_re = jnp.concatenate([x for b in left for x in (b[0:64, :], -b[64:128, :])], axis=0)
    mix_im = jnp.concatenate([x for b in left for x in (b[64:128, :], b[0:64, :])], axis=0)
    jre[EB:BP, :] = jnp.zeros((BP - EB, PLOC), BF16)
    jim[EB:BP, :] = jnp.zeros((BP - EB, PLOC), BF16)
    jre[0:EB, :] = dot(exc, mix_re).astype(BF16)
    jim[0:EB, :] = dot(exc, mix_im).astype(BF16)
    jlre[...] = dot(ohb[...], jre[...]).astype(BF16)
    jlim[...] = dot(ohb[...], jim[...]).astype(BF16)
    scale = 1.0 / math.sqrt(PLOC * PTSD)

    fs[used:ROWS, :] = jnp.zeros((ROWS - used, 512), BF16)
    for s in range(SLOTS):
        w = WIDTH[s]
        rows = slice(BASE[s], BASE[s] + w)
        prod = dot(jnp.concatenate([jlre[rows, :], jlim[rows, :]], axis=0), kall[:, 256 * s : 256 * s + 256])
        re = prod[0:w, 0:128] - prod[w:, 128:]
        im = prod[0:w, 128:] + prod[w:, 0:128]
        for k, val in enumerate((re, im)):
            high = val.astype(BF16)
            fs[rows, 128 * k : 128 * k + 128] = high
            fs[rows, 256 + 128 * k : 384 + 128 * k] = (val - high.astype(F32)).astype(BF16)
    placed = dot(ohc[...], fs[...])
    covre[...] = placed[:, 0:128] + placed[:, 256:384]
    covim[...] = placed[:, 128:256] + placed[:, 384:512]

    low = iota((8, BLOCK), 0) < 4
    for c in range(PTSD):
        fbuf[c, 0:8, :] = scale * covre[8 * c : 8 * c + 8, :]
        fbuf[c, 8:16, :] = scale * covim[8 * c : 8 * c + 8, :]
    for t in range(PTSD // 2):
        re = scale * covre[256 + 8 * t : 264 + 8 * t, :]
        im = scale * covim[256 + 8 * t : 264 + 8 * t, :]
        fbuf[2 * t, 16:24, :] = jnp.where(low, re, pltpu.roll(im, 4, 0))
        fbuf[2 * t + 1, 16:24, :] = jnp.where(low, pltpu.roll(re, 4, 0), im)

    def hops(o):
        return o[0] + min(o[1], 4 - o[1]) + min(o[2], 4 - o[2])

    offsets = [(dx, dz, dy) for dx in range(2) for dz in range(4) for dy in range(4)][1:]
    offsets.sort(key=hops, reverse=True)
    near = [o for o in offsets if o[0] == 0]

    def at_offset(o):
        return PLANE * ((far + o[0]) % 2) + 4 * ((z + o[1]) % 4) + (y + o[2]) % 4

    def start_scatter(src, dst, ss, rs):
        for k, o in enumerate(offsets):
            to = at_offset(o)
            pltpu.make_async_remote_copy(
                src_ref=src.at[to], dst_ref=dst.at[k], send_sem=ss, recv_sem=rs,
                device_id={"pts": to}, device_id_type=MESH,
            ).start()

    def start_gather(buf, ss, rs):
        for o in offsets:
            pltpu.make_async_remote_copy(
                src_ref=buf.at[p], dst_ref=buf.at[p], send_sem=ss, recv_sem=rs,
                device_id={"pts": at_offset(o)}, device_id_type=MESH,
            ).start()

    def wait_all(buf, sem):
        pltpu.make_async_copy(buf.at[pl.ds(0, PTSD - 1)], buf.at[pl.ds(0, PTSD - 1)], sem).wait()

    pl.semaphore_wait(plane_sem, 1)
    start_scatter(fbuf, frecv, rs_ss, rs_rs)
    for n in range(ROWS // 128):
        cols = slice(128 * n, 128 * n + 128)
        ohbt[:, cols] = jnp.transpose(ohb[cols, :].astype(F32)).astype(BF16)
    multb[...] = dot(ohc[...], multq[...].astype(BF16))
    wait_all(frecv, rs_rs)
    whole = fbuf[p]
    for d in range(PTSD - 1):
        whole = whole + frecv[d]

    def total_of(x, op):
        return op(op(x, axis=0, keepdims=True), axis=1, keepdims=True)

    def thirds(x):
        high = x.astype(BF16).astype(F32)
        mid = (x - high).astype(BF16).astype(F32)
        return [high, mid, x - high - mid]

    re_a, im_a, both_b = whole[0:8], whole[8:16], whole[16:24]
    times_a = multb[pl.ds(pl.multiple_of(8 * p, 8), 8), :]
    times_b = multb[pl.ds(pl.multiple_of(256 + 8 * (p // 2), 8), 8), :]
    turned = pltpu.roll(times_b, 4, 0)
    times_b = jnp.where(low == (p % 2 == 0), times_b, turned)
    square = both_b * both_b
    neg_a = jnp.where(times_a > 0.0, -SHARPNESS * (re_a * re_a + im_a * im_a), NEG)
    neg_b = jnp.where(times_b > 0.0, -SHARPNESS * (square + pltpu.roll(square, 4, 0)), NEG)
    own_peak = total_of(jnp.maximum(neg_a, neg_b), jnp.max)
    expo_a = jnp.where(times_a > 0.0, jnp.exp(neg_a - own_peak), 0.0)
    expo_b = jnp.where(times_b > 0.0, jnp.exp(neg_b - own_peak), 0.0)
    own_part = total_of(times_a * expo_a + jnp.where(low, times_b * expo_b, 0.0), jnp.sum)
    notes = jnp.zeros((8, BLOCK), F32)
    for k, val in enumerate(thirds(own_peak) + thirds(own_part)):
        notes = jnp.where(iota((8, BLOCK), 0) == k, val, notes)
    agbuf[p] = jnp.concatenate(
        [2.0 * expo_a * re_a, 2.0 * expo_a * im_a, 2.0 * expo_b * both_b, notes], axis=0
    ).astype(BF16)
    start_gather(agbuf, ag_ss, ag_rs)
    wait_all(fbuf, rs_ss)
    wait_all(agbuf, ag_rs)

    for c in range(PTSD):
        notes = agbuf[c, 16:32, :].astype(F32)[8:16]
        peak_s[c : c + 1, :] = (notes[0:1] + notes[1:2]) + notes[2:3]
        part_s[c : c + 1, :] = (notes[3:4] + notes[4:5]) + notes[5:6]
    peak = jnp.max(peak_s[...], axis=0, keepdims=True)
    gauge = jnp.exp(peak_s[...] - peak)
    part = jnp.sum(part_s[...] * gauge, axis=0, keepdims=True)
    peak_s[...] = gauge
    first = iota((8, BLOCK), 0) < 1
    stats[f] = jnp.where(first, jnp.broadcast_to(peak, (8, BLOCK)), jnp.broadcast_to(part, (8, BLOCK)))

    def feed_copies(buf, ss, rs):
        return [
            pltpu.make_async_remote_copy(
                src_ref=buf.at[f], dst_ref=buf.at[f], send_sem=ss.at[d - 1], recv_sem=rs.at[d - 1],
                device_id={"feed": (f + d) % FEED}, device_id_type=MESH,
            )
            for d in range(1, FEED)
        ]

    st_copies = feed_copies(stats, st_ss, st_rs)
    for c in st_copies:
        c.start()
    for c in range(PTSD):
        rows = agbuf[c, 0:16, :].astype(F32) * peak_s[c : c + 1, :]
        sens[8 * c : 8 * c + 8, 0:128] = rows[0:8]
        sens[8 * c : 8 * c + 8, 128:256] = rows[8:16]
    for t in range(PTSD // 2):
        even = agbuf[2 * t, 16:32, :].astype(F32)[0:8] * peak_s[2 * t : 2 * t + 1, :]
        odd = agbuf[2 * t + 1, 16:32, :].astype(F32)[0:8] * peak_s[2 * t + 1 : 2 * t + 2, :]
        sens[256 + 8 * t : 264 + 8 * t, 0:128] = jnp.where(low, even, pltpu.roll(odd, 4, 0))
        sens[256 + 8 * t : 264 + 8 * t, 128:256] = jnp.where(low, pltpu.roll(even, 4, 0), odd)
    times = jnp.concatenate([multq[...], multq[...]], axis=1)
    grid[...] = (times * dot(ohct[...], sens[...].astype(BF16))).astype(BF16)

    yg[used:ROWS, :] = jnp.zeros((ROWS - used, 2 * PLOC), BF16)
    slope8 = jnp.zeros((8, PLOC), F32)
    for s in range(SLOTS):
        w = WIDTH[s]
        rows = slice(BASE[s], BASE[s] + w)
        sr = grid[rows, 0:128]
        si = grid[rows, 128:256]
        rate = rates[s : s + 1, :]
        rr = (rate * sr.astype(F32)).astype(BF16)
        ri = (rate * si.astype(F32)).astype(BF16)
        left_s = jnp.concatenate(
            [
                jnp.concatenate([sr, si], axis=1),
                jnp.concatenate([si, -sr], axis=1),
                jnp.concatenate([ri, -rr], axis=1),
                jnp.concatenate([-rr, -ri], axis=1),
            ],
            axis=0,
        )
        back = lax.dot_general(
            left_s, kall[:, 256 * s : 256 * s + 256], (((1,), (1,)), ((), ())), preferred_element_type=F32
        )
        yg[rows, 0:PLOC] = back[0:w, :].astype(BF16)
        yg[rows, PLOC:] = back[w : 2 * w, :].astype(BF16)
        turn = jlre[rows, :].astype(F32) * back[2 * w : 3 * w, :] + jlim[rows, :].astype(F32) * back[3 * w :, :]
        slope8 = slope8 + jnp.sum(turn.reshape(w // 8, 8, PLOC), axis=0)
    slope_row = jnp.sum(slope8, axis=0, keepdims=True)

    for c in st_copies:
        c.wait_recv()
    peaks = [stats[k, 0:1, 0:1] for k in range(FEED)]
    parts = [stats[k, 1:2, 0:1] for k in range(FEED)]
    top_peak = jnp.maximum(jnp.maximum(peaks[0], peaks[1]), jnp.maximum(peaks[2], peaks[3]))
    denom = sum(parts[k] * jnp.exp(peaks[k] - top_peak) for k in range(FEED))
    obj_ref[...] = jnp.broadcast_to(-(top_peak + jnp.log(denom)) / SHARPNESS, (1, 128))
    factor = scale * jnp.exp(peak[:, 0:1] - top_peak) / denom

    weighted = w16[...] * slope_row
    m = iota((32, 128), 0) * 128 + iota((32, 128), 1)
    grid_coef = jnp.zeros((32, 128), F32)
    for blk in range(PLOC // BLOCK):
        sums = jnp.sum(weighted[:, blk * BLOCK : (blk + 1) * BLOCK], axis=1, keepdims=True)
        i = m // NCV - row_ref[blk]
        j = m % NCV - col_ref[blk]
        key = jnp.where((i >= 0) & (i < 4) & (j >= 0) & (j < 4), 4 * i + j, -1)
        for k in range(16):
            grid_coef = grid_coef + jnp.where(key == k, sums[k : k + 1, :], 0.0)

    by_beam = dot(ohbt[...], yg[...]).astype(BF16)
    grad = jnp.concatenate([by_beam[:, 0:PLOC], by_beam[:, PLOC:]], axis=0)
    light = jnp.concatenate([il_all[k] for k in range(FEED)], axis=0)
    prod = lax.dot_general(light, grad, (((1,), (1,)), ((), ())), preferred_element_type=F32)
    pad_a[...] = jnp.full((8, BP), -1.0, F32)
    pad_a[0:1, 0:BEAMS] = bg_ref[...].astype(F32)
    grp = pad_a[0:1, :]
    ge_re = jnp.zeros((32, BP), F32)
    ge_im = jnp.zeros((32, BP), F32)
    for k in range(FEED):
        up = prod[128 * k : 128 * k + 64, :]
        dn = prod[128 * k + 64 : 128 * k + 128, :]
        re = up[:, 0:BP] + dn[:, BP:]
        im = up[:, BP:] - dn[:, 0:BP]
        for h in range(2):
            own = grp == float(2 * k + h)
            ge_re = ge_re + jnp.where(own, re[32 * h : 32 * h + 32, :], 0.0)
            ge_im = ge_im + jnp.where(own, im[32 * h : 32 * h + 32, :], 0.0)
    gbuf[...] = jnp.zeros((PTSD, 8, 128), F32)
    pieces = (ge_re[:, 0:128], ge_re[:, 128:], ge_im[:, 0:128], ge_im[:, 128:], grid_coef)
    for k, piece in enumerate(pieces):
        for c in range(PTSD):
            gbuf[c, k : k + 1, :] = factor * piece[c : c + 1, :]

    def wait_plane(sem):
        pltpu.make_async_copy(grecv, grecv, sem).wait()

    for k, o in enumerate(near):
        to = at_offset(o)
        pltpu.make_async_remote_copy(
            src_ref=gbuf.at[pl.ds(2 * (to % PLANE), 2)], dst_ref=grecv.at[k], send_sem=g_ss, recv_sem=g_rs,
            device_id={"pts": to}, device_id_type=MESH,
        ).start()
    wait_plane(g_rs)
    tile = gbuf[pl.ds(2 * flat, 2)]
    for d in range(PLANE - 1):
        tile = tile + grecv[d]
    spot = 2 * f + far
    fb[spot] = tile
    fb_copies = [
        pltpu.make_async_remote_copy(
            src_ref=fb.at[spot], dst_ref=fb.at[spot], send_sem=b_ss.at[k], recv_sem=b_rs.at[k],
            device_id=to, device_id_type=MESH,
        )
        for k, to in enumerate(x_ring)
    ]
    for c in fb_copies:
        c.start()
    for c in fb_copies:
        c.wait_recv()
    total = fb[0]
    for k in range(1, RING):
        total = total + fb[k]
    gag[pl.ds(2 * flat, 2)] = total
    mine2 = gag.at[pl.ds(2 * flat, 2)]
    for o in near:
        pltpu.make_async_remote_copy(
            src_ref=mine2, dst_ref=mine2, send_sem=c_ss, recv_sem=c_rs,
            device_id={"pts": at_offset(o)}, device_id_type=MESH,
        ).start()
    wait_plane(c_rs)

    for c in range(PTSD):
        gcoef_ref[c : c + 1, :] = gag[c, 4:5, :]
    half = [jnp.concatenate([gag[c, k : k + 1, :] for c in range(PTSD)], axis=0) for k in range(4)]
    for h in range(2):
        keep = grp == (2 * f + h).astype(F32)
        for k in range(2):
            rows = jnp.concatenate([half[2 * k], half[2 * k + 1]], axis=1)
            out = jnp.where(keep, rows, 0.0)
            gexc_ref[GROUP_SIZE * h : GROUP_SIZE * (h + 1), k, :] = out[0:GROUP_SIZE, 0:BEAMS]

    for c in to_par + to_sib + passed + st_copies + fb_copies:
        c.wait_send()
    wait_all(agbuf, ag_ss)
    wait_plane(g_ss)
    wait_plane(c_ss)


def store(obj_ref, gcoef_ref, gexc_ref, obj_out, gcoef_out, gexc_out, sem):
    copies = [
        pltpu.make_async_copy(a, b, sem.at[k])
        for k, (a, b) in enumerate(((gexc_ref, gexc_out), (gcoef_ref, gcoef_out), (obj_ref, obj_out)))
    ]
    for c in copies:
        c.start()
    for c in copies:
        c.wait()


def local(
    illumination,
    excitation,
    beam_group,
    positions,
    params,
    span_rows,
    span_cols,
    surface_coef,
    directions,
    cover_blocks,
    cover_count,
):
    vmem = pl.BlockSpec(memory_space=pltpu.VMEM)
    hbm = pl.BlockSpec(memory_space=pltpu.HBM)
    dma = pltpu.SemaphoreType.DMA
    values = (
        jnp.transpose(illumination, (1, 0, 2)),
        jnp.transpose(excitation, (2, 0, 1)),
        beam_group.reshape(1, BEAMS),
        positions,
        params,
        span_rows,
        span_cols,
        surface_coef,
        directions,
        cover_blocks.T,
        cover_count.reshape(1, BEAMS),
    )
    scalar = (5, 6, 7)
    scratch = [
        *[(pltpu.SMEM if k in scalar else pltpu.VMEM)(v.shape, v.dtype) for k, v in enumerate(values)],
        dma((len(values),)),
        pltpu.VMEM((FEED, 128, PLOC), BF16),
        pltpu.VMEM((FEED, EB, 128), BF16),
        pltpu.VMEM((NDB, BLOCK), F32),
        pltpu.VMEM((NDB, BLOCK), F32),
        pltpu.VMEM((PLOC, 128), F32),
        pltpu.VMEM((PLOC, 128), F32),
        pltpu.VMEM((PLOC, 128), F32),
        pltpu.VMEM((16, PLOC), F32),
        pltpu.VMEM((PLOC, SLOTS * 256), BF16),
        pltpu.VMEM((SLOTS, 128), F32),
        pltpu.VMEM((8, BP), F32),
        pltpu.VMEM((NDB, BP), F32),
        pltpu.VMEM((NDB, BP), F32),
        pltpu.VMEM((NDB, 128), F32),
        pltpu.VMEM((ROWS, BP), BF16),
        pltpu.VMEM((BP, ROWS), BF16),
        pltpu.VMEM((CAP, ROWS), BF16),
        pltpu.VMEM((ROWS, CAP), BF16),
        pltpu.VMEM((ROWS, 128), F32),
        pltpu.VMEM((CAP, 128), F32),
        pltpu.VMEM((BP, PLOC), BF16),
        pltpu.VMEM((BP, PLOC), BF16),
        pltpu.VMEM((ROWS, PLOC), BF16),
        pltpu.VMEM((ROWS, PLOC), BF16),
        pltpu.VMEM((ROWS, 512), BF16),
        pltpu.VMEM((PTSD, CH, 128), F32),
        pltpu.VMEM((PTSD - 1, CH, 128), F32),
        pltpu.VMEM((PTSD, 32, 128), BF16),
        pltpu.VMEM((CAP, 128), F32),
        pltpu.VMEM((CAP, 128), F32),
        pltpu.VMEM((CAP, 256), F32),
        pltpu.VMEM((PTSD, 128), F32),
        pltpu.VMEM((PTSD, 128), F32),
        pltpu.VMEM((ROWS, 256), BF16),
        pltpu.VMEM((ROWS, 2 * PLOC), BF16),
        pltpu.VMEM((FEED, 8, 128), F32),
        pltpu.VMEM((PTSD, 8, 128), F32),
        pltpu.VMEM((PLANE - 1, 2, 8, 128), F32),
        pltpu.VMEM((RING, 2, 8, 128), F32),
        pltpu.VMEM((PTSD, 8, 128), F32),
        pltpu.SemaphoreType.REGULAR,
        pltpu.SemaphoreType.REGULAR,
        pltpu.SemaphoreType.REGULAR,
        dma((9,)), dma((9,)),
        dma, dma, dma, dma,
        dma((3,)), dma((3,)),
        dma, dma,
        dma((RING - 1,)), dma((RING - 1,)),
        dma, dma,
    ]
    shapes = (
        jax.ShapeDtypeStruct((1, 128), F32),
        jax.ShapeDtypeStruct((32, 128), F32),
        jax.ShapeDtypeStruct((2 * GROUP_SIZE, 2, BEAMS), F32),
    )
    results = pl.pallas_call(
        body,
        out_shape=shapes,
        in_specs=[hbm] * len(values),
        out_specs=(vmem, vmem, vmem),
        scratch_shapes=scratch,
        compiler_params=pltpu.CompilerParams(
            collective_id=0, has_side_effects=True, vmem_limit_bytes=60 * 1024 * 1024
        ),
        name="coverage",
    )(*values)
    objective, grad_coef, grad_exc = pl.pallas_call(
        store,
        out_shape=shapes,
        in_specs=[vmem] * 3,
        out_specs=(hbm, hbm, hbm),
        scratch_shapes=[dma((3,))],
        name="store",
    )(*results)
    return objective[0, 0], grad_coef.reshape(NC), jnp.transpose(grad_exc, (1, 2, 0))


def solution(mesh):
    return jax.shard_map(
        local,
        mesh=mesh,
        in_specs=(
            P(None, "feed", "pts"),
            P(None, None, "feed"),
            P(),
            P(None, "pts"),
            P(None, "pts"),
            P("pts"),
            P("pts"),
            P(),
            P(),
            P(),
            P(),
        ),
        out_specs=(P(), P(), P(None, None, "feed")),
        check_vma=False,
    )
```

```python
import functools
import math

import jax
import jax.numpy as jnp
from jax import lax
from jax.experimental import pallas as pl
from jax.experimental.pallas import tpu as pltpu
from jax.sharding import PartitionSpec as P

MESH = pl.DeviceIdType.MESH
F32 = jnp.float32
BF16 = jnp.bfloat16

GROUP_SIZE = 25
BEAMS = 200
NDB = 64
BLOCK = 128
CBMAX = 8
NCV = 64
NC = 4096
SHARPNESS = 2.0
TWO_PI = 2.0 * math.pi

FEED = 4
PTSD = 32
PLOC = 512
BP = 256
EB = 208
SLOTS = NDB // FEED
CAP = 384
CH = 24
NEG = -1e30
PAIRS = 900
WIDTH = tuple(-(-min(BEAMS, PAIRS // (FEED * s + 1)) // 16) * 16 for s in range(SLOTS))
BASE = tuple(sum(WIDTH[:s]) for s in range(SLOTS))
ROWS = -(-sum(WIDTH) // 128) * 128
PLANE = 16
RING = 8

COS_C = (0.99999921, -19.73898036, 64.92865742, -85.27162153, 58.79049212, -21.07110563)
SIN_C = (6.28318492, -41.34158923, 81.59994333, -76.61447253, 41.34288235, -12.47124354)


def horner(coefs, z):
    acc = jnp.full(z.shape, coefs[-1], F32)
    for c in coefs[-2::-1]:
        acc = acc * z + c
    return acc


def iota(shape, dim):
    return lax.broadcasted_iota(jnp.int32, shape, dim)


def columns(row, n):
    return jnp.transpose(jnp.broadcast_to(row, (n, row.shape[1])))


def dot(a, b):
    return jnp.dot(a, b, preferred_element_type=F32)


def body(
    il_in, ex_in, bg_in, pos_in, par_in, row_in, col_in, coef_in, dir_in, cb_in, cnt_in,
    obj_ref, gcoef_ref, gexc_ref,
    il_ref, ex_ref, bg_ref, pos_ref, par_ref, row_ref, col_ref, coef_ref, dir_ref, cb_ref, cnt_ref, in_sem,
    il_all, e_all, dirx, diry, xb, yb, hb, w16, kall, rates, pad_a,
    rt_s, mt_s, rank_s, ohb, ohbt, ohc, ohct, multq, multb, jre, jim, jlre, jlim, fs,
    fbuf, frecv, agbuf, covre, covim, sens, peak_s, part_s, grid, yg, stats, gbuf, grecv, fb, gag, next_sem, row_sem, plane_sem,
    il_ss, il_rs, rs_ss, rs_rs, ag_ss, ag_rs, st_ss, st_rs, g_ss, g_rs, b_ss, b_rs, c_ss, c_rs,
):
    f = lax.axis_index("feed")
    p = lax.axis_index("pts")
    sib = f + 1 - 2 * (f % 2)
    par = (f + 2) % FEED
    par_sib = (sib + 2) % FEED

    barrier = pltpu.get_barrier_semaphore()
    far = p // PLANE
    flat = p % PLANE
    y = p % 4
    z = flat // 4
    y_ring = [{"pts": p - y + (y + d) % 4} for d in range(1, 4)]
    z_next = [{"pts": p - 4 * z + 4 * ((z + d) % 4)} for d in (1, 3)]
    across = {"pts": (p + PLANE) % PTSD}
    x_ring = [
        {"feed": (f + d // 2) % FEED, "pts": (p + PLANE * (d % 2)) % PTSD} for d in range(1, RING)
    ]
    greeted = [{"feed": par}, {"feed": sib}, *y_ring, *z_next, across]
    for to in greeted:
        pl.semaphore_signal(barrier, inc=1, device_id=to, device_id_type=MESH)

    held = (il_ref, ex_ref, bg_ref, cb_ref, cnt_ref, dir_ref, pos_ref, par_ref, coef_ref, row_ref, col_ref)
    given = (il_in, ex_in, bg_in, cb_in, cnt_in, dir_in, pos_in, par_in, coef_in, row_in, col_in)
    loads = [pltpu.make_async_copy(a, b, in_sem.at[k]) for k, (a, b) in enumerate(zip(given, held))]
    for c in loads:
        c.start()
    for c in loads[:3]:
        c.wait()

    r64 = iota((64, 50), 0)
    place = jnp.where(
        (iota((64, 50), 1) == GROUP_SIZE * (r64 // 32) + r64 % 32) & (r64 % 32 < GROUP_SIZE), 1.0, 0.0
    ).astype(BF16)
    il_all[f, 0:64, :] = dot(place, il_ref[:, 0, :]).astype(BF16)
    il_all[f, 64:128, :] = dot(place, il_ref[:, 1, :]).astype(BF16)

    pad_a[...] = jnp.full((8, BP), -1.0, F32)
    pad_a[0:1, 0:BEAMS] = bg_ref[...].astype(F32)
    grp_row = pad_a[0:1, :]
    l128 = iota((50, 128), 1)
    r50 = iota((50, 128), 0)
    lane_feed = GROUP_SIZE * ((l128 % 64) // 32) + l128 % 32
    fits = (r50 == lane_feed) & (l128 % 32 < GROUP_SIZE)
    q_re = jnp.where(fits & (l128 < 64), 1.0, 0.0).astype(BF16)
    q_im = jnp.where(fits & (l128 >= 64), 1.0, 0.0).astype(BF16)
    first_dims = (((0,), (0,)), ((), ()))
    ex = lax.dot_general(ex_ref[:, 0, :], q_re, first_dims, preferred_element_type=F32)
    ex = ex + lax.dot_general(ex_ref[:, 1, :], q_im, first_dims, preferred_element_type=F32)
    grp_cols = columns(grp_row, 128)[0:BEAMS, :]
    lane_grp = ((iota((BEAMS, 128), 1) % 64) // 32 + 2 * f).astype(F32)
    e_all[f, 0:BEAMS, :] = jnp.where(grp_cols == lane_grp, ex, 0.0).astype(BF16)
    e_all[f, BEAMS:EB, :] = jnp.zeros((EB - BEAMS, 128), BF16)

    pl.semaphore_wait(barrier, len(greeted))
    for to in z_next:
        pl.semaphore_signal(next_sem, inc=1, device_id=to, device_id_type=MESH)

    def feed_copy(k, slot, to):
        part = e_all.at[slot] if k % 3 == 0 else il_all.at[slot, pl.ds(64 * (k % 3 - 1), 64)]
        return pltpu.make_async_remote_copy(
            src_ref=part, dst_ref=part, send_sem=il_ss.at[k], recv_sem=il_rs.at[k],
            device_id={"feed": to}, device_id_type=MESH,
        )

    to_par = [feed_copy(k, f, par) for k in range(3)]
    to_sib = [feed_copy(k + 3, f, sib) for k in range(3)]
    passed = [feed_copy(k + 6, par, sib) for k in range(3)]
    for c in to_par + to_sib:
        c.start()

    for c in loads[3:]:
        c.wait()

    pad_a[...] = jnp.full((8, BP), -1.0, F32)
    pad_a[:, 0:BEAMS] = cb_ref[...].astype(F32)
    cover = pad_a[...]
    pad_a[...] = jnp.zeros((8, BP), F32)
    pad_a[0:1, 0:BEAMS] = cnt_ref[...].astype(F32)
    count = pad_a[0:1, :]
    k_io = iota((NDB, BP), 0).astype(F32)
    mult = jnp.zeros((NDB, BP), F32)
    for c in range(CBMAX):
        mult = mult + jnp.where((cover[c : c + 1, :] == k_io) & (count > c), 1.0, 0.0)
    ind = jnp.where(mult > 0.0, 1.0, 0.0)
    n_col = jnp.sum(ind, axis=1, keepdims=True)
    n_b = jnp.broadcast_to(n_col, (NDB, 128))
    n_row = jnp.transpose(jnp.concatenate([n_b, jnp.full((NDB, 128), -1.0, F32)], 0))[0:1, :]
    lane = iota((NDB, 128), 1)
    sub = iota((NDB, 128), 0)
    ahead = (n_row > n_b) | ((n_row == n_b) & (lane < sub))
    rank = jnp.sum(jnp.where(ahead, 1.0, 0.0), axis=1, keepdims=True)
    rank_b = jnp.broadcast_to(rank, (NDB, 128))

    def deal(r):
        level = jnp.floor(r * 0.25)
        odd = level - 2.0 * jnp.floor(level * 0.5)
        place_in = r - 4.0 * level
        return level, jnp.where(odd > 0.5, 3.0 - place_in, place_in)

    fq = f.astype(F32)
    lev_b, bin_b = deal(rank_b)
    rank_row = jnp.transpose(jnp.concatenate([rank_b, jnp.full((NDB, 128), 400.0, F32)], 0))[0:1, :]
    lev_row, bin_row = deal(rank_row)
    before = (bin_row == fq) & (lev_row < lev_b) & (lane < NDB)
    off_col = jnp.sum(jnp.where(before, n_row, 0.0), axis=1, keepdims=True)
    upper = jnp.where(iota((BP, BP), 0) < iota((BP, BP), 1), 1.0, 0.0).astype(BF16)
    rt_s[...] = jnp.where(ind > 0.0, dot(ind.astype(BF16), upper), -1.0)
    mt_s[...] = mult
    rank_s[...] = rank_b
    off_b = jnp.broadcast_to(off_col, (NDB, 128))

    def target(s):
        return 4 * s + f + (s % 2) * (3 - 2 * f)

    def basis(t):
        m = 1.0 - t
        t2 = t * t
        t3 = t2 * t
        return [
            m * m * m / 6.0,
            (3.0 * t3 - 6.0 * t2 + 4.0) / 6.0,
            (-3.0 * t3 + 3.0 * t2 + 3.0 * t + 1.0) / 6.0,
            t3 / 6.0,
        ]

    bu = basis(par_ref[0:1, :])
    bv = basis(par_ref[1:2, :])
    for i in range(4):
        for j in range(4):
            w16[4 * i + j : 4 * i + j + 1, :] = bu[i] * bv[j]
    heights = []
    for blk in range(PLOC // BLOCK):
        base = row_ref[blk] * NCV + col_ref[blk]
        h = jnp.zeros((1, BLOCK), F32)
        for i in range(4):
            for j in range(4):
                k = 4 * i + j
                h = h + w16[k : k + 1, blk * BLOCK : (blk + 1) * BLOCK] * coef_ref[base + i * NCV + j]
        heights.append(h)
    hb[...] = columns(jnp.concatenate(heights, axis=1), 128)
    xb[...] = columns(pos_ref[0:1, :], 128)
    yb[...] = columns(pos_ref[1:2, :], 128)

    for k in range(NDB):
        dirx[k : k + 1, :] = dir_ref[0:1, k * BLOCK : (k + 1) * BLOCK]
        diry[k : k + 1, :] = dir_ref[1:2, k * BLOCK : (k + 1) * BLOCK]

    def phases(s, carry):
        is_s = rank_s[...] == target(s).astype(F32)
        ux = jnp.sum(jnp.where(is_s, dirx[...], 0.0), axis=0, keepdims=True)
        uy = jnp.sum(jnp.where(is_s, diry[...], 0.0), axis=0, keepdims=True)
        uz1 = 1.0 + jnp.sqrt(1.0 - ux * ux - uy * uy)
        rates[pl.ds(s, 1), :] = TWO_PI * uz1
        base = pl.multiple_of(s * 256, 256)
        for c in range(PLOC // 64):
            rows = pl.ds(64 * c, 64)
            t = xb[rows, :] * ux + yb[rows, :] * uy + hb[rows, :] * uz1
            r = t - jnp.round(t)
            z = r * r
            kall[rows, pl.ds(base, 128)] = horner(COS_C, z).astype(BF16)
            kall[rows, pl.ds(base + 128, 128)] = (r * horner(SIN_C, z)).astype(BF16)
        return carry

    lax.fori_loop(0, SLOTS // 2, phases, 0)
    pl.semaphore_wait(next_sem, len(z_next))
    for to in z_next:
        pl.semaphore_signal(row_sem, inc=1, device_id=to, device_id_type=MESH)
    lax.fori_loop(SLOTS // 2, SLOTS, phases, 0)
    pl.semaphore_wait(row_sem, len(z_next))
    pl.semaphore_signal(plane_sem, inc=1, device_id=across, device_id_type=MESH)

    used = BASE[-1] + WIDTH[-1]
    ohb[used:ROWS, :] = jnp.zeros((ROWS - used, BP), BF16)
    ohct[used:ROWS, :] = jnp.zeros((ROWS - used, CAP), BF16)
    multq[used:ROWS, :] = jnp.zeros((ROWS - used, 128), F32)
    for s in range(SLOTS):
        rows = slice(BASE[s], BASE[s] + WIDTH[s])
        is_s = rank_b == target(s).astype(F32)
        off = jnp.sum(jnp.where(is_s, off_b, 0.0), axis=0, keepdims=True)[:, 0:1]
        load = jnp.sum(jnp.where(is_s, n_b, 0.0), axis=0, keepdims=True)[:, 0:1]
        is_w = is_s[:, 0:1]
        order = jnp.sum(jnp.where(is_w, rt_s[...], 0.0), axis=0, keepdims=True)
        times = jnp.sum(jnp.where(is_w, mt_s[...], 0.0), axis=0, keepdims=True)
        hit = order == iota((WIDTH[s], BP), 0).astype(F32)
        ohb[rows, :] = jnp.where(hit, 1.0, 0.0).astype(BF16)
        multq[rows, :] = jnp.broadcast_to(
            jnp.sum(jnp.where(hit, times, 0.0), axis=1, keepdims=True), (WIDTH[s], 128)
        )
        w = iota((WIDTH[s], CAP), 0).astype(F32)
        r = iota((WIDTH[s], CAP), 1).astype(F32)
        ohct[rows, :] = jnp.where((r - w == off) & (w < load), 1.0, 0.0).astype(BF16)
    for n in range(ROWS // 128):
        cols = slice(128 * n, 128 * n + 128)
        ohc[:, cols] = jnp.transpose(ohct[cols, :].astype(F32)).astype(BF16)

    for c, onward in zip(to_par, passed):
        c.wait_recv()
        onward.start()
    for c in to_sib + passed:
        c.wait_recv()

    exc = jnp.concatenate([e_all[k] for k in range(FEED)], axis=1)
    left = [il_all[k] for k in range(FEED)]
    mix_re = jnp.concatenate([x for b in left for x in (b[0:64, :], -b[64:128, :])], axis=0)
    mix_im = jnp.concatenate([x for b in left for x in (b[64:128, :], b[0:64, :])], axis=0)
    jre[EB:BP, :] = jnp.zeros((BP - EB, PLOC), BF16)
    jim[EB:BP, :] = jnp.zeros((BP - EB, PLOC), BF16)
    jre[0:EB, :] = dot(exc, mix_re).astype(BF16)
    jim[0:EB, :] = dot(exc, mix_im).astype(BF16)
    jlre[...] = dot(ohb[...], jre[...]).astype(BF16)
    jlim[...] = dot(ohb[...], jim[...]).astype(BF16)
    scale = 1.0 / math.sqrt(PLOC * PTSD)

    fs[used:ROWS, :] = jnp.zeros((ROWS - used, 512), BF16)
    for s in range(SLOTS):
        w = WIDTH[s]
        rows = slice(BASE[s], BASE[s] + w)
        prod = dot(jnp.concatenate([jlre[rows, :], jlim[rows, :]], axis=0), kall[:, 256 * s : 256 * s + 256])
        re = prod[0:w, 0:128] - prod[w:, 128:]
        im = prod[0:w, 128:] + prod[w:, 0:128]
        for k, val in enumerate((re, im)):
            high = val.astype(BF16)
            fs[rows, 128 * k : 128 * k + 128] = high
            fs[rows, 256 + 128 * k : 384 + 128 * k] = (val - high.astype(F32)).astype(BF16)
    placed = dot(ohc[...], fs[...])
    covre[...] = placed[:, 0:128] + placed[:, 256:384]
    covim[...] = placed[:, 128:256] + placed[:, 384:512]

    low = iota((8, BLOCK), 0) < 4
    for c in range(PTSD):
        fbuf[c, 0:8, :] = scale * covre[8 * c : 8 * c + 8, :]
        fbuf[c, 8:16, :] = scale * covim[8 * c : 8 * c + 8, :]
    for t in range(PTSD // 2):
        re = scale * covre[256 + 8 * t : 264 + 8 * t, :]
        im = scale * covim[256 + 8 * t : 264 + 8 * t, :]
        fbuf[2 * t, 16:24, :] = jnp.where(low, re, pltpu.roll(im, 4, 0))
        fbuf[2 * t + 1, 16:24, :] = jnp.where(low, pltpu.roll(re, 4, 0), im)

    def hops(o):
        return o[0] + min(o[1], 4 - o[1]) + min(o[2], 4 - o[2])

    offsets = [(dx, dz, dy) for dx in range(2) for dz in range(4) for dy in range(4)][1:]
    offsets.sort(key=hops, reverse=True)
    near = [o for o in offsets if o[0] == 0]

    def at_offset(o):
        return PLANE * ((far + o[0]) % 2) + 4 * ((z + o[1]) % 4) + (y + o[2]) % 4

    def start_scatter(src, dst, ss, rs):
        for k, o in enumerate(offsets):
            to = at_offset(o)
            pltpu.make_async_remote_copy(
                src_ref=src.at[to], dst_ref=dst.at[k], send_sem=ss, recv_sem=rs,
                device_id={"pts": to}, device_id_type=MESH,
            ).start()

    def start_gather(buf, ss, rs):
        for o in offsets:
            pltpu.make_async_remote_copy(
                src_ref=buf.at[p], dst_ref=buf.at[p], send_sem=ss, recv_sem=rs,
                device_id={"pts": at_offset(o)}, device_id_type=MESH,
            ).start()

    def wait_all(buf, sem):
        pltpu.make_async_copy(buf.at[pl.ds(0, PTSD - 1)], buf.at[pl.ds(0, PTSD - 1)], sem).wait()

    pl.semaphore_wait(plane_sem, 1)
    start_scatter(fbuf, frecv, rs_ss, rs_rs)
    for n in range(ROWS // 128):
        cols = slice(128 * n, 128 * n + 128)
        ohbt[:, cols] = jnp.transpose(ohb[cols, :].astype(F32)).astype(BF16)
    multb[...] = dot(ohc[...], multq[...].astype(BF16))
    wait_all(frecv, rs_rs)
    whole = fbuf[p]
    for d in range(PTSD - 1):
        whole = whole + frecv[d]

    def total_of(x, op):
        return op(op(x, axis=0, keepdims=True), axis=1, keepdims=True)

    def thirds(x):
        high = x.astype(BF16).astype(F32)
        mid = (x - high).astype(BF16).astype(F32)
        return [high, mid, x - high - mid]

    re_a, im_a, both_b = whole[0:8], whole[8:16], whole[16:24]
    times_a = multb[pl.ds(pl.multiple_of(8 * p, 8), 8), :]
    times_b = multb[pl.ds(pl.multiple_of(256 + 8 * (p // 2), 8), 8), :]
    turned = pltpu.roll(times_b, 4, 0)
    times_b = jnp.where(low == (p % 2 == 0), times_b, turned)
    square = both_b * both_b
    neg_a = jnp.where(times_a > 0.0, -SHARPNESS * (re_a * re_a + im_a * im_a), NEG)
    neg_b = jnp.where(times_b > 0.0, -SHARPNESS * (square + pltpu.roll(square, 4, 0)), NEG)
    own_peak = total_of(jnp.maximum(neg_a, neg_b), jnp.max)
    expo_a = jnp.where(times_a > 0.0, jnp.exp(neg_a - own_peak), 0.0)
    expo_b = jnp.where(times_b > 0.0, jnp.exp(neg_b - own_peak), 0.0)
    own_part = total_of(times_a * expo_a + jnp.where(low, times_b * expo_b, 0.0), jnp.sum)
    notes = jnp.zeros((8, BLOCK), F32)
    for k, val in enumerate(thirds(own_peak) + thirds(own_part)):
        notes = jnp.where(iota((8, BLOCK), 0) == k, val, notes)
    agbuf[p] = jnp.concatenate(
        [2.0 * expo_a * re_a, 2.0 * expo_a * im_a, 2.0 * expo_b * both_b, notes], axis=0
    ).astype(BF16)
    start_gather(agbuf, ag_ss, ag_rs)
    wait_all(fbuf, rs_ss)
    wait_all(agbuf, ag_rs)

    for c in range(PTSD):
        notes = agbuf[c, 16:32, :].astype(F32)[8:16]
        peak_s[c : c + 1, :] = (notes[0:1] + notes[1:2]) + notes[2:3]
        part_s[c : c + 1, :] = (notes[3:4] + notes[4:5]) + notes[5:6]
    peak = jnp.max(peak_s[...], axis=0, keepdims=True)
    gauge = jnp.exp(peak_s[...] - peak)
    part = jnp.sum(part_s[...] * gauge, axis=0, keepdims=True)
    peak_s[...] = gauge
    first = iota((8, BLOCK), 0) < 1
    stats[f] = jnp.where(first, jnp.broadcast_to(peak, (8, BLOCK)), jnp.broadcast_to(part, (8, BLOCK)))

    def feed_copies(buf, ss, rs):
        return [
            pltpu.make_async_remote_copy(
                src_ref=buf.at[f], dst_ref=buf.at[f], send_sem=ss.at[d - 1], recv_sem=rs.at[d - 1],
                device_id={"feed": (f + d) % FEED}, device_id_type=MESH,
            )
            for d in range(1, FEED)
        ]

    st_copies = feed_copies(stats, st_ss, st_rs)
    for c in st_copies:
        c.start()
    for c in range(PTSD):
        rows = agbuf[c, 0:16, :].astype(F32) * peak_s[c : c + 1, :]
        sens[8 * c : 8 * c + 8, 0:128] = rows[0:8]
        sens[8 * c : 8 * c + 8, 128:256] = rows[8:16]
    for t in range(PTSD // 2):
        even = agbuf[2 * t, 16:32, :].astype(F32)[0:8] * peak_s[2 * t : 2 * t + 1, :]
        odd = agbuf[2 * t + 1, 16:32, :].astype(F32)[0:8] * peak_s[2 * t + 1 : 2 * t + 2, :]
        sens[256 + 8 * t : 264 + 8 * t, 0:128] = jnp.where(low, even, pltpu.roll(odd, 4, 0))
        sens[256 + 8 * t : 264 + 8 * t, 128:256] = jnp.where(low, pltpu.roll(even, 4, 0), odd)
    times = jnp.concatenate([multq[...], multq[...]], axis=1)
    grid[...] = (times * dot(ohct[...], sens[...].astype(BF16))).astype(BF16)

    yg[used:ROWS, :] = jnp.zeros((ROWS - used, 2 * PLOC), BF16)
    slope8 = jnp.zeros((8, PLOC), F32)
    for s in range(SLOTS):
        w = WIDTH[s]
        rows = slice(BASE[s], BASE[s] + w)
        sr = grid[rows, 0:128]
        si = grid[rows, 128:256]
        rate = rates[s : s + 1, :]
        rr = (rate * sr.astype(F32)).astype(BF16)
        ri = (rate * si.astype(F32)).astype(BF16)
        left_s = jnp.concatenate(
            [
                jnp.concatenate([sr, si], axis=1),
                jnp.concatenate([si, -sr], axis=1),
                jnp.concatenate([ri, -rr], axis=1),
                jnp.concatenate([-rr, -ri], axis=1),
            ],
            axis=0,
        )
        back = lax.dot_general(
            left_s, kall[:, 256 * s : 256 * s + 256], (((1,), (1,)), ((), ())), preferred_element_type=F32
        )
        yg[rows, 0:PLOC] = back[0:w, :].astype(BF16)
        yg[rows, PLOC:] = back[w : 2 * w, :].astype(BF16)
        turn = jlre[rows, :].astype(F32) * back[2 * w : 3 * w, :] + jlim[rows, :].astype(F32) * back[3 * w :, :]
        slope8 = slope8 + jnp.sum(turn.reshape(w // 8, 8, PLOC), axis=0)
    slope_row = jnp.sum(slope8, axis=0, keepdims=True)

    weighted = w16[...] * slope_row
    m = iota((32, 128), 0) * 128 + iota((32, 128), 1)
    grid_coef = jnp.zeros((32, 128), F32)
    for blk in range(PLOC // BLOCK):
        sums = jnp.sum(weighted[:, blk * BLOCK : (blk + 1) * BLOCK], axis=1, keepdims=True)
        i = m // NCV - row_ref[blk]
        j = m % NCV - col_ref[blk]
        key = jnp.where((i >= 0) & (i < 4) & (j >= 0) & (j < 4), 4 * i + j, -1)
        for k in range(16):
            grid_coef = grid_coef + jnp.where(key == k, sums[k : k + 1, :], 0.0)

    by_beam = dot(ohbt[...], yg[...]).astype(BF16)
    grad = jnp.concatenate([by_beam[:, 0:PLOC], by_beam[:, PLOC:]], axis=0)
    light = jnp.concatenate([il_all[k] for k in range(FEED)], axis=0)
    prod = lax.dot_general(light, grad, (((1,), (1,)), ((), ())), preferred_element_type=F32)
    pad_a[...] = jnp.full((8, BP), -1.0, F32)
    pad_a[0:1, 0:BEAMS] = bg_ref[...].astype(F32)
    grp = pad_a[0:1, :]
    ge_re = jnp.zeros((32, BP), F32)
    ge_im = jnp.zeros((32, BP), F32)
    for k in range(FEED):
        up = prod[128 * k : 128 * k + 64, :]
        dn = prod[128 * k + 64 : 128 * k + 128, :]
        re = up[:, 0:BP] + dn[:, BP:]
        im = up[:, BP:] - dn[:, 0:BP]
        for h in range(2):
            own = grp == float(2 * k + h)
            ge_re = ge_re + jnp.where(own, re[32 * h : 32 * h + 32, :], 0.0)
            ge_im = ge_im + jnp.where(own, im[32 * h : 32 * h + 32, :], 0.0)
    gbuf[...] = jnp.zeros((PTSD, 8, 128), F32)
    pieces = (ge_re[:, 0:128], ge_re[:, 128:], ge_im[:, 0:128], ge_im[:, 128:], grid_coef)
    for k, piece in enumerate(pieces):
        for c in range(PTSD):
            gbuf[c, k : k + 1, :] = piece[c : c + 1, :]

    def wait_plane(sem):
        pltpu.make_async_copy(grecv, grecv, sem).wait()

    for k, o in enumerate(near):
        to = at_offset(o)
        pltpu.make_async_remote_copy(
            src_ref=gbuf.at[pl.ds(2 * (to % PLANE), 2)], dst_ref=grecv.at[k], send_sem=g_ss, recv_sem=g_rs,
            device_id={"pts": to}, device_id_type=MESH,
        ).start()
    wait_plane(g_rs)
    tile = gbuf[pl.ds(2 * flat, 2)]
    for d in range(PLANE - 1):
        tile = tile + grecv[d]

    for c in st_copies:
        c.wait_recv()
    peaks = [stats[k, 0:1, 0:1] for k in range(FEED)]
    parts = [stats[k, 1:2, 0:1] for k in range(FEED)]
    top_peak = jnp.maximum(jnp.maximum(peaks[0], peaks[1]), jnp.maximum(peaks[2], peaks[3]))
    denom = sum(parts[k] * jnp.exp(peaks[k] - top_peak) for k in range(FEED))
    obj_ref[...] = jnp.broadcast_to(-(top_peak + jnp.log(denom)) / SHARPNESS, (1, 128))
    factor = scale * jnp.exp(peak[:, 0:1] - top_peak) / denom
    spot = 2 * f + far
    fb[spot] = tile * jnp.broadcast_to(factor, (8, BLOCK))
    fb_copies = [
        pltpu.make_async_remote_copy(
            src_ref=fb.at[spot], dst_ref=fb.at[spot], send_sem=b_ss.at[k], recv_sem=b_rs.at[k],
            device_id=to, device_id_type=MESH,
        )
        for k, to in enumerate(x_ring)
    ]
    for c in fb_copies:
        c.start()
    for c in fb_copies:
        c.wait_recv()
    total = fb[0]
    for k in range(1, RING):
        total = total + fb[k]
    gag[pl.ds(2 * flat, 2)] = total
    mine2 = gag.at[pl.ds(2 * flat, 2)]
    for o in near:
        pltpu.make_async_remote_copy(
            src_ref=mine2, dst_ref=mine2, send_sem=c_ss, recv_sem=c_rs,
            device_id={"pts": at_offset(o)}, device_id_type=MESH,
        ).start()
    wait_plane(c_rs)

    for c in range(PTSD):
        gcoef_ref[c : c + 1, :] = gag[c, 4:5, :]
    half = [jnp.concatenate([gag[c, k : k + 1, :] for c in range(PTSD)], axis=0) for k in range(4)]
    for h in range(2):
        keep = grp == (2 * f + h).astype(F32)
        for k in range(2):
            rows = jnp.concatenate([half[2 * k], half[2 * k + 1]], axis=1)
            out = jnp.where(keep, rows, 0.0)
            gexc_ref[GROUP_SIZE * h : GROUP_SIZE * (h + 1), k, :] = out[0:GROUP_SIZE, 0:BEAMS]

    for c in to_par + to_sib + passed + st_copies + fb_copies:
        c.wait_send()
    wait_all(agbuf, ag_ss)
    wait_plane(g_ss)
    wait_plane(c_ss)


def store(obj_ref, gcoef_ref, gexc_ref, obj_out, gcoef_out, gexc_out, sem):
    copies = [
        pltpu.make_async_copy(a, b, sem.at[k])
        for k, (a, b) in enumerate(((gexc_ref, gexc_out), (gcoef_ref, gcoef_out), (obj_ref, obj_out)))
    ]
    for c in copies:
        c.start()
    for c in copies:
        c.wait()


def local(
    illumination,
    excitation,
    beam_group,
    positions,
    params,
    span_rows,
    span_cols,
    surface_coef,
    directions,
    cover_blocks,
    cover_count,
):
    vmem = pl.BlockSpec(memory_space=pltpu.VMEM)
    hbm = pl.BlockSpec(memory_space=pltpu.HBM)
    dma = pltpu.SemaphoreType.DMA
    values = (
        jnp.transpose(illumination, (1, 0, 2)),
        jnp.transpose(excitation, (2, 0, 1)),
        beam_group.reshape(1, BEAMS),
        positions,
        params,
        span_rows,
        span_cols,
        surface_coef,
        directions,
        cover_blocks.T,
        cover_count.reshape(1, BEAMS),
    )
    scalar = (5, 6, 7)
    scratch = [
        *[(pltpu.SMEM if k in scalar else pltpu.VMEM)(v.shape, v.dtype) for k, v in enumerate(values)],
        dma((len(values),)),
        pltpu.VMEM((FEED, 128, PLOC), BF16),
        pltpu.VMEM((FEED, EB, 128), BF16),
        pltpu.VMEM((NDB, BLOCK), F32),
        pltpu.VMEM((NDB, BLOCK), F32),
        pltpu.VMEM((PLOC, 128), F32),
        pltpu.VMEM((PLOC, 128), F32),
        pltpu.VMEM((PLOC, 128), F32),
        pltpu.VMEM((16, PLOC), F32),
        pltpu.VMEM((PLOC, SLOTS * 256), BF16),
        pltpu.VMEM((SLOTS, 128), F32),
        pltpu.VMEM((8, BP), F32),
        pltpu.VMEM((NDB, BP), F32),
        pltpu.VMEM((NDB, BP), F32),
        pltpu.VMEM((NDB, 128), F32),
        pltpu.VMEM((ROWS, BP), BF16),
        pltpu.VMEM((BP, ROWS), BF16),
        pltpu.VMEM((CAP, ROWS), BF16),
        pltpu.VMEM((ROWS, CAP), BF16),
        pltpu.VMEM((ROWS, 128), F32),
        pltpu.VMEM((CAP, 128), F32),
        pltpu.VMEM((BP, PLOC), BF16),
        pltpu.VMEM((BP, PLOC), BF16),
        pltpu.VMEM((ROWS, PLOC), BF16),
        pltpu.VMEM((ROWS, PLOC), BF16),
        pltpu.VMEM((ROWS, 512), BF16),
        pltpu.VMEM((PTSD, CH, 128), F32),
        pltpu.VMEM((PTSD - 1, CH, 128), F32),
        pltpu.VMEM((PTSD, 32, 128), BF16),
        pltpu.VMEM((CAP, 128), F32),
        pltpu.VMEM((CAP, 128), F32),
        pltpu.VMEM((CAP, 256), F32),
        pltpu.VMEM((PTSD, 128), F32),
        pltpu.VMEM((PTSD, 128), F32),
        pltpu.VMEM((ROWS, 256), BF16),
        pltpu.VMEM((ROWS, 2 * PLOC), BF16),
        pltpu.VMEM((FEED, 8, 128), F32),
        pltpu.VMEM((PTSD, 8, 128), F32),
        pltpu.VMEM((PLANE - 1, 2, 8, 128), F32),
        pltpu.VMEM((RING, 2, 8, 128), F32),
        pltpu.VMEM((PTSD, 8, 128), F32),
        pltpu.SemaphoreType.REGULAR,
        pltpu.SemaphoreType.REGULAR,
        pltpu.SemaphoreType.REGULAR,
        dma((9,)), dma((9,)),
        dma, dma, dma, dma,
        dma((3,)), dma((3,)),
        dma, dma,
        dma((RING - 1,)), dma((RING - 1,)),
        dma, dma,
    ]
    shapes = (
        jax.ShapeDtypeStruct((1, 128), F32),
        jax.ShapeDtypeStruct((32, 128), F32),
        jax.ShapeDtypeStruct((2 * GROUP_SIZE, 2, BEAMS), F32),
    )
    results = pl.pallas_call(
        body,
        out_shape=shapes,
        in_specs=[hbm] * len(values),
        out_specs=(vmem, vmem, vmem),
        scratch_shapes=scratch,
        compiler_params=pltpu.CompilerParams(
            collective_id=0, has_side_effects=True, vmem_limit_bytes=60 * 1024 * 1024
        ),
        name="coverage",
    )(*values)
    objective, grad_coef, grad_exc = pl.pallas_call(
        store,
        out_shape=shapes,
        in_specs=[vmem] * 3,
        out_specs=(hbm, hbm, hbm),
        scratch_shapes=[dma((3,))],
        name="store",
    )(*results)
    return objective[0, 0], grad_coef.reshape(NC), jnp.transpose(grad_exc, (1, 2, 0))


def solution(mesh):
    return jax.shard_map(
        local,
        mesh=mesh,
        in_specs=(
            P(None, "feed", "pts"),
            P(None, None, "feed"),
            P(),
            P(None, "pts"),
            P(None, "pts"),
            P("pts"),
            P("pts"),
            P(),
            P(),
            P(),
            P(),
        ),
        out_specs=(P(), P(), P(None, None, "feed")),
        check_vma=False,
    )
```

```python
import functools
import math

import jax
import jax.numpy as jnp
from jax import lax
from jax.experimental import pallas as pl
from jax.experimental.pallas import tpu as pltpu
from jax.sharding import PartitionSpec as P

MESH = pl.DeviceIdType.MESH
F32 = jnp.float32
BF16 = jnp.bfloat16

GROUP_SIZE = 25
BEAMS = 200
NDB = 64
BLOCK = 128
CBMAX = 8
NCV = 64
NC = 4096
SHARPNESS = 2.0
TWO_PI = 2.0 * math.pi

FEED = 4
PTSD = 32
PLOC = 512
BP = 256
EB = 208
SLOTS = NDB // FEED
CAP = 384
CH = 24
NEG = -1e30
PAIRS = 900
WIDTH = tuple(-(-min(BEAMS, PAIRS // (FEED * s + 1)) // 16) * 16 for s in range(SLOTS))
BASE = tuple(sum(WIDTH[:s]) for s in range(SLOTS))
ROWS = -(-sum(WIDTH) // 128) * 128
PLANE = 16
RING = 8

COS_C = (0.99999921, -19.73898036, 64.92865742, -85.27162153, 58.79049212, -21.07110563)
SIN_C = (6.28318492, -41.34158923, 81.59994333, -76.61447253, 41.34288235, -12.47124354)


def horner(coefs, z):
    acc = jnp.full(z.shape, coefs[-1], F32)
    for c in coefs[-2::-1]:
        acc = acc * z + c
    return acc


def iota(shape, dim):
    return lax.broadcasted_iota(jnp.int32, shape, dim)


def columns(row, n):
    return jnp.transpose(jnp.broadcast_to(row, (n, row.shape[1])))


def dot(a, b):
    return jnp.dot(a, b, preferred_element_type=F32)


def body(
    il_in, ex_in, bg_in, pos_in, par_in, row_in, col_in, coef_in, dir_in, cb_in, cnt_in,
    obj_ref, gcoef_ref, gexc_ref,
    il_ref, ex_ref, bg_ref, pos_ref, par_ref, row_ref, col_ref, coef_ref, dir_ref, cb_ref, cnt_ref, in_sem,
    il_all, e_all, dirx, diry, xb, yb, hb, w16, kall, rates, pad_a,
    rt_s, mt_s, rank_s, ohb, ohbt, ohc, ohct, multq, multb, jre, jim, jlre, jlim, fs,
    fbuf, frecv, agbuf, covre, covim, sens, peak_s, part_s, grid, yg, stats, gbuf, grecv, fb, gag, next_sem, row_sem, plane_sem,
    il_ss, il_rs, rs_ss, rs_rs, ag_ss, ag_rs, st_ss, st_rs, g_ss, g_rs, b_ss, b_rs, c_ss, c_rs,
):
    f = lax.axis_index("feed")
    p = lax.axis_index("pts")
    sib = f + 1 - 2 * (f % 2)
    par = (f + 2) % FEED
    par_sib = (sib + 2) % FEED

    barrier = pltpu.get_barrier_semaphore()
    far = p // PLANE
    flat = p % PLANE
    y = p % 4
    z = flat // 4
    y_ring = [{"pts": p - y + (y + d) % 4} for d in range(1, 4)]
    z_next = [{"pts": p - 4 * z + 4 * ((z + d) % 4)} for d in (1, 3)]
    across = {"pts": (p + PLANE) % PTSD}
    x_ring = [
        {"feed": (f + d // 2) % FEED, "pts": (p + PLANE * (d % 2)) % PTSD} for d in range(1, RING)
    ]
    greeted = [{"feed": par}, {"feed": sib}, *y_ring, *z_next, across]
    for to in greeted:
        pl.semaphore_signal(barrier, inc=1, device_id=to, device_id_type=MESH)

    held = (il_ref, ex_ref, bg_ref, cb_ref, cnt_ref, dir_ref, pos_ref, par_ref, coef_ref, row_ref, col_ref)
    given = (il_in, ex_in, bg_in, cb_in, cnt_in, dir_in, pos_in, par_in, coef_in, row_in, col_in)
    loads = [pltpu.make_async_copy(a, b, in_sem.at[k]) for k, (a, b) in enumerate(zip(given, held))]
    for c in loads:
        c.start()
    for c in loads[:3]:
        c.wait()

    r64 = iota((64, 50), 0)
    place = jnp.where(
        (iota((64, 50), 1) == GROUP_SIZE * (r64 // 32) + r64 % 32) & (r64 % 32 < GROUP_SIZE), 1.0, 0.0
    ).astype(BF16)
    il_all[f, 0:64, :] = dot(place, il_ref[:, 0, :]).astype(BF16)
    il_all[f, 64:128, :] = dot(place, il_ref[:, 1, :]).astype(BF16)

    pad_a[...] = jnp.full((8, BP), -1.0, F32)
    pad_a[0:1, 0:BEAMS] = bg_ref[...].astype(F32)
    grp_row = pad_a[0:1, :]
    l128 = iota((50, 128), 1)
    r50 = iota((50, 128), 0)
    lane_feed = GROUP_SIZE * ((l128 % 64) // 32) + l128 % 32
    fits = (r50 == lane_feed) & (l128 % 32 < GROUP_SIZE)
    q_re = jnp.where(fits & (l128 < 64), 1.0, 0.0).astype(BF16)
    q_im = jnp.where(fits & (l128 >= 64), 1.0, 0.0).astype(BF16)
    first_dims = (((0,), (0,)), ((), ()))
    ex = lax.dot_general(ex_ref[:, 0, :], q_re, first_dims, preferred_element_type=F32)
    ex = ex + lax.dot_general(ex_ref[:, 1, :], q_im, first_dims, preferred_element_type=F32)
    grp_cols = columns(grp_row, 128)[0:BEAMS, :]
    lane_grp = ((iota((BEAMS, 128), 1) % 64) // 32 + 2 * f).astype(F32)
    e_all[f, 0:BEAMS, :] = jnp.where(grp_cols == lane_grp, ex, 0.0).astype(BF16)
    e_all[f, BEAMS:EB, :] = jnp.zeros((EB - BEAMS, 128), BF16)

    pl.semaphore_wait(barrier, len(greeted))
    for to in z_next:
        pl.semaphore_signal(next_sem, inc=1, device_id=to, device_id_type=MESH)

    def feed_copy(k, slot, to):
        part = e_all.at[slot] if k % 3 == 0 else il_all.at[slot, pl.ds(64 * (k % 3 - 1), 64)]
        return pltpu.make_async_remote_copy(
            src_ref=part, dst_ref=part, send_sem=il_ss.at[k], recv_sem=il_rs.at[k],
            device_id={"feed": to}, device_id_type=MESH,
        )

    to_par = [feed_copy(k, f, par) for k in range(3)]
    to_sib = [feed_copy(k + 3, f, sib) for k in range(3)]
    passed = [feed_copy(k + 6, par, sib) for k in range(3)]
    for c in to_par + to_sib:
        c.start()

    for c in loads[3:]:
        c.wait()

    pad_a[...] = jnp.full((8, BP), -1.0, F32)
    pad_a[:, 0:BEAMS] = cb_ref[...].astype(F32)
    cover = pad_a[...]
    pad_a[...] = jnp.zeros((8, BP), F32)
    pad_a[0:1, 0:BEAMS] = cnt_ref[...].astype(F32)
    count = pad_a[0:1, :]
    k_io = iota((NDB, BP), 0).astype(F32)
    mult = jnp.zeros((NDB, BP), F32)
    for c in range(CBMAX):
        mult = mult + jnp.where((cover[c : c + 1, :] == k_io) & (count > c), 1.0, 0.0)
    ind = jnp.where(mult > 0.0, 1.0, 0.0)
    n_col = jnp.sum(ind, axis=1, keepdims=True)
    n_b = jnp.broadcast_to(n_col, (NDB, 128))
    n_row = jnp.transpose(jnp.concatenate([n_b, jnp.full((NDB, 128), -1.0, F32)], 0))[0:1, :]
    lane = iota((NDB, 128), 1)
    sub = iota((NDB, 128), 0)
    ahead = (n_row > n_b) | ((n_row == n_b) & (lane < sub))
    rank = jnp.sum(jnp.where(ahead, 1.0, 0.0), axis=1, keepdims=True)
    rank_b = jnp.broadcast_to(rank, (NDB, 128))

    def deal(r):
        level = jnp.floor(r * 0.25)
        odd = level - 2.0 * jnp.floor(level * 0.5)
        place_in = r - 4.0 * level
        return level, jnp.where(odd > 0.5, 3.0 - place_in, place_in)

    fq = f.astype(F32)
    lev_b, bin_b = deal(rank_b)
    rank_row = jnp.transpose(jnp.concatenate([rank_b, jnp.full((NDB, 128), 400.0, F32)], 0))[0:1, :]
    lev_row, bin_row = deal(rank_row)
    before = (bin_row == fq) & (lev_row < lev_b) & (lane < NDB)
    off_col = jnp.sum(jnp.where(before, n_row, 0.0), axis=1, keepdims=True)
    upper = jnp.where(iota((BP, BP), 0) < iota((BP, BP), 1), 1.0, 0.0).astype(BF16)
    rt_s[...] = jnp.where(ind > 0.0, dot(ind.astype(BF16), upper), -1.0)
    mt_s[...] = mult
    rank_s[...] = rank_b
    off_b = jnp.broadcast_to(off_col, (NDB, 128))

    def target(s):
        return 4 * s + f + (s % 2) * (3 - 2 * f)

    def basis(t):
        m = 1.0 - t
        t2 = t * t
        t3 = t2 * t
        return [
            m * m * m / 6.0,
            (3.0 * t3 - 6.0 * t2 + 4.0) / 6.0,
            (-3.0 * t3 + 3.0 * t2 + 3.0 * t + 1.0) / 6.0,
            t3 / 6.0,
        ]

    bu = basis(par_ref[0:1, :])
    bv = basis(par_ref[1:2, :])
    for i in range(4):
        for j in range(4):
            w16[4 * i + j : 4 * i + j + 1, :] = bu[i] * bv[j]
    heights = []
    for blk in range(PLOC // BLOCK):
        base = row_ref[blk] * NCV + col_ref[blk]
        h = jnp.zeros((1, BLOCK), F32)
        for i in range(4):
            for j in range(4):
                k = 4 * i + j
                h = h + w16[k : k + 1, blk * BLOCK : (blk + 1) * BLOCK] * coef_ref[base + i * NCV + j]
        heights.append(h)
    hb[...] = columns(jnp.concatenate(heights, axis=1), 128)
    xb[...] = columns(pos_ref[0:1, :], 128)
    yb[...] = columns(pos_ref[1:2, :], 128)

    for k in range(NDB):
        dirx[k : k + 1, :] = dir_ref[0:1, k * BLOCK : (k + 1) * BLOCK]
        diry[k : k + 1, :] = dir_ref[1:2, k * BLOCK : (k + 1) * BLOCK]

    def phases(s, carry):
        is_s = rank_s[...] == target(s).astype(F32)
        ux = jnp.sum(jnp.where(is_s, dirx[...], 0.0), axis=0, keepdims=True)
        uy = jnp.sum(jnp.where(is_s, diry[...], 0.0), axis=0, keepdims=True)
        uz1 = 1.0 + jnp.sqrt(1.0 - ux * ux - uy * uy)
        rates[pl.ds(s, 1), :] = TWO_PI * uz1
        base = pl.multiple_of(s * 256, 256)
        for c in range(PLOC // 64):
            rows = pl.ds(64 * c, 64)
            t = xb[rows, :] * ux + yb[rows, :] * uy + hb[rows, :] * uz1
            r = t - jnp.round(t)
            z = r * r
            kall[rows, pl.ds(base, 128)] = horner(COS_C, z).astype(BF16)
            kall[rows, pl.ds(base + 128, 128)] = (r * horner(SIN_C, z)).astype(BF16)
        return carry

    lax.fori_loop(0, SLOTS // 2, phases, 0)
    pl.semaphore_wait(next_sem, len(z_next))
    for to in z_next:
        pl.semaphore_signal(row_sem, inc=1, device_id=to, device_id_type=MESH)
    lax.fori_loop(SLOTS // 2, SLOTS, phases, 0)
    pl.semaphore_wait(row_sem, len(z_next))
    pl.semaphore_signal(plane_sem, inc=1, device_id=across, device_id_type=MESH)

    used = BASE[-1] + WIDTH[-1]
    ohb[used:ROWS, :] = jnp.zeros((ROWS - used, BP), BF16)
    ohct[used:ROWS, :] = jnp.zeros((ROWS - used, CAP), BF16)
    multq[used:ROWS, :] = jnp.zeros((ROWS - used, 128), F32)
    for s in range(SLOTS):
        rows = slice(BASE[s], BASE[s] + WIDTH[s])
        is_s = rank_b == target(s).astype(F32)
        off = jnp.sum(jnp.where(is_s, off_b, 0.0), axis=0, keepdims=True)[:, 0:1]
        load = jnp.sum(jnp.where(is_s, n_b, 0.0), axis=0, keepdims=True)[:, 0:1]
        is_w = is_s[:, 0:1]
        order = jnp.sum(jnp.where(is_w, rt_s[...], 0.0), axis=0, keepdims=True)
        times = jnp.sum(jnp.where(is_w, mt_s[...], 0.0), axis=0, keepdims=True)
        hit = order == iota((WIDTH[s], BP), 0).astype(F32)
        ohb[rows, :] = jnp.where(hit, 1.0, 0.0).astype(BF16)
        multq[rows, :] = jnp.broadcast_to(
            jnp.sum(jnp.where(hit, times, 0.0), axis=1, keepdims=True), (WIDTH[s], 128)
        )
        w = iota((WIDTH[s], CAP), 0).astype(F32)
        r = iota((WIDTH[s], CAP), 1).astype(F32)
        ohct[rows, :] = jnp.where((r - w == off) & (w < load), 1.0, 0.0).astype(BF16)
    for n in range(ROWS // 128):
        cols = slice(128 * n, 128 * n + 128)
        ohc[:, cols] = jnp.transpose(ohct[cols, :].astype(F32)).astype(BF16)

    for c, onward in zip(to_par, passed):
        c.wait_recv()
        onward.start()
    for c in to_sib + passed:
        c.wait_recv()

    exc = jnp.concatenate([e_all[k] for k in range(FEED)], axis=1)
    left = [il_all[k] for k in range(FEED)]
    mix_re = jnp.concatenate([x for b in left for x in (b[0:64, :], -b[64:128, :])], axis=0)
    mix_im = jnp.concatenate([x for b in left for x in (b[64:128, :], b[0:64, :])], axis=0)
    jre[EB:BP, :] = jnp.zeros((BP - EB, PLOC), BF16)
    jim[EB:BP, :] = jnp.zeros((BP - EB, PLOC), BF16)
    jre[0:EB, :] = dot(exc, mix_re).astype(BF16)
    jim[0:EB, :] = dot(exc, mix_im).astype(BF16)
    jlre[...] = dot(ohb[...], jre[...]).astype(BF16)
    jlim[...] = dot(ohb[...], jim[...]).astype(BF16)
    scale = 1.0 / math.sqrt(PLOC * PTSD)

    fs[used:ROWS, :] = jnp.zeros((ROWS - used, 512), BF16)
    for s in range(SLOTS):
        w = WIDTH[s]
        rows = slice(BASE[s], BASE[s] + w)
        prod = dot(jnp.concatenate([jlre[rows, :], jlim[rows, :]], axis=0), kall[:, 256 * s : 256 * s + 256])
        re = prod[0:w, 0:128] - prod[w:, 128:]
        im = prod[0:w, 128:] + prod[w:, 0:128]
        for k, val in enumerate((re, im)):
            high = val.astype(BF16)
            fs[rows, 128 * k : 128 * k + 128] = high
            fs[rows, 256 + 128 * k : 384 + 128 * k] = (val - high.astype(F32)).astype(BF16)
    placed = dot(ohc[...], fs[...])
    covre[...] = placed[:, 0:128] + placed[:, 256:384]
    covim[...] = placed[:, 128:256] + placed[:, 384:512]

    low = iota((8, BLOCK), 0) < 4
    for c in range(PTSD):
        fbuf[c, 0:8, :] = scale * covre[8 * c : 8 * c + 8, :]
        fbuf[c, 8:16, :] = scale * covim[8 * c : 8 * c + 8, :]
    for t in range(PTSD // 2):
        re = scale * covre[256 + 8 * t : 264 + 8 * t, :]
        im = scale * covim[256 + 8 * t : 264 + 8 * t, :]
        fbuf[2 * t, 16:24, :] = jnp.where(low, re, pltpu.roll(im, 4, 0))
        fbuf[2 * t + 1, 16:24, :] = jnp.where(low, pltpu.roll(re, 4, 0), im)

    def hops(o):
        return o[0] + min(o[1], 4 - o[1]) + min(o[2], 4 - o[2])

    offsets = [(dx, dz, dy) for dx in range(2) for dz in range(4) for dy in range(4)][1:]
    offsets.sort(key=hops, reverse=True)
    near = [o for o in offsets if o[0] == 0]

    def at_offset(o):
        return PLANE * ((far + o[0]) % 2) + 4 * ((z + o[1]) % 4) + (y + o[2]) % 4

    def start_scatter(src, dst, ss, rs):
        for k, o in enumerate(offsets):
            to = at_offset(o)
            pltpu.make_async_remote_copy(
                src_ref=src.at[to], dst_ref=dst.at[k], send_sem=ss, recv_sem=rs,
                device_id={"pts": to}, device_id_type=MESH,
            ).start()

    def start_gather(buf, ss, rs):
        for o in offsets:
            pltpu.make_async_remote_copy(
                src_ref=buf.at[p], dst_ref=buf.at[p], send_sem=ss, recv_sem=rs,
                device_id={"pts": at_offset(o)}, device_id_type=MESH,
            ).start()

    def wait_all(buf, sem):
        pltpu.make_async_copy(buf.at[pl.ds(0, PTSD - 1)], buf.at[pl.ds(0, PTSD - 1)], sem).wait()

    pl.semaphore_wait(plane_sem, 1)
    start_scatter(fbuf, frecv, rs_ss, rs_rs)
    for n in range(ROWS // 128):
        cols = slice(128 * n, 128 * n + 128)
        ohbt[:, cols] = jnp.transpose(ohb[cols, :].astype(F32)).astype(BF16)
    multb[...] = dot(ohc[...], multq[...].astype(BF16))
    wait_all(frecv, rs_rs)
    whole = fbuf[p]
    for d in range(PTSD - 1):
        whole = whole + frecv[d]

    def total_of(x, op):
        return op(op(x, axis=0, keepdims=True), axis=1, keepdims=True)

    def thirds(x):
        high = x.astype(BF16).astype(F32)
        mid = (x - high).astype(BF16).astype(F32)
        return [high, mid, x - high - mid]

    re_a, im_a, both_b = whole[0:8], whole[8:16], whole[16:24]
    times_a = multb[pl.ds(pl.multiple_of(8 * p, 8), 8), :]
    times_b = multb[pl.ds(pl.multiple_of(256 + 8 * (p // 2), 8), 8), :]
    turned = pltpu.roll(times_b, 4, 0)
    times_b = jnp.where(low == (p % 2 == 0), times_b, turned)
    square = both_b * both_b
    neg_a = jnp.where(times_a > 0.0, -SHARPNESS * (re_a * re_a + im_a * im_a), NEG)
    neg_b = jnp.where(times_b > 0.0, -SHARPNESS * (square + pltpu.roll(square, 4, 0)), NEG)
    own_peak = total_of(jnp.maximum(neg_a, neg_b), jnp.max)
    expo_a = jnp.where(times_a > 0.0, jnp.exp(neg_a - own_peak), 0.0)
    expo_b = jnp.where(times_b > 0.0, jnp.exp(neg_b - own_peak), 0.0)
    own_part = total_of(times_a * expo_a + jnp.where(low, times_b * expo_b, 0.0), jnp.sum)
    notes = jnp.zeros((8, BLOCK), F32)
    for k, val in enumerate(thirds(own_peak) + thirds(own_part)):
        notes = jnp.where(iota((8, BLOCK), 0) == k, val, notes)
    agbuf[p] = jnp.concatenate(
        [2.0 * expo_a * re_a, 2.0 * expo_a * im_a, 2.0 * expo_b * both_b, notes], axis=0
    ).astype(BF16)
    start_gather(agbuf, ag_ss, ag_rs)
    wait_all(fbuf, rs_ss)
    wait_all(agbuf, ag_rs)

    for c in range(PTSD):
        notes = agbuf[c, 16:32, :].astype(F32)[8:16]
        peak_s[c : c + 1, :] = (notes[0:1] + notes[1:2]) + notes[2:3]
        part_s[c : c + 1, :] = (notes[3:4] + notes[4:5]) + notes[5:6]
    peak = jnp.max(peak_s[...], axis=0, keepdims=True)
    gauge = jnp.exp(peak_s[...] - peak)
    part = jnp.sum(part_s[...] * gauge, axis=0, keepdims=True)
    peak_s[...] = gauge
    first = iota((8, BLOCK), 0) < 1
    stats[f] = jnp.where(first, jnp.broadcast_to(peak, (8, BLOCK)), jnp.broadcast_to(part, (8, BLOCK)))

    def feed_copies(buf, ss, rs):
        return [
            pltpu.make_async_remote_copy(
                src_ref=buf.at[f], dst_ref=buf.at[f], send_sem=ss.at[d - 1], recv_sem=rs.at[d - 1],
                device_id={"feed": (f + d) % FEED}, device_id_type=MESH,
            )
            for d in range(1, FEED)
        ]

    st_copies = feed_copies(stats, st_ss, st_rs)
    for c in st_copies:
        c.start()
    for c in range(PTSD):
        rows = agbuf[c, 0:16, :].astype(F32) * peak_s[c : c + 1, :]
        sens[8 * c : 8 * c + 8, 0:128] = rows[0:8]
        sens[8 * c : 8 * c + 8, 128:256] = rows[8:16]
    for t in range(PTSD // 2):
        even = agbuf[2 * t, 16:32, :].astype(F32)[0:8] * peak_s[2 * t : 2 * t + 1, :]
        odd = agbuf[2 * t + 1, 16:32, :].astype(F32)[0:8] * peak_s[2 * t + 1 : 2 * t + 2, :]
        sens[256 + 8 * t : 264 + 8 * t, 0:128] = jnp.where(low, even, pltpu.roll(odd, 4, 0))
        sens[256 + 8 * t : 264 + 8 * t, 128:256] = jnp.where(low, pltpu.roll(even, 4, 0), odd)
    times = jnp.concatenate([multq[...], multq[...]], axis=1)
    grid[...] = (times * dot(ohct[...], sens[...].astype(BF16))).astype(BF16)

    yg[used:ROWS, :] = jnp.zeros((ROWS - used, 2 * PLOC), BF16)
    slope8 = jnp.zeros((8, PLOC), F32)
    for s in range(SLOTS):
        w = WIDTH[s]
        rows = slice(BASE[s], BASE[s] + w)
        sr = grid[rows, 0:128]
        si = grid[rows, 128:256]
        rate = rates[s : s + 1, :]
        rr = (rate * sr.astype(F32)).astype(BF16)
        ri = (rate * si.astype(F32)).astype(BF16)
        left_s = jnp.concatenate(
            [
                jnp.concatenate([sr, si], axis=1),
                jnp.concatenate([si, -sr], axis=1),
                jnp.concatenate([ri, -rr], axis=1),
                jnp.concatenate([-rr, -ri], axis=1),
            ],
            axis=0,
        )
        back = lax.dot_general(
            left_s, kall[:, 256 * s : 256 * s + 256], (((1,), (1,)), ((), ())), preferred_element_type=F32
        )
        yg[rows, 0:PLOC] = back[0:w, :].astype(BF16)
        yg[rows, PLOC:] = back[w : 2 * w, :].astype(BF16)
        turn = jlre[rows, :].astype(F32) * back[2 * w : 3 * w, :] + jlim[rows, :].astype(F32) * back[3 * w :, :]
        slope8 = slope8 + jnp.sum(turn.reshape(w // 8, 8, PLOC), axis=0)
    slope_row = jnp.sum(slope8, axis=0, keepdims=True)

    weighted = w16[...] * slope_row
    m = iota((32, 128), 0) * 128 + iota((32, 128), 1)
    grid_coef = jnp.zeros((32, 128), F32)
    for blk in range(PLOC // BLOCK):
        sums = jnp.sum(weighted[:, blk * BLOCK : (blk + 1) * BLOCK], axis=1, keepdims=True)
        i = m // NCV - row_ref[blk]
        j = m % NCV - col_ref[blk]
        key = jnp.where((i >= 0) & (i < 4) & (j >= 0) & (j < 4), 4 * i + j, -1)
        for k in range(16):
            grid_coef = grid_coef + jnp.where(key == k, sums[k : k + 1, :], 0.0)

    by_beam = dot(ohbt[...], yg[...]).astype(BF16)
    grad = jnp.concatenate([by_beam[:, 0:PLOC], by_beam[:, PLOC:]], axis=0)
    light = jnp.concatenate([il_all[k] for k in range(FEED)], axis=0)
    prod = lax.dot_general(light, grad, (((1,), (1,)), ((), ())), preferred_element_type=F32)
    pad_a[...] = jnp.full((8, BP), -1.0, F32)
    pad_a[0:1, 0:BEAMS] = bg_ref[...].astype(F32)
    grp = pad_a[0:1, :]
    ge_re = jnp.zeros((32, BP), F32)
    ge_im = jnp.zeros((32, BP), F32)
    for k in range(FEED):
        up = prod[128 * k : 128 * k + 64, :]
        dn = prod[128 * k + 64 : 128 * k + 128, :]
        re = up[:, 0:BP] + dn[:, BP:]
        im = up[:, BP:] - dn[:, 0:BP]
        for h in range(2):
            own = grp == float(2 * k + h)
            ge_re = ge_re + jnp.where(own, re[32 * h : 32 * h + 32, :], 0.0)
            ge_im = ge_im + jnp.where(own, im[32 * h : 32 * h + 32, :], 0.0)

    lane = iota((1, 128), 1)
    free = 112

    def start_lane(c, k):
        return 64 * (k // 2) + 16 * (c // 4)

    def spot_of(j, k):
        return j // 2, slice(4 * (j % 2) + k, 4 * (j % 2) + k + 1)

    last = grid_coef[24:32]
    for k, piece in enumerate((ge_re[:, 0:128], ge_re[:, 128:], ge_im[:, 0:128], ge_im[:, 128:])):
        for c in range(GROUP_SIZE):
            row = piece[c : c + 1, :]
            if k % 2 == 1 and c < 16:
                turned = pltpu.roll(last, (free - start_lane(c, k)) % 128, 1)
                row = jnp.where(lane >= free, turned[4 + c % 4 : 5 + c % 4, :], row)
            gbuf[spot_of(c, k)] = row
        for c in range(32 - GROUP_SIZE):
            gbuf[spot_of(GROUP_SIZE + c, k)] = grid_coef[4 * c + k : 4 * c + k + 1, :]

    def wait_plane(sem):
        pltpu.make_async_copy(grecv, grecv, sem).wait()

    for k, o in enumerate(near):
        to = at_offset(o)
        pltpu.make_async_remote_copy(
            src_ref=gbuf.at[to % PLANE], dst_ref=grecv.at[k], send_sem=g_ss, recv_sem=g_rs,
            device_id={"pts": to}, device_id_type=MESH,
        ).start()
    wait_plane(g_rs)
    tile = gbuf[flat]
    for d in range(PLANE - 1):
        tile = tile + grecv[d]

    for c in st_copies:
        c.wait_recv()
    peaks = [stats[k, 0:1, 0:1] for k in range(FEED)]
    parts = [stats[k, 1:2, 0:1] for k in range(FEED)]
    top_peak = jnp.maximum(jnp.maximum(peaks[0], peaks[1]), jnp.maximum(peaks[2], peaks[3]))
    denom = sum(parts[k] * jnp.exp(peaks[k] - top_peak) for k in range(FEED))
    obj_ref[...] = jnp.broadcast_to(-(top_peak + jnp.log(denom)) / SHARPNESS, (1, 128))
    factor = scale * jnp.exp(peak[:, 0:1] - top_peak) / denom
    spot = 2 * f + far
    fb[spot] = tile * jnp.broadcast_to(factor, (8, BLOCK))
    fb_copies = [
        pltpu.make_async_remote_copy(
            src_ref=fb.at[spot], dst_ref=fb.at[spot], send_sem=b_ss.at[k], recv_sem=b_rs.at[k],
            device_id=to, device_id_type=MESH,
        )
        for k, to in enumerate(x_ring)
    ]
    for c in fb_copies:
        c.start()
    for c in fb_copies:
        c.wait_recv()
    total = fb[0]
    for k in range(1, RING):
        total = total + fb[k]
    gag[flat] = total
    mine = gag.at[flat]
    for o in near:
        pltpu.make_async_remote_copy(
            src_ref=mine, dst_ref=mine, send_sem=c_ss, recv_sem=c_rs,
            device_id={"pts": at_offset(o)}, device_id_type=MESH,
        ).start()
    wait_plane(c_rs)

    for k in range(4):
        for c in range(32 - GROUP_SIZE):
            gcoef_ref[4 * c + k : 4 * c + k + 1, :] = gag[spot_of(GROUP_SIZE + c, k)]
    tails = [jnp.zeros((1, 128), F32)] * 4
    for k in (1, 3):
        for c in range(16):
            begin = start_lane(c, k)
            turned = pltpu.roll(gag[c // 2], (begin - free) % 128, 1)[spot_of(c, k)[1], :]
            inside = (lane >= begin) & (lane < begin + 16)
            tails[c % 4] = jnp.where(inside, turned, tails[c % 4])
    for c in range(4):
        gcoef_ref[28 + c : 29 + c, :] = tails[c]
    half = [jnp.concatenate([gag[spot_of(c, k)] for c in range(GROUP_SIZE)], axis=0) for k in range(4)]
    for h in range(2):
        keep = grp == (2 * f + h).astype(F32)
        for k in range(2):
            rows = jnp.concatenate([half[2 * k], half[2 * k + 1]], axis=1)
            out = jnp.where(keep, rows, 0.0)
            gexc_ref[GROUP_SIZE * h : GROUP_SIZE * (h + 1), k, :] = out[:, 0:BEAMS]

    for c in to_par + to_sib + passed + st_copies + fb_copies:
        c.wait_send()
    wait_all(agbuf, ag_ss)
    wait_plane(g_ss)
    wait_plane(c_ss)


def store(obj_ref, gcoef_ref, gexc_ref, obj_out, gcoef_out, gexc_out, sem):
    copies = [
        pltpu.make_async_copy(a, b, sem.at[k])
        for k, (a, b) in enumerate(((gexc_ref, gexc_out), (gcoef_ref, gcoef_out), (obj_ref, obj_out)))
    ]
    for c in copies:
        c.start()
    for c in copies:
        c.wait()


def local(
    illumination,
    excitation,
    beam_group,
    positions,
    params,
    span_rows,
    span_cols,
    surface_coef,
    directions,
    cover_blocks,
    cover_count,
):
    vmem = pl.BlockSpec(memory_space=pltpu.VMEM)
    hbm = pl.BlockSpec(memory_space=pltpu.HBM)
    dma = pltpu.SemaphoreType.DMA
    values = (
        jnp.transpose(illumination, (1, 0, 2)),
        jnp.transpose(excitation, (2, 0, 1)),
        beam_group.reshape(1, BEAMS),
        positions,
        params,
        span_rows,
        span_cols,
        surface_coef,
        directions,
        cover_blocks.T,
        cover_count.reshape(1, BEAMS),
    )
    scalar = (5, 6, 7)
    scratch = [
        *[(pltpu.SMEM if k in scalar else pltpu.VMEM)(v.shape, v.dtype) for k, v in enumerate(values)],
        dma((len(values),)),
        pltpu.VMEM((FEED, 128, PLOC), BF16),
        pltpu.VMEM((FEED, EB, 128), BF16),
        pltpu.VMEM((NDB, BLOCK), F32),
        pltpu.VMEM((NDB, BLOCK), F32),
        pltpu.VMEM((PLOC, 128), F32),
        pltpu.VMEM((PLOC, 128), F32),
        pltpu.VMEM((PLOC, 128), F32),
        pltpu.VMEM((16, PLOC), F32),
        pltpu.VMEM((PLOC, SLOTS * 256), BF16),
        pltpu.VMEM((SLOTS, 128), F32),
        pltpu.VMEM((8, BP), F32),
        pltpu.VMEM((NDB, BP), F32),
        pltpu.VMEM((NDB, BP), F32),
        pltpu.VMEM((NDB, 128), F32),
        pltpu.VMEM((ROWS, BP), BF16),
        pltpu.VMEM((BP, ROWS), BF16),
        pltpu.VMEM((CAP, ROWS), BF16),
        pltpu.VMEM((ROWS, CAP), BF16),
        pltpu.VMEM((ROWS, 128), F32),
        pltpu.VMEM((CAP, 128), F32),
        pltpu.VMEM((BP, PLOC), BF16),
        pltpu.VMEM((BP, PLOC), BF16),
        pltpu.VMEM((ROWS, PLOC), BF16),
        pltpu.VMEM((ROWS, PLOC), BF16),
        pltpu.VMEM((ROWS, 512), BF16),
        pltpu.VMEM((PTSD, CH, 128), F32),
        pltpu.VMEM((PTSD - 1, CH, 128), F32),
        pltpu.VMEM((PTSD, 32, 128), BF16),
        pltpu.VMEM((CAP, 128), F32),
        pltpu.VMEM((CAP, 128), F32),
        pltpu.VMEM((CAP, 256), F32),
        pltpu.VMEM((PTSD, 128), F32),
        pltpu.VMEM((PTSD, 128), F32),
        pltpu.VMEM((ROWS, 256), BF16),
        pltpu.VMEM((ROWS, 2 * PLOC), BF16),
        pltpu.VMEM((FEED, 8, 128), F32),
        pltpu.VMEM((PLANE, 8, 128), F32),
        pltpu.VMEM((PLANE - 1, 8, 128), F32),
        pltpu.VMEM((RING, 8, 128), F32),
        pltpu.VMEM((PLANE, 8, 128), F32),
        pltpu.SemaphoreType.REGULAR,
        pltpu.SemaphoreType.REGULAR,
        pltpu.SemaphoreType.REGULAR,
        dma((9,)), dma((9,)),
        dma, dma, dma, dma,
        dma((3,)), dma((3,)),
        dma, dma,
        dma((RING - 1,)), dma((RING - 1,)),
        dma, dma,
    ]
    shapes = (
        jax.ShapeDtypeStruct((1, 128), F32),
        jax.ShapeDtypeStruct((32, 128), F32),
        jax.ShapeDtypeStruct((2 * GROUP_SIZE, 2, BEAMS), F32),
    )
    results = pl.pallas_call(
        body,
        out_shape=shapes,
        in_specs=[hbm] * len(values),
        out_specs=(vmem, vmem, vmem),
        scratch_shapes=scratch,
        compiler_params=pltpu.CompilerParams(
            collective_id=0, has_side_effects=True, vmem_limit_bytes=60 * 1024 * 1024
        ),
        name="coverage",
    )(*values)
    objective, grad_coef, grad_exc = pl.pallas_call(
        store,
        out_shape=shapes,
        in_specs=[vmem] * 3,
        out_specs=(hbm, hbm, hbm),
        scratch_shapes=[dma((3,))],
        name="store",
    )(*results)
    return objective[0, 0], grad_coef.reshape(NC), jnp.transpose(grad_exc, (1, 2, 0))


def solution(mesh):
    return jax.shard_map(
        local,
        mesh=mesh,
        in_specs=(
            P(None, "feed", "pts"),
            P(None, None, "feed"),
            P(),
            P(None, "pts"),
            P(None, "pts"),
            P("pts"),
            P("pts"),
            P(),
            P(),
            P(),
            P(),
        ),
        out_specs=(P(), P(), P(None, None, "feed")),
        check_vma=False,
    )
```
